32 devices in a mesh: replica: 16 (over z, y, core), fsdp: 2 (over x).
Axes of the slice: x: 2, y: 2, z: 4, core: 2. Of those that a mesh axis runs over, the one named last changes fastest.
Arguments:
- tokens: bfloat16 [4096, 1024], P(('replica', 'fsdp')), may hold values from -6 to 6
- seq_lens: int32 [32, 2], P(('replica', 'fsdp')), may hold values from 16 to 96, as said below
- norm_gain: bfloat16 [1024], P('fsdp'), may hold values from 0.099609375 to 1.8984375
- in_weight: bfloat16 [1024, 4384], P('fsdp'), may hold values from -0.1875 to 0.1875
- conv_weight: bfloat16 [4, 2304], P(None, 'fsdp'), may hold values from -3 to 3
- conv_bias: bfloat16 [2304], P('fsdp'), may hold values from -1.5 to 1.5
- step_bias: bfloat16 [32], P('fsdp'), may hold values from -4.5 to -2
- decay_log: bfloat16 [32], P('fsdp'), may hold values from -4 to 0
- skip_gain: bfloat16 [32], P('fsdp'), may hold values from 0.5 to 2
- out_gain: bfloat16 [2048], P('fsdp'), may hold values from 0.099609375 to 1.8984375
- out_weight: bfloat16 [2048, 1024], P('fsdp'), may hold values from -0.125 to 0.125
- cotangent: bfloat16 [4096, 1024], P(('replica', 'fsdp')), may hold values from -6 to 6
Outputs:
- block_out: bfloat16 [4096, 1024], P(('replica', 'fsdp'))
- grad_tokens: float32 [4096, 1024], P(('replica', 'fsdp'))
- norm_gain_grad: float32 [1024], P('fsdp')
- in_weight_grad: float32 [1024, 4384], P('fsdp')
- conv_weight_grad: float32 [4, 2304], P(None, 'fsdp')
- conv_bias_grad: float32 [2304], P('fsdp')
- step_bias_grad: float32 [32], P('fsdp')
- decay_log_grad: float32 [32], P('fsdp')
- skip_gain_grad: float32 [32], P('fsdp')
- out_gain_grad: float32 [2048], P('fsdp')
- out_weight_grad: float32 [2048, 1024], P('fsdp')
The draws below stay inside these ranges and needn't reach their ends.
Inputs may be any that keep to these rules, and one draw needn't show every extreme that they name: `seq_lens`: on each device the sequences fill the first slots, the rest being padding; each length is at least 16, a device's two lengths sum to at most 128, and some device holds exactly 128 tokens of sequences.
All inputs are finite; a program needn't handle non-finite values.
Results may differ from the reference program's by a relative error of at most 0.0074.
Values may be sent and summed in bfloat16 or wider, within the bound.
No kernel may reach another device: no remote copies, remote signals or barrier semaphores. Data moves between devices by JAX's collectives and lax.ppermute only.
A program may use at most 192 MiB of HBM per device.

```python
import math
import jax
import jax.numpy as jnp
from jax import lax

D = 1024
INNER = 2048
HEADS = 32
STATE = 128
CONV = 4
SEQS_DEV = 2
TOK_DEV = 128
HEADDIM = 64
CHANNELS = 2304
PROJ = 4384
TOKENS = 4096
N_REPLICA = 16
N_FSDP = 2


def draw_seq_lens(key, part):
    key = jax.random.fold_in(key, 11)
    device_count = N_REPLICA * N_FSDP
    key_first, key_second, key_pick = jax.random.split(key, 3)
    least = TOK_DEV // 8
    most = 3 * TOK_DEV // 4
    first_len = jax.random.randint(key_first, (device_count,), least, most + 1)
    room = jnp.minimum(most, TOK_DEV - first_len)
    second_len = jax.random.randint(key_second, (device_count,), least, room + 1)
    order = jax.random.permutation(key_pick, device_count)
    devices = jnp.arange(device_count, dtype=jnp.int32)
    full_device = devices == order[0]
    short_device = devices == order[1]
    first_len = jnp.where(full_device, TOK_DEV // 4, jnp.where(short_device, least, first_len))
    second_len = jnp.where(full_device, TOK_DEV - TOK_DEV // 4, jnp.where(short_device, least, second_len))
    return jnp.stack([first_len, second_len], axis=1).astype(jnp.int32)


def levels(key, dims, pieces, low, top_value):
    level = 1.0
    for axis_at, blocks in pieces:
        draws = jax.random.uniform(jax.random.fold_in(jax.random.fold_in(key, 6), axis_at), (blocks,), jnp.float32, low / len(pieces), top_value / len(pieces))
        level = level * jnp.repeat(jnp.exp(draws), dims[axis_at] // blocks).reshape((-1,) + (1,) * (len(dims) - 1 - axis_at))
    return level


def scatter_about(stream_key, dims, scale, limit, cuts=(), held_as=jnp.bfloat16):
    array = jax.random.normal(stream_key, dims, jnp.float32) * scale
    if len(cuts) > 0:
        array = levels(stream_key, dims, cuts, -0.22, 0.18) * array
    return jnp.clip(array, min=-limit, max=limit).astype(held_as)


def setup_inputs(seed: int = 0) -> dict:
    arg_keys = jax.random.split(jax.random.key(seed), 13)
    return {
        "tokens": scatter_about(arg_keys[0], (TOKENS, D), 1.0, 6.0, ((0, 32),)),
        "seq_lens": draw_seq_lens(jax.random.fold_in(arg_keys[12], 71), 0),
        "norm_gain": jnp.clip(1.0 + 0.18 * jax.random.normal(arg_keys[2], (D,), jnp.float32), 0.099609375, 1.8984375).astype(jnp.bfloat16),
        "in_weight": scatter_about(arg_keys[3], (D, PROJ), D ** -0.5, 0.1875, ((0, 2),)),
        "conv_weight": scatter_about(arg_keys[4], (CONV, CHANNELS), CONV ** -0.5, 3.0, ((1, 2),)),
        "conv_bias": scatter_about(arg_keys[5], (CHANNELS,), 0.3, 1.5, ((0, 2),)),
        "step_bias": jnp.clip(-4.5 + 2.5 * jax.random.uniform(arg_keys[6], (HEADS,), jnp.float32) ** levels(arg_keys[6], (HEADS,), ((0, 2),), -0.2, 0.2), -4.5, -2.0).astype(jnp.bfloat16),
        "decay_log": jnp.clip(-4.0 + 4.0 * jax.random.uniform(arg_keys[7], (HEADS,), jnp.float32) ** levels(arg_keys[7], (HEADS,), ((0, 2),), -0.2, 0.2), -4.0, 0.0).astype(jnp.bfloat16),
        "skip_gain": jnp.clip(0.5 + 1.5 * jax.random.uniform(arg_keys[8], (HEADS,), jnp.float32) ** levels(arg_keys[8], (HEADS,), ((0, 2),), -0.2, 0.2), 0.5, 2.0).astype(jnp.bfloat16),
        "out_gain": jnp.clip(1.0 + 0.18 * jax.random.normal(arg_keys[9], (INNER,), jnp.float32), 0.099609375, 1.8984375).astype(jnp.bfloat16),
        "out_weight": scatter_about(arg_keys[10], (INNER, D), INNER ** -0.5, 0.125, ((0, 2),)),
        "cotangent": scatter_about(arg_keys[11], (TOKENS, D), 1.0, 6.0, ((0, 32),)),
    }


EPSILON = 1e-05

@jax.custom_vjp
def low(v):
    return lax.optimization_barrier(v.astype(jnp.bfloat16)).astype(jnp.float32)

@jax.custom_vjp
def low_back(v):
    return v

def low_keep(v):
    return (low(v), None)

def low_pass(kept, grad):
    return (grad,)

def back_keep(v):
    return (v, None)

def back_low(kept, grad):
    return (low(grad),)
low.defvjp(low_keep, low_pass)
low_back.defvjp(back_keep, back_low)

def segment_layout(lengths_row, row_count):
    position = jnp.arange(row_count, dtype=jnp.int32)
    bounds = jnp.cumsum(lengths_row).astype(jnp.int32)
    segment = lax.optimization_barrier(jnp.sum((position[:, None] >= bounds[None, :]).astype(jnp.int32), axis=1))
    starts = jnp.concatenate([jnp.zeros((1,), jnp.int32), bounds])
    labels = jnp.arange(starts.shape[0], dtype=jnp.int32)
    seg_start = lax.optimization_barrier(jnp.sum(jnp.where(segment[:, None] == labels[None, :], starts[None, :], 0), axis=1)).astype(jnp.int32)
    return (position, segment, seg_start)

def conv_and_rates(mixed_in, rate_raw, conv_kernel, conv_shift, rate_bias, decay_rate, position, seg_start):
    row_count = mixed_in.shape[0]
    tap_count = conv_kernel.shape[0]
    summed = jnp.broadcast_to(conv_shift, mixed_in.shape)
    for offset in range(tap_count):
        behind = tap_count - 1 - offset
        shifted = jnp.concatenate([jnp.zeros((behind, mixed_in.shape[1]), mixed_in.dtype), mixed_in[:row_count - behind]], axis=0)
        usable = (position - behind >= seg_start)[:, None]
        summed = summed + conv_kernel[offset] * jnp.where(usable, shifted, 0.0)
    active = jax.nn.silu(summed)
    step_size = jax.nn.softplus(rate_raw + rate_bias)
    cumulative = jnp.cumsum(step_size * -jnp.exp(decay_rate), axis=0)
    return (active, step_size, cumulative)

def mixer_forward(values, lengths_row, weights):
    norm_scale, in_matrix, conv_kernel, conv_shift, rate_bias, decay_rate, skip_scale, out_scale, out_matrix = weights
    row_count = values.shape[0]
    position, segment, seg_start = segment_layout(lengths_row, row_count)
    inverse_rms = lax.rsqrt(lax.optimization_barrier(jnp.mean(values * values, axis=-1, keepdims=True)) + EPSILON)
    normed = low(values * inverse_rms * norm_scale)
    projected = low_back(jnp.dot(normed, in_matrix, precision=lax.Precision.HIGHEST))
    gate_part = projected[:, :INNER]
    mixed_in = projected[:, INNER:INNER + CHANNELS]
    rate_raw = projected[:, INNER + CHANNELS:]
    active, step_size, cumulative = conv_and_rates(mixed_in, rate_raw, conv_kernel, conv_shift, rate_bias, decay_rate, position, seg_start)
    x_active = active[:, :INNER]
    head_input = low(x_active).reshape(row_count, HEADS, HEADDIM)
    state_input = low(active[:, INNER:INNER + STATE])
    state_output = low(active[:, INNER + STATE:])
    inner_part = low_back(jnp.dot(state_output, state_input.T, precision=lax.Precision.HIGHEST))
    same_mask = (position[None, :] <= position[:, None]) & (segment[None, :] == segment[:, None])
    spread = cumulative.T[:, :, None] - cumulative.T[:, None, :]
    masked = jnp.where(same_mask[None], spread, 0.0)
    decays = jnp.where(same_mask[None], jnp.exp(masked), 0.0)
    mixing = low(inner_part[None] * decays * step_size.T[:, None, :])
    scan_out = low_back(jnp.einsum('hts,shp->thp', mixing, head_input, precision=lax.Precision.HIGHEST)).reshape(row_count, INNER)
    direct = (x_active.reshape(row_count, HEADS, HEADDIM) * skip_scale[None, :, None]).reshape(row_count, INNER)
    gated = (scan_out + direct) * jax.nn.silu(gate_part)
    inverse_out = lax.rsqrt(lax.optimization_barrier(jnp.mean(gated * gated, axis=-1, keepdims=True)) + EPSILON)
    out_normed = low(gated * inverse_out * out_scale)
    return values + jnp.dot(out_normed, out_matrix, precision=lax.Precision.HIGHEST)

def reference(tokens, seq_lens, norm_gain, in_weight, conv_weight, conv_bias, step_bias, decay_log, skip_gain, out_gain, out_weight, cotangent):
    buffers = N_REPLICA * N_FSDP
    per_step = math.gcd(buffers, max(1, 4096 // TOK_DEV))
    step_count = buffers // per_step
    weights = tuple((item.astype(jnp.float32) for item in (norm_gain, in_weight, conv_weight, conv_bias, step_bias, decay_log, skip_gain, out_gain, out_weight)))
    inputs = tokens.astype(jnp.float32).reshape(step_count, per_step, TOK_DEV, D)
    length_groups = seq_lens.reshape(step_count, per_step, SEQS_DEV)
    cotangent_groups = cotangent.astype(jnp.float32).reshape(step_count, per_step, TOK_DEV, D)

    def one_step(totals, scan_item):
        values_group, lengths_group, cotangent_group = scan_item

        def group_forward(values_all, params):

            def single_buffer(values_one, lengths_one):
                return mixer_forward(values_one, lengths_one, params)
            return jax.vmap(single_buffer)(values_all, lengths_group)
        result, pullback = jax.vjp(group_forward, values_group, weights)
        grad_values, grad_weights = pullback(cotangent_group)
        totals = jax.tree.map(lambda left_sum, right_sum: left_sum + right_sum, totals, grad_weights)
        return (totals, (result.astype(jnp.bfloat16), grad_values))
    zero_grads = tuple((jnp.zeros_like(item) for item in weights))
    totals, (results, grad_values) = lax.scan(one_step, zero_grads, (inputs, length_groups, cotangent_groups))
    return (results.reshape(TOKENS, D), grad_values.reshape(TOKENS, D), totals[0], totals[1], totals[2], totals[3], totals[4], totals[5], totals[6], totals[7], totals[8])
```

```python
from functools import partial

import jax
import jax.numpy as jnp
from jax import lax
from jax.sharding import PartitionSpec as P

EPSILON = 1e-05


def segment_layout(lengths_row, row_count):
    position = jnp.arange(row_count, dtype=jnp.int32)
    bounds = jnp.cumsum(lengths_row)
    segment = jnp.sum((position[:, None] >= bounds[None, :]).astype(jnp.int32), axis=1)
    starts = jnp.concatenate([jnp.zeros((1,), jnp.int32), bounds])
    labels = jnp.arange(starts.shape[0], dtype=jnp.int32)
    seg_start = jnp.sum(jnp.where(segment[:, None] == labels[None, :], starts[None, :], 0), axis=1)
    return (position, segment, seg_start)


def input_norm(values, norm_scale):
    inverse_rms = lax.rsqrt(jnp.mean(values * values, axis=-1, keepdims=True) + EPSILON)
    return values * inverse_rms * norm_scale


def gated_norm(mixed_values, gate_part, out_scale):
    gated = mixed_values * jax.nn.silu(gate_part)
    inverse_rms = lax.rsqrt(jnp.mean(gated * gated, axis=-1, keepdims=True) + EPSILON)
    return gated * inverse_rms * out_scale


def conv_and_rates(
    mixed_in, rate_raw, conv_kernel, conv_shift, rate_bias, decay_rate, position, seg_start
):
    row_count = mixed_in.shape[0]
    tap_count = conv_kernel.shape[0]
    summed = jnp.broadcast_to(conv_shift, mixed_in.shape)
    for offset in range(tap_count):
        behind = tap_count - 1 - offset
        shifted = jnp.concatenate(
            [
                jnp.zeros((behind, mixed_in.shape[1]), mixed_in.dtype),
                mixed_in[: row_count - behind],
            ],
            axis=0,
        )
        usable = (position - behind >= seg_start)[:, None]
        summed = summed + conv_kernel[offset] * jnp.where(usable, shifted, 0.0)
    active = jax.nn.silu(summed)
    step_size = jax.nn.softplus(rate_raw + rate_bias)
    cumulative = jnp.cumsum(step_size * -jnp.exp(decay_rate), axis=0)
    return (active, step_size, cumulative)


def decay_weights(inner_part, cum_rows, cum_keys, step_keys, same_mask):
    spread = cum_rows.T[:, :, None] - cum_keys.T[:, None, :]
    masked = jnp.where(same_mask[None], spread, 0.0)
    decays = jnp.where(same_mask[None], jnp.exp(masked), 0.0)
    return inner_part[None] * decays * step_keys.T[:, None, :]


AXES = ("replica", "fsdp")


def swap(value, replica_bits, fsdp_bits):
    replicas, owners = lax.axis_size("replica"), lax.axis_size("fsdp")
    pairs = [
        (r * owners + f, (r ^ replica_bits) * owners + (f ^ fsdp_bits))
        for r in range(replicas)
        for f in range(owners)
    ]
    return lax.ppermute(value, AXES, pairs)


def swap_owner(value):
    return swap(value, 0, 1)


def swap_core(value):
    return swap(value, 1, 0)


def join(place, own, other, axis):
    return jnp.where(
        place == 0,
        jnp.concatenate([own, other], axis=axis),
        jnp.concatenate([other, own], axis=axis),
    )


def part_of(value, place, parts, axis):
    size = value.shape[axis] // parts
    return lax.dynamic_slice_in_dim(value, place * size, size, axis)


def chip_bits():
    chips = lax.axis_size("replica") // 2
    return max(chips.bit_length() - 1, 0)


def scatter_sum(block, order):
    chip = lax.axis_index("replica") // 2
    rows, cols = block.shape
    kept = block.reshape((2,) * len(order) + (rows >> len(order), cols))
    for bit in order:
        mine = (chip >> bit) & 1
        sent = lax.dynamic_index_in_dim(kept, 1 - mine, 0, keepdims=False).astype(jnp.bfloat16)
        got = swap(sent, 2 << bit, 0)
        kept = lax.dynamic_index_in_dim(kept, mine, 0, keepdims=False) + got.astype(jnp.float32)
    return kept


def spread(chunk, order):
    chip = lax.axis_index("replica") // 2
    chunk = chunk.astype(jnp.bfloat16)
    for bit in reversed(order):
        chunk = join((chip >> bit) & 1, chunk, swap(chunk, 2 << bit, 0), 0)
    return chunk


def orders():
    first = list(range(chip_bits()))
    second = first[1:2] + first[:1] + first[2:]
    return (first, second)


def total_over_chips(block):
    half = block.shape[0] // 2
    parts = []
    for at, order in enumerate(orders()):
        parts.append(spread(scatter_sum(block[at * half : (at + 1) * half], order), order))
    return jnp.concatenate(parts, axis=0)


def rows_product(left, right):
    return lax.dot_general(
        left, right, (((0,), (0,)), ((), ())), preferred_element_type=jnp.float32
    )


def per_device(
    tokens,
    seq_lens,
    norm_gain,
    in_weight,
    conv_weight,
    conv_bias,
    step_bias,
    decay_log,
    skip_gain,
    out_gain,
    out_weight,
    cotangent,
):
    owner = lax.axis_index("fsdp")
    core = lax.axis_index("replica") % 2
    owners = lax.axis_size("fsdp")
    row_count, width = tokens.shape
    inner_width = out_weight.shape[0] * owners
    channels = conv_bias.shape[0] * owners
    head_count = skip_gain.shape[0] * owners
    state_width = (channels - inner_width) // 2
    head_size = inner_width // head_count
    taps = conv_weight.shape[0]
    pieces = (conv_weight, conv_bias, step_bias, decay_log, skip_gain, out_gain)
    packed = jnp.concatenate([piece.reshape(-1) for piece in pieces])
    packed_other = swap_owner(packed)
    full = []
    at = 0
    for piece in pieces:
        other = packed_other[at : at + piece.size].reshape(piece.shape)
        at += piece.size
        full.append(join(owner, piece, other, piece.ndim - 1).astype(jnp.float32))
    conv_full, shift_full, bias_full, log_full, skip_float, out_scale_full = full
    tokens_pair = jnp.concatenate([tokens, swap_owner(tokens)], axis=0)
    cotangent_pair = jnp.concatenate([cotangent, swap_owner(cotangent)], axis=0)
    values_pair = tokens_pair.astype(jnp.float32)
    inverse_rms = lax.rsqrt(jnp.mean(values_pair * values_pair, axis=-1, keepdims=True) + EPSILON)
    gain_half = norm_gain.astype(jnp.float32)
    means_half = part_of(values_pair, owner, owners, 1) * inverse_rms
    normed_half = (means_half * gain_half).astype(jnp.bfloat16)
    part_rest = jnp.dot(
        normed_half, in_weight[:, inner_width:], preferred_element_type=jnp.float32
    )
    rest_other = swap_owner(part_rest[row_count:].astype(jnp.bfloat16))
    part_gate = jnp.dot(
        normed_half, in_weight[:, :inner_width], preferred_element_type=jnp.float32
    )
    gate_other = swap_owner(part_gate[row_count:].astype(jnp.bfloat16))
    part_q = lax.dot_general(
        cotangent_pair, out_weight, (((1,), (1,)), ((), ())), preferred_element_type=jnp.float32
    )
    q_other = swap_owner(part_q[row_count:].astype(jnp.bfloat16))
    grad_out_normed = join(owner, part_q[:row_count], q_other.astype(jnp.float32), 1)
    rest = part_rest[:row_count] + rest_other.astype(jnp.float32)
    gate_part = part_gate[:row_count] + gate_other.astype(jnp.float32)
    normed_all = jnp.concatenate([normed_half, swap_core(normed_half)], axis=0)
    cotangent_all = jnp.concatenate([cotangent_pair, swap_core(cotangent_pair)], axis=0)

    position, segment, seg_start = segment_layout(seq_lens[0], row_count)
    mixed_in = rest[:, :channels]
    rate_raw = rest[:, channels:]
    prepare = partial(conv_and_rates, position=position, seg_start=seg_start)
    (active, step_size, cumulative), prepare_pullback = jax.vjp(
        prepare, mixed_in, rate_raw, conv_full, shift_full, bias_full, log_full
    )
    x_active = active[:, :inner_width]
    head_input = x_active.reshape(row_count, head_count, head_size).astype(jnp.bfloat16)
    state_input = active[:, inner_width : inner_width + state_width].astype(jnp.bfloat16)
    state_output = active[:, inner_width + state_width :].astype(jnp.bfloat16)
    inner_part = lax.dot_general(
        state_output, state_input, (((1,), (1,)), ((), ())), preferred_element_type=jnp.float32
    )
    same_mask = (position[None, :] <= position[:, None]) & (
        segment[None, :] == segment[:, None]
    )
    mixing_float, mixing_pullback = jax.vjp(
        partial(decay_weights, same_mask=same_mask), inner_part, cumulative, cumulative, step_size
    )
    mixing = mixing_float.astype(jnp.bfloat16)
    scan_parts = jnp.einsum("hts,shp->thp", mixing, head_input, preferred_element_type=jnp.float32)
    scan_out = scan_parts.reshape(row_count, inner_width)
    direct = (
        x_active.reshape(row_count, head_count, head_size) * skip_float[None, :, None]
    ).reshape(row_count, inner_width)
    mixed_out = scan_out + direct
    out_normed, gated_pullback = jax.vjp(gated_norm, mixed_out, gate_part, out_scale_full)
    out_low = out_normed.astype(jnp.bfloat16)
    out_pair = jnp.concatenate(
        [
            part_of(out_low, owner, owners, 1),
            swap_owner(part_of(out_low, 1 - owner, owners, 1)),
        ],
        axis=0,
    )
    branch = jnp.dot(out_pair, out_weight, preferred_element_type=jnp.float32)
    branch_other = swap_owner(branch[row_count:].astype(jnp.bfloat16))
    block_out = (
        values_pair[:row_count] + branch[:row_count] + branch_other.astype(jnp.float32)
    ).astype(jnp.bfloat16)
    out_all = jnp.concatenate(
        [part_of(out_pair, core, 2, 1), swap_core(part_of(out_pair, 1 - core, 2, 1))], axis=0
    )
    out_total = total_over_chips(rows_product(out_all, cotangent_all))

    grad_mixed, grad_gate, out_gain_grad = gated_pullback(grad_out_normed)
    gate_low = grad_gate.astype(jnp.bfloat16)
    gate_pair = jnp.concatenate([gate_low, swap_owner(gate_low)], axis=0)
    gate_all = jnp.concatenate(
        [part_of(gate_pair, core, 2, 1), swap_core(part_of(gate_pair, 1 - core, 2, 1))], axis=0
    )
    gate_total = total_over_chips(rows_product(normed_all, gate_all))
    grad_heads = grad_mixed.reshape(row_count, head_count, head_size)
    skip_gain_grad = jnp.sum(
        grad_heads * x_active.reshape(row_count, head_count, head_size), axis=(0, 2)
    )
    grad_low = grad_heads.astype(jnp.bfloat16)
    grad_input = grad_heads * skip_float[None, :, None]
    grad_mixing = jnp.einsum(
        "thp,shp->hts", grad_low, head_input, preferred_element_type=jnp.float32
    )
    grad_input = grad_input + jnp.einsum(
        "hts,thp->shp", mixing, grad_low, preferred_element_type=jnp.float32
    )
    grad_inner, grad_cum_rows, grad_cum_keys, grad_step_keys = mixing_pullback(grad_mixing)
    grad_inner_low = grad_inner.astype(jnp.bfloat16)
    grad_state_out = jnp.dot(grad_inner_low, state_input, preferred_element_type=jnp.float32)
    grad_state_in = rows_product(grad_inner_low, state_output)
    grad_cum = grad_cum_keys + grad_cum_rows
    grad_active = jnp.concatenate(
        [grad_input.reshape(row_count, inner_width), grad_state_in, grad_state_out], axis=1
    )
    grad_mixed_in, grad_rate_raw, conv_grad, shift_grad, bias_grad, log_grad = prepare_pullback(
        (grad_active, grad_step_keys, grad_cum)
    )
    rest_low = jnp.concatenate([grad_mixed_in, grad_rate_raw], axis=1).astype(jnp.bfloat16)
    rest_pair = jnp.concatenate([rest_low, swap_owner(rest_low)], axis=0)
    mixed_pair, rate_pair = rest_pair[:, :channels], rest_pair[:, channels:]
    rest_all = jnp.concatenate(
        [
            jnp.concatenate([part_of(mixed_pair, core, 2, 1), rate_pair], axis=1),
            swap_core(
                jnp.concatenate([part_of(mixed_pair, 1 - core, 2, 1), rate_pair], axis=1)
            ),
        ],
        axis=0,
    )
    rest_total = total_over_chips(rows_product(normed_all, rest_all))
    grad_normed = lax.dot_general(
        gate_pair,
        in_weight[:, :inner_width],
        (((1,), (1,)), ((), ())),
        preferred_element_type=jnp.float32,
    ) + lax.dot_general(
        rest_pair,
        in_weight[:, inner_width:],
        (((1,), (1,)), ((), ())),
        preferred_element_type=jnp.float32,
    )
    norm_gain_grad = jnp.sum(grad_normed * means_half, axis=0)
    grad_means = grad_normed * gain_half
    grad_means_full = join(
        owner, grad_means[:row_count], swap_owner(grad_means[row_count:]), 1
    )
    means = values_pair[:row_count] * inverse_rms[:row_count]
    grad_values = inverse_rms[:row_count] * (
        grad_means_full
        - means * jnp.mean(grad_means_full * means, axis=-1, keepdims=True)
    )
    grad_tokens = cotangent.astype(jnp.float32) + grad_values
    norm_wide = join(owner, norm_gain_grad, jnp.zeros_like(norm_gain_grad), 0)
    smalls = (norm_wide, conv_grad, shift_grad, bias_grad, log_grad, skip_gain_grad, out_gain_grad)
    sums = lax.psum(jnp.concatenate([item.reshape(-1) for item in smalls]), AXES)
    small_out = []
    at = 0
    for item in smalls:
        whole = sums[at : at + item.size].reshape(item.shape)
        at += item.size
        small_out.append(part_of(whole, owner, owners, item.ndim - 1))
    out_weight_grad = join(core, out_total, swap_core(out_total), 0).astype(jnp.float32)
    gate_full = join(core, gate_total, swap_core(gate_total), 1)
    half_channels = channels // 2
    rest_other_core = swap_core(rest_total)
    mixed_full = join(
        core, rest_total[:, :half_channels], rest_other_core[:, :half_channels], 1
    )
    in_weight_grad = jnp.concatenate(
        [gate_full, mixed_full, rest_total[:, half_channels:]], axis=1
    ).astype(jnp.float32)
    return (
        block_out,
        grad_tokens,
        small_out[0],
        in_weight_grad,
        small_out[1],
        small_out[2],
        small_out[3],
        small_out[4],
        small_out[5],
        small_out[6],
        out_weight_grad,
    )


def solution(mesh):
    placed = (
        P(("replica", "fsdp"), None),
        P(("replica", "fsdp"), None),
        P("fsdp"),
        P("fsdp", None),
        P(None, "fsdp"),
        P("fsdp"),
        P("fsdp"),
        P("fsdp"),
        P("fsdp"),
        P("fsdp"),
        P("fsdp", None),
        P(("replica", "fsdp"), None),
    )
    return jax.shard_map(
        per_device,
        mesh=mesh,
        in_specs=placed,
        out_specs=(
            P(("replica", "fsdp"), None),
            P(("replica", "fsdp"), None),
            P("fsdp"),
            P("fsdp", None),
            P(None, "fsdp"),
            P("fsdp"),
            P("fsdp"),
            P("fsdp"),
            P("fsdp"),
            P("fsdp"),
            P("fsdp", None),
        ),
        check_vma=False,
    )
```

```python
import jax
import jax.numpy as jnp
from jax import lax
from jax.experimental import pallas as pl
from jax.experimental.pallas import tpu as pltpu
from jax.sharding import PartitionSpec as P

EPSILON = 1e-05
AXES = ("replica", "fsdp")
OWNER, LENGTH_ONE, LENGTH_TWO, CORE, BITS = 0, 1, 2, 3, 4
LANES = 128
FAR = -1e30


def full_rows(meta_ref, mine_ref, peer_ref):
    first = meta_ref[0] == 0
    mine, peer = mine_ref[...], peer_ref[...]
    return (jnp.where(first, mine, peer), jnp.where(first, peer, mine), mine + peer)


def row_marks(meta_ref, rows):
    end_one, end_two = meta_ref[1], meta_ref[1] + meta_ref[2]
    position = lax.broadcasted_iota(jnp.int32, (rows, 1), 0)
    start = jnp.where(position >= end_two, end_two, jnp.where(position >= end_one, end_one, 0))
    return (position, start)


def kept_pairs(start, rows):
    key = lax.broadcasted_iota(jnp.int32, (rows, rows), 1)
    query = lax.broadcasted_iota(jnp.int32, (rows, rows), 0)
    return (key <= query) & (key >= start)


def channel_row(low, high, row, tile):
    half = low.shape[1] // LANES
    source = low if tile < half else high
    at = (tile if tile < half else tile - half) * LANES
    return source[row : row + 1, at : at + LANES]


def exact_dot(left, right):
    return jnp.dot(
        left, right, precision=lax.Precision.HIGHEST, preferred_element_type=jnp.float32
    )


def pair_operand(values, lane):
    zero = jnp.zeros_like(values)
    return jnp.concatenate(
        [jnp.where(lane < LANES // 2, values, zero), jnp.where(lane < LANES // 2, zero, values)],
        axis=0,
    )


def forward_body(meta_ref, own_ref, got_ref, mine_ref, peer_ref, xbc_ref, conv_ref, mixed_ref, rates_ref):
    rows, channels = conv_ref.shape
    tiles = channels // LANES
    pairs = tiles - 2
    heads = 2 * pairs
    taps = 4
    low, high, both = full_rows(meta_ref, mine_ref, peer_ref)
    position, start = row_marks(meta_ref, rows)
    usable = [position - (taps - 1 - k) >= start for k in range(taps)]
    lane = lax.broadcasted_iota(jnp.int32, (1, LANES), 1)
    bias = both[6:7, 0:heads]
    decay = both[6:7, LANES : LANES + heads]
    skip = both[6:7, 2 * LANES : 2 * LANES + heads]
    rate = own_ref[:, channels:] + got_ref[:, channels:].astype(jnp.float32) + bias
    step = jnp.maximum(rate, 0.0) + jnp.log1p(jnp.exp(-jnp.abs(rate)))
    rate_sigmoid = jax.nn.sigmoid(rate)
    lower = jnp.where(
        lax.broadcasted_iota(jnp.int32, (rows, rows), 1)
        <= lax.broadcasted_iota(jnp.int32, (rows, rows), 0),
        1.0,
        0.0,
    ).astype(jnp.float32)
    cum = exact_dot(lower, step * -jnp.exp(decay))
    rates_ref[0] = step
    rates_ref[1] = cum
    rates_ref[2] = rate_sigmoid
    step_t, cum_t = step.T, cum.T
    mask = kept_pairs(start, rows)

    def active_tile(tile):
        at = tile * LANES
        xbc = own_ref[:, at : at + LANES] + got_ref[:, at : at + LANES].astype(jnp.float32)
        xbc_ref[:, at : at + LANES] = xbc
        conv = channel_row(low, high, 4, tile) + channel_row(low, high, taps - 1, tile) * xbc
        for k in range(taps - 1):
            shifted = pltpu.roll(xbc, taps - 1 - k, 0)
            conv = conv + channel_row(low, high, k, tile) * jnp.where(usable[k], shifted, 0.0)
        conv_ref[:, at : at + LANES] = conv
        return conv * jax.nn.sigmoid(conv)

    keys = active_tile(tiles - 2).astype(jnp.bfloat16)
    queries = active_tile(tiles - 1).astype(jnp.bfloat16)
    inner = lax.dot_general(
        queries, keys, (((1,), (1,)), ((), ())), preferred_element_type=jnp.float32
    )
    for pair in range(pairs):
        act = active_tile(pair)
        mixing = []
        for h in (2 * pair, 2 * pair + 1):
            spread = jnp.where(mask, cum[:, h : h + 1] - cum_t[h : h + 1, :], FAR)
            mixing.append((inner * jnp.exp(spread) * step_t[h : h + 1, :]).astype(jnp.bfloat16))
        scan = jnp.dot(
            jnp.concatenate(mixing, axis=1),
            pair_operand(act.astype(jnp.bfloat16), lane),
            preferred_element_type=jnp.float32,
        )
        gain = jnp.where(
            lane < LANES // 2, skip[:, 2 * pair : 2 * pair + 1], skip[:, 2 * pair + 1 : 2 * pair + 2]
        )
        mixed_ref[:, pair * LANES : (pair + 1) * LANES] = scan + gain * act


def gate_body(meta_ref, mixed_ref, own_ref, got_ref, q_own_ref, q_got_ref, mine_ref, peer_ref, keep_ref, send_ref, dgate_ref, dmixed_ref, gain_grad_ref):
    rows, inner_width = mixed_ref.shape
    half = inner_width // 2
    first = meta_ref[0] == 0
    low, high, _ = full_rows(meta_ref, mine_ref, peer_ref)
    width = 2 * LANES
    tiles = inner_width // width

    def cut(tile):
        return slice(tile * width, (tile + 1) * width)

    def gate_of(tile):
        gate = own_ref[:, cut(tile)] + got_ref[:, cut(tile)].astype(jnp.float32)
        return (gate, jax.nn.sigmoid(gate))

    def half_cut(tile):
        at = tile * width % half
        return slice(at, at + width)

    def gain_of(tile):
        return (low if tile * width < half else high)[5:6, half_cut(tile)]

    def q_of(tile):
        own = q_own_ref[:, half_cut(tile)]
        got = q_got_ref[:, half_cut(tile)].astype(jnp.float32)
        return jnp.where(first == (tile * width < half), own, got)

    squares = jnp.zeros((rows, 1), jnp.float32)
    cross = jnp.zeros((rows, 1), jnp.float32)
    for tile in range(tiles):
        gate, sigmoid = gate_of(tile)
        gated = mixed_ref[:, cut(tile)] * (gate * sigmoid)
        squares = squares + jnp.sum(gated * gated, axis=1, keepdims=True)
        cross = cross + jnp.sum(q_of(tile) * gain_of(tile) * gated, axis=1, keepdims=True)
    inverse = lax.rsqrt(squares / inner_width + EPSILON)
    mean_cross = cross * inverse / inner_width
    for tile in range(tiles):
        gate, sigmoid = gate_of(tile)
        silu = gate * sigmoid
        mixed = mixed_ref[:, cut(tile)]
        normed = mixed * silu * inverse
        gain = gain_of(tile)
        out = (normed * gain).astype(jnp.bfloat16)
        in_low = tile * width < half

        @pl.when(first == in_low)
        def _():
            keep_ref[:, half_cut(tile)] = out

        @pl.when(first != in_low)
        def _():
            send_ref[:, half_cut(tile)] = out

        q = q_of(tile)
        gain_grad_ref[:, cut(tile)] = jnp.sum(q * normed, axis=0, keepdims=True)
        dgated = inverse * (q * gain - normed * mean_cross)
        dmixed_ref[:, cut(tile)] = dgated * silu
        dgate_ref[tile * width // half, :, half_cut(tile)] = (
            dgated * mixed * (sigmoid * (1.0 + gate * (1.0 - sigmoid)))
        ).astype(jnp.bfloat16)


def backward_body(meta_ref, dmixed_ref, xbc_ref, conv_ref, rates_ref, mine_ref, peer_ref, gain_grad_ref, rest_ref, small_ref):
    rows, channels = conv_ref.shape
    tiles = channels // LANES
    pairs = tiles - 2
    heads = 2 * pairs
    taps = 4
    half_tiles = tiles // 2
    small_ref[...] = jnp.zeros(small_ref.shape, jnp.float32)
    low, high, both = full_rows(meta_ref, mine_ref, peer_ref)
    position, start = row_marks(meta_ref, rows)
    usable = [position - (taps - 1 - k) >= start for k in range(taps)]
    lane = lax.broadcasted_iota(jnp.int32, (1, LANES), 1)
    decay = both[6:7, LANES : LANES + heads]
    skip = both[6:7, 2 * LANES : 2 * LANES + heads]
    step, cum, rate_sigmoid = rates_ref[0], rates_ref[1], rates_ref[2]
    step_t, cum_t = step.T, cum.T
    mask = kept_pairs(start, rows)

    def cut(tile):
        return slice(tile * LANES, (tile + 1) * LANES)

    def act_of(tile):
        conv = conv_ref[:, cut(tile)]
        sigmoid = jax.nn.sigmoid(conv)
        return (conv * sigmoid, sigmoid * (1.0 + conv * (1.0 - sigmoid)))

    def finish_tile(tile, dconv):
        owner, at = tile // half_tiles, tile % half_tiles * LANES
        xbc = xbc_ref[:, cut(tile)]
        small_ref[owner, 4:5, at : at + LANES] = jnp.sum(dconv, axis=0, keepdims=True)
        small_ref[owner, taps - 1 : taps, at : at + LANES] = jnp.sum(
            dconv * xbc, axis=0, keepdims=True
        )
        total = channel_row(low, high, taps - 1, tile) * dconv
        for k in range(taps - 1):
            behind = taps - 1 - k
            kept = jnp.where(usable[k], dconv, 0.0)
            small_ref[owner, k : k + 1, at : at + LANES] = jnp.sum(
                kept * pltpu.roll(xbc, behind, 0), axis=0, keepdims=True
            )
            total = total + channel_row(low, high, k, tile) * pltpu.roll(kept, rows - behind, 0)
        rest_ref[owner, :, at : at + LANES] = total.astype(jnp.bfloat16)

    keys_act, keys_slope = act_of(tiles - 2)
    queries_act, queries_slope = act_of(tiles - 1)
    keys, queries = keys_act.astype(jnp.bfloat16), queries_act.astype(jnp.bfloat16)
    inner = lax.dot_general(
        queries, keys, (((1,), (1,)), ((), ())), preferred_element_type=jnp.float32
    )
    dinner = jnp.zeros((rows, rows), jnp.float32)
    dstep_rows = []
    dcum = jnp.zeros((rows, heads), jnp.float32)
    skip_grad = jnp.zeros((1, heads), jnp.float32)
    head_lane = lax.broadcasted_iota(jnp.int32, (1, heads), 1)
    for pair in range(pairs):
        act, slope = act_of(pair)
        dmixed = dmixed_ref[:, cut(pair)]
        dscan = dmixed.astype(jnp.bfloat16)
        operand = pair_operand(act.astype(jnp.bfloat16), lane)
        dmixing = lax.dot_general(
            dscan, operand, (((1,), (1,)), ((), ())), preferred_element_type=jnp.float32
        )
        direct = jnp.sum(dmixed * act, axis=0, keepdims=True)
        mixing = []
        for j in range(2):
            h = 2 * pair + j
            spread = jnp.where(mask, cum[:, h : h + 1] - cum_t[h : h + 1, :], FAR)
            decays = jnp.exp(spread)
            step_row = step_t[h : h + 1, :]
            weight = inner * decays
            mixing.append((weight * step_row).astype(jnp.bfloat16))
            grad = dmixing[:, j * rows : (j + 1) * rows]
            dinner = dinner + grad * decays * step_row
            term = grad * weight
            dstep_rows.append(jnp.sum(term, axis=0, keepdims=True))
            dcum = dcum + jnp.where(
                head_lane == h, jnp.sum(term * step_row, axis=1, keepdims=True), 0.0
            )
            in_head = (lane < LANES // 2) if j == 0 else (lane >= LANES // 2)
            skip_grad = skip_grad + jnp.where(
                head_lane == h,
                jnp.sum(jnp.where(in_head, direct, 0.0), axis=1, keepdims=True),
                0.0,
            )
        dinput = lax.dot_general(
            jnp.concatenate(mixing, axis=1),
            dscan,
            (((0,), (0,)), ((), ())),
            preferred_element_type=jnp.float32,
        )
        gain = jnp.where(
            lane < LANES // 2, skip[:, 2 * pair : 2 * pair + 1], skip[:, 2 * pair + 1 : 2 * pair + 2]
        )
        dact = jnp.where(lane < LANES // 2, dinput[:rows], dinput[rows:]) + gain * dmixed
        finish_tile(pair, dact * slope)
    dinner_low = dinner.astype(jnp.bfloat16)
    dqueries = jnp.dot(dinner_low, keys, preferred_element_type=jnp.float32)
    dkeys = lax.dot_general(
        dinner_low, queries, (((0,), (0,)), ((), ())), preferred_element_type=jnp.float32
    )
    finish_tile(tiles - 2, dkeys * keys_slope)
    finish_tile(tiles - 1, dqueries * queries_slope)
    dstep_t = jnp.concatenate(dstep_rows, axis=0)
    dstep = dstep_t.T
    dcum = dcum - step * dstep
    upper = jnp.where(
        lax.broadcasted_iota(jnp.int32, (rows, rows), 1)
        >= lax.broadcasted_iota(jnp.int32, (rows, rows), 0),
        1.0,
        0.0,
    ).astype(jnp.float32)
    drate = exact_dot(upper, dcum)
    speed = jnp.exp(decay)
    draw = (dstep - drate * speed) * rate_sigmoid
    for owner in range(2):
        rest_ref[owner, :, channels // 2 :] = draw.astype(jnp.bfloat16)
    bias_grad = jnp.sum(draw, axis=0, keepdims=True)
    decay_grad = jnp.sum(-drate * step * speed, axis=0, keepdims=True)
    half_inner = pairs * LANES // 2
    half_heads = heads // 2
    for owner in range(2):
        small_ref[owner, 5:6, 0:half_inner] = gain_grad_ref[
            :, owner * half_inner : (owner + 1) * half_inner
        ]
        for place, item in enumerate((bias_grad, decay_grad, skip_grad)):
            at = place * LANES
            small_ref[owner, 6:7, at : at + half_heads] = item[
                :, owner * half_heads : (owner + 1) * half_heads
            ]


def whole(shape, dtype):
    return jax.ShapeDtypeStruct(shape, dtype)


def call(body, out_shape, operands, flops):
    in_specs = [pl.BlockSpec(memory_space=pltpu.SMEM)] + [
        pl.BlockSpec(memory_space=pltpu.VMEM) for _ in operands[1:]
    ]
    moved = sum(item.size * item.dtype.itemsize for item in (*operands, *out_shape))
    return pl.pallas_call(
        body,
        out_shape=out_shape,
        in_specs=in_specs,
        out_specs=[pl.BlockSpec(memory_space=pltpu.VMEM) for _ in out_shape],
        compiler_params=pltpu.CompilerParams(vmem_limit_bytes=40 << 20),
        cost_estimate=pl.CostEstimate(flops=flops, bytes_accessed=moved, transcendentals=0),
    )(*operands)


def unit_rows(tokens):
    values = tokens.astype(jnp.float32)
    return lax.rsqrt(jnp.mean(values * values, axis=-1, keepdims=True) + EPSILON)


def project_body(meta_ref, tokens_ref, gain_ref, weight_ref, normed_ref, rest_ref, gate_ref):
    depth = weight_ref.shape[0]
    inner_width = gate_ref.shape[1]
    inverse = unit_rows(tokens_ref[...])
    mine = pl.ds(pl.multiple_of(meta_ref[OWNER] * depth, LANES), depth)
    means = tokens_ref[:, mine].astype(jnp.float32) * inverse
    normed = (means * gain_ref[...]).astype(jnp.bfloat16)
    normed_ref[...] = normed
    rest_ref[...] = jnp.dot(
        normed, weight_ref[:, inner_width:], preferred_element_type=jnp.float32
    ).astype(rest_ref.dtype)
    gate_ref[...] = jnp.dot(
        normed, weight_ref[:, :inner_width], preferred_element_type=jnp.float32
    ).astype(gate_ref.dtype)


def lanes_product(left, right):
    return lax.dot_general(
        left, right, (((1,), (1,)), ((), ())), preferred_element_type=jnp.float32
    )


def rows_product(left, right):
    return lax.dot_general(
        left, right, (((0,), (0,)), ((), ())), preferred_element_type=jnp.float32
    )


def cotangent_body(meta_ref, own_ref, other_ref, weight_ref, q_own_ref, q_send_ref):
    q_own_ref[...] = lanes_product(own_ref[...], weight_ref[...])
    q_send_ref[...] = lanes_product(other_ref[...], weight_ref[...]).astype(q_send_ref.dtype)


def branch_body(meta_ref, keep_ref, got_ref, weight_ref, own_ref, send_ref):
    own_ref[...] = jnp.dot(
        keep_ref[...], weight_ref[...], preferred_element_type=jnp.float32
    )
    send_ref[...] = jnp.dot(
        got_ref[...], weight_ref[...], preferred_element_type=jnp.float32
    ).astype(send_ref.dtype)


def input_grad_body(meta_ref, tokens_ref, other_ref, gain_ref, weight_ref, gate_own_ref, gate_got_ref, rest_own_ref, rest_got_ref, dmeans_ref, send_ref, gain_grad_ref):
    depth = weight_ref.shape[0]
    half_inner = gate_own_ref.shape[2]
    half_rest = rest_own_ref.shape[2] - (weight_ref.shape[1] - 2 * half_inner) % LANES
    mine = pl.ds(pl.multiple_of(meta_ref[OWNER] * depth, LANES), depth)
    gain = gain_ref[...]
    gain_grad = jnp.zeros_like(gain)
    for rows_ref, gate_ref, rest_ref, out_ref in (
        (other_ref, gate_got_ref, rest_got_ref, send_ref),
        (tokens_ref, gate_own_ref, rest_own_ref, dmeans_ref),
    ):
        dnormed = jnp.zeros(out_ref.shape, jnp.float32)
        at = 0
        for part in (
            gate_ref[0],
            gate_ref[1],
            rest_ref[0, :, :half_rest],
            rest_ref[1, :, :half_rest],
            rest_ref[0, :, half_rest:],
        ):
            width = part.shape[1]
            dnormed = dnormed + lanes_product(part, weight_ref[:, at : at + width])
            at += width
        means = rows_ref[:, mine].astype(jnp.float32) * unit_rows(rows_ref[...])
        gain_grad = gain_grad + jnp.sum(dnormed * means, axis=0, keepdims=True)
        out_ref[...] = dnormed * gain
    gain_grad_ref[...] = gain_grad


def tokens_grad_body(meta_ref, tokens_ref, cotangent_ref, own_ref, got_ref, out_ref):
    half = own_ref.shape[1]
    first = meta_ref[OWNER] == 0
    inverse = unit_rows(tokens_ref[...])
    parts = []
    cross = jnp.zeros_like(inverse)
    for side in range(2):
        cut = slice(side * half, (side + 1) * half)
        dmeans = jnp.where(first == (side == 0), own_ref[...], got_ref[...])
        means = tokens_ref[:, cut].astype(jnp.float32) * inverse
        cross = cross + jnp.sum(dmeans * means, axis=1, keepdims=True)
        parts.append((cut, dmeans, means))
    for cut, dmeans, means in parts:
        out_ref[:, cut] = cotangent_ref[:, cut].astype(jnp.float32) + inverse * (
            dmeans - means * (cross / (2 * half))
        )


def block_grad(left_refs, right_refs, left_at, core, outs, bits):
    half = 2 * LANES
    right = jnp.concatenate(
        [ref[...] if len(ref.shape) == 2 else ref[core] for ref in right_refs], axis=0
    )
    for order, (send_ref, keep_ref) in enumerate(outs):
        for ref, bit in ((send_ref, 1 - bits[order]), (keep_ref, bits[order])):
            cut = order * half + bit * LANES
            left = jnp.concatenate(
                [
                    left_ref[:, pl.ds(pl.multiple_of(at + cut, LANES), LANES)]
                    for left_ref, at in zip(left_refs, left_at)
                ],
                axis=0,
            )
            ref[...] = rows_product(left, right).astype(ref.dtype)


def block_grad_body(quarter_left, meta_ref, l_own, l_got, l_sib, r_own, r_got, r_sib, send_a, keep_a, send_b, keep_b):
    core = meta_ref[CORE]
    at = core * l_sib.shape[1] if quarter_left else 0
    block_grad(
        (l_own, l_got, l_sib),
        (r_own, r_got, r_sib),
        (at, at, 0),
        core,
        ((send_a, keep_a), (send_b, keep_b)),
        (meta_ref[BITS], meta_ref[BITS + 1]),
    )


def sum_step_body(step, meta_ref, keep_a, got_a, keep_b, got_b, *outs):
    if step == 2:
        for keep, got, out in ((keep_a, got_a, outs[0]), (keep_b, got_b, outs[1])):
            out[...] = (keep[...] + got[...].astype(jnp.float32)).astype(out.dtype)
        return
    rows = keep_a.shape[0] // 2
    bits = (
        (meta_ref[BITS + 1], meta_ref[BITS]) if step == 0 else (meta_ref[BITS + 2],) * 2
    )
    for order, (keep, got) in enumerate(((keep_a, got_a), (keep_b, got_b))):
        for out, bit in ((outs[2 * order], 1 - bits[order]), (outs[2 * order + 1], bits[order])):
            cut = pl.ds(pl.multiple_of(bit * rows, rows), rows)
            out[...] = (keep[cut, :] + got[cut, :].astype(jnp.float32)).astype(out.dtype)


def chunk_places(meta_ref, order):
    outer, inner = meta_ref[BITS + 1 - order], meta_ref[BITS + 2]
    places = []
    for p in range(4):
        high = outer if p < 2 else 1 - outer
        low = inner if p % 2 == 0 else 1 - inner
        places.append(2 * high + low)
    return places


def write_chunks(meta_ref, order, half, out_ref, groups):
    own_half = meta_ref[BITS + order] == half
    for p, place in enumerate(chunk_places(meta_ref, order)):
        size = LANES // 4
        rows = slice(p * size, (p + 1) * size)
        target = pl.ds(pl.multiple_of(place * size, size), size)
        for cut, choose in groups:
            out_ref[target, cut] = choose(own_half, rows).astype(jnp.float32)


def in_weight_body(meta_ref, *refs):
    out_ref = refs[-1]
    gate, rest = refs[0:8], refs[8:16]
    first = meta_ref[CORE] == 0
    step = pl.program_id(0)
    half_inner = gate[0].shape[1]
    half_channels = rest[0].shape[1] // LANES * LANES
    tail = rest[0].shape[1] - half_channels

    def chooser(group, order, side, cut):
        own, got, sib_own, sib_got = group[4 * order : 4 * order + 4]

        def choose(own_half, rows):
            mine = jnp.where(own_half, own[rows, cut], got[rows, cut])
            sibling = jnp.where(own_half, sib_own[rows, cut], sib_got[rows, cut])
            return jnp.where(first == (side == 0), mine, sibling)

        return choose

    for order in range(2):
        for half in range(2):

            @pl.when(step == 2 * order + half)
            def _():
                groups = []
                for side in range(2):
                    at = side * half_inner
                    groups.append(
                        (
                            slice(at, at + half_inner),
                            chooser(gate, order, side, slice(0, half_inner)),
                        )
                    )
                    at = 2 * half_inner + side * half_channels
                    groups.append(
                        (
                            slice(at, at + half_channels),
                            chooser(rest, order, side, slice(0, half_channels)),
                        )
                    )
                at = 2 * half_inner + 2 * half_channels
                groups.append(
                    (
                        slice(at, at + tail),
                        chooser(rest, order, 0, slice(half_channels, half_channels + tail)),
                    )
                )
                write_chunks(meta_ref, order, half, out_ref, groups)


def out_weight_body(meta_ref, *refs):
    out_ref = refs[-1]
    pieces = refs[:-1]
    step = pl.program_id(0)
    cut = slice(0, out_ref.shape[1])
    for side in range(2):
        for order in range(2):
            for half in range(2):

                @pl.when(step == 4 * side + 2 * order + half)
                def _():
                    own, got, sib_own, sib_got = pieces[4 * order : 4 * order + 4]

                    def choose(own_half, rows):
                        mine = jnp.where(own_half, own[rows, :], got[rows, :])
                        sibling = jnp.where(own_half, sib_own[rows, :], sib_got[rows, :])
                        return jnp.where((meta_ref[CORE] == 0) == (side == 0), mine, sibling)

                    write_chunks(meta_ref, order, half, out_ref, [(cut, choose)])


def assemble(body, out, operands):
    return pl.pallas_call(
        body,
        grid=(out.shape[0] // LANES,),
        out_shape=out,
        in_specs=[pl.BlockSpec(memory_space=pltpu.SMEM)]
        + [pl.BlockSpec(item.shape, lambda i: (0, 0)) for item in operands[1:]],
        out_specs=pl.BlockSpec((LANES, out.shape[1]), lambda i: (i, 0)),
        compiler_params=pltpu.CompilerParams(vmem_limit_bytes=48 << 20),
        cost_estimate=pl.CostEstimate(
            flops=out.size, bytes_accessed=out.size * 6, transcendentals=0
        ),
    )(*operands)


def swap(value, replica_bits, fsdp_bits):
    replicas, owners = lax.axis_size("replica"), lax.axis_size("fsdp")
    pairs = [
        (r * owners + f, (r ^ replica_bits) * owners + (f ^ fsdp_bits))
        for r in range(replicas)
        for f in range(owners)
    ]
    return lax.ppermute(value, AXES, pairs)


def swap_owner(value):
    return swap(value, 0, 1)


def swap_core(value):
    return swap(value, 1, 0)


def swap_chip(value, bit):
    return swap(value, 2 << bit, 0)


def join(place, own, other, axis):
    return jnp.where(
        place == 0,
        jnp.concatenate([own, other], axis=axis),
        jnp.concatenate([other, own], axis=axis),
    )


def part_of(value, place, parts, axis):
    size = value.shape[axis] // parts
    return lax.dynamic_slice_in_dim(value, place * size, size, axis)


def total_over_chips(block):
    chip = lax.axis_index("replica") // 2
    bits = range((lax.axis_size("replica") // 2).bit_length() - 1)
    rows, cols = block.shape
    kept = block.reshape((2,) * len(bits) + (rows >> len(bits), cols))
    for bit in bits:
        mine = (chip >> bit) & 1
        sent = lax.dynamic_index_in_dim(kept, 1 - mine, 0, keepdims=False).astype(jnp.bfloat16)
        got = swap_chip(sent, bit)
        kept = lax.dynamic_index_in_dim(kept, mine, 0, keepdims=False) + got.astype(jnp.float32)
    chunk = kept.astype(jnp.bfloat16)
    for bit in reversed(bits):
        chunk = join((chip >> bit) & 1, chunk, swap_chip(chunk, bit), 0)
    return chunk


def eight_chip_pieces(meta, left, right, quarter_left):
    f32, low = jnp.float32, jnp.bfloat16
    cols = right[2].shape[1]

    def pieces(rows):
        return [whole((rows, cols), low), whole((rows, cols), f32)] * 2

    def body(*refs):
        block_grad_body(quarter_left, *refs)

    send_a, keep_a, send_b, keep_b = call(body, pieces(LANES), (meta, *left, *right), 512 * 1024 * cols)
    got_a, got_b = swap_chip(send_a, 0), swap_chip(send_b, 1)

    def first(*refs):
        sum_step_body(0, *refs)

    def second(*refs):
        sum_step_body(1, *refs)

    def third(*refs):
        sum_step_body(2, *refs)

    send_a, keep_a, send_b, keep_b = call(
        first, pieces(LANES // 2), (meta, keep_a, got_a, keep_b, got_b), 0
    )
    got_a, got_b = swap_chip(send_a, 1), swap_chip(send_b, 0)
    send_a, keep_a, send_b, keep_b = call(
        second, pieces(LANES // 4), (meta, keep_a, got_a, keep_b, got_b), 0
    )
    got_a, got_b = swap_chip(send_a, 2), swap_chip(send_b, 2)
    sums = call(
        third, [whole((LANES // 4, cols), low)] * 2, (meta, keep_a, got_a, keep_b, got_b), 0
    )
    out = []
    for chunk, order in zip(sums, ((2, 1, 0), (2, 0, 1))):
        for bit in order[:2]:
            chunk = jnp.concatenate([chunk, swap_chip(chunk, bit)], axis=0)
        got = swap_chip(chunk, order[2])
        out += [chunk, got, swap_core(chunk), swap_core(got)]
    return out


def per_device(
    tokens,
    seq_lens,
    norm_gain,
    in_weight,
    conv_weight,
    conv_bias,
    step_bias,
    decay_log,
    skip_gain,
    out_gain,
    out_weight,
    cotangent,
):
    f32, low = jnp.float32, jnp.bfloat16
    owner = lax.axis_index("fsdp")
    replica = lax.axis_index("replica")
    core, chip = replica % 2, replica // 2
    chips = lax.axis_size("replica") // 2
    rows, width = tokens.shape
    half_inner = out_weight.shape[0]
    inner_width = 2 * half_inner
    half_channels = conv_bias.shape[0]
    channels = 2 * half_channels
    half_heads = skip_gain.shape[0]
    heads = 2 * half_heads
    rest_width = channels + heads
    meta = jnp.stack(
        [owner, seq_lens[0, 0], seq_lens[0, 1], core, chip & 1, (chip >> 1) & 1, (chip >> 2) & 1]
    ).astype(jnp.int32)

    def row(item):
        item = item.astype(f32).reshape(-1, item.shape[-1])
        return jnp.pad(item, ((0, 0), (0, half_channels - item.shape[-1])))

    def head_row(item):
        item = item.astype(f32)
        there = jnp.zeros_like(item)
        placed = jnp.where(
            owner == 0, jnp.concatenate([item, there]), jnp.concatenate([there, item])
        )
        return jnp.pad(placed, (0, LANES - heads))

    head_rows = jnp.concatenate([head_row(step_bias), head_row(decay_log), head_row(skip_gain)])
    mine = jnp.concatenate(
        [
            row(conv_weight),
            row(conv_bias),
            row(out_gain),
            row(head_rows),
            jnp.zeros((1, half_channels), f32),
        ],
        axis=0,
    )
    tokens_other = swap_owner(tokens)
    peer = swap_owner(mine)
    held, _ = lax.optimization_barrier((cotangent, tokens_other))
    cotangent_other = swap_owner(held)
    gain = norm_gain.astype(f32).reshape(1, -1)

    def project(source, dtype):
        return call(
            project_body,
            [
                whole((rows, width // 2), low),
                whole((rows, rest_width), dtype),
                whole((rows, inner_width), dtype),
            ],
            (meta, source, gain, in_weight),
            rows * width * (rest_width + inner_width),
        )

    normed_own, rest_own, gate_own = project(tokens, f32)
    normed_other, rest_send, gate_send = project(tokens_other, low)
    rest_got = swap_owner(rest_send)
    q_own, q_send = call(
        cotangent_body,
        [whole((rows, half_inner), f32), whole((rows, half_inner), low)],
        (meta, cotangent, cotangent_other, out_weight),
        4 * rows * width * half_inner,
    )
    q_got = swap_owner(q_send)
    gate_got = swap_owner(gate_send)
    normed_sib = swap_core(jnp.concatenate([normed_own, normed_other], axis=0))
    cotangent_sib = swap_core(jnp.concatenate([cotangent, cotangent_other], axis=0))

    xbc, conv, mixed, rates = call(
        forward_body,
        [
            whole((rows, channels), f32),
            whole((rows, channels), f32),
            whole((rows, inner_width), f32),
            whole((3, rows, heads), f32),
        ],
        (meta, rest_own, rest_got, mine, peer),
        10**9,
    )
    out_keep, out_send, dgate, dmixed, gain_grad = call(
        gate_body,
        [
            whole((rows, half_inner), low),
            whole((rows, half_inner), low),
            whole((2, rows, half_inner), low),
            whole((rows, inner_width), f32),
            whole((1, inner_width), f32),
        ],
        (meta, mixed, gate_own, gate_got, q_own, q_got, mine, peer),
        10**9,
    )
    out_got = swap_owner(out_send)
    dgate_got = swap_owner(dgate)
    drest, small = call(
        backward_body,
        [
            whole((2, rows, half_channels + heads), low),
            whole((2, 8, half_channels), f32),
        ],
        (meta, dmixed, xbc, conv, rates, mine, peer, gain_grad),
        10**9,
    )
    drest_got = swap_owner(drest)
    out_sib = swap_core(
        jnp.concatenate(
            [part_of(out_keep, 1 - core, 2, 1), part_of(out_got, 1 - core, 2, 1)], axis=0
        )
    )

    def sibling_part(own, got):
        return swap_core(
            jnp.concatenate(
                [
                    lax.dynamic_index_in_dim(own, 1 - core, 0, keepdims=False),
                    lax.dynamic_index_in_dim(got, 1 - core, 0, keepdims=False),
                ],
                axis=0,
            )
        )

    dgate_sib = sibling_part(dgate, dgate_got)
    drest_sib = sibling_part(drest, drest_got)
    normed_all = (normed_own, normed_other, normed_sib)
    out_sources = ((out_keep, out_got, out_sib), (cotangent, cotangent_other, cotangent_sib))
    gate_sources = (normed_all, (dgate, dgate_got, dgate_sib))
    rest_sources = (normed_all, (drest, drest_got, drest_sib))
    if chips == 8:
        out_pieces = eight_chip_pieces(meta, *out_sources, True)
        gate_pieces = eight_chip_pieces(meta, *gate_sources, False)
        rest_pieces = eight_chip_pieces(meta, *rest_sources, False)
        in_weight_grad = assemble(
            in_weight_body, whole(in_weight.shape, f32), (meta, *gate_pieces, *rest_pieces)
        )
        out_weight_grad = assemble(
            out_weight_body, whole(out_weight.shape, f32), (meta, *out_pieces)
        )
    else:

        def block_of(left, right, quarter_left):
            if quarter_left:
                left = (part_of(left[0], core, 2, 1), part_of(left[1], core, 2, 1), left[2])
            else:
                right = (right[0][core], right[1][core], right[2])
            return total_over_chips(
                rows_product(jnp.concatenate(left, axis=0), jnp.concatenate(right, axis=0))
            )

        out_total = block_of(*out_sources, True)
        gate_total = block_of(*gate_sources, False)
        rest_total = block_of(*rest_sources, False)
        rest_sib = swap_core(rest_total)
        out_weight_grad = join(core, out_total, swap_core(out_total), 0).astype(f32)
        in_weight_grad = jnp.concatenate(
            [
                join(core, gate_total, swap_core(gate_total), 1),
                join(core, rest_total[:, :half_channels], rest_sib[:, :half_channels], 1),
                rest_total[:, half_channels:],
            ],
            axis=1,
        ).astype(f32)

    branch_own, branch_send = call(
        branch_body,
        [whole((rows, width), f32), whole((rows, width), low)],
        (meta, out_keep, out_got, out_weight),
        4 * rows * width * half_inner,
    )
    branch_got = swap_owner(branch_send)
    block_out = (tokens.astype(f32) + branch_own + branch_got.astype(f32)).astype(low)

    dmeans_own, dmeans_send, norm_grad = call(
        input_grad_body,
        [
            whole((rows, width // 2), f32),
            whole((rows, width // 2), f32),
            whole((1, width // 2), f32),
        ],
        (meta, tokens, tokens_other, gain, in_weight, dgate, dgate_got, drest, drest_got),
        4 * rows * width * (rest_width + inner_width),
    )
    (grad_tokens,) = call(
        tokens_grad_body,
        [whole((rows, width), f32)],
        (meta, tokens, cotangent, dmeans_own, swap_owner(dmeans_send)),
        0,
    )

    total = lax.dynamic_index_in_dim(small, owner, 0, keepdims=False) + swap_owner(
        lax.dynamic_index_in_dim(small, 1 - owner, 0, keepdims=False)
    )
    total = jnp.concatenate([total[:7], row(norm_grad)], axis=0)
    bit = 1
    while bit < 2 * chips:
        total = total + swap(total, bit, 0)
        bit *= 2
    return (
        block_out,
        grad_tokens,
        total[7, : width // 2],
        in_weight_grad,
        total[0:4],
        total[4],
        total[6, 0:half_heads],
        total[6, LANES : LANES + half_heads],
        total[6, 2 * LANES : 2 * LANES + half_heads],
        total[5, :half_inner],
        out_weight_grad,
    )


def solution(mesh):
    placed = (
        P(("replica", "fsdp"), None),
        P(("replica", "fsdp"), None),
        P("fsdp"),
        P("fsdp", None),
        P(None, "fsdp"),
        P("fsdp"),
        P("fsdp"),
        P("fsdp"),
        P("fsdp"),
        P("fsdp"),
        P("fsdp", None),
        P(("replica", "fsdp"), None),
    )
    return jax.shard_map(
        per_device,
        mesh=mesh,
        in_specs=placed,
        out_specs=(
            P(("replica", "fsdp"), None),
            P(("replica", "fsdp"), None),
            P("fsdp"),
            P("fsdp", None),
            P(None, "fsdp"),
            P("fsdp"),
            P("fsdp"),
            P("fsdp"),
            P("fsdp"),
            P("fsdp"),
            P("fsdp", None),
        ),
        check_vma=False,
    )
```

```python
import jax
import jax.numpy as jnp
from jax import lax
from jax.experimental import pallas as pl
from jax.experimental.pallas import tpu as pltpu
from jax.sharding import PartitionSpec as P

EPSILON = 1e-05
AXES = ("replica", "fsdp")
LANES = 128
FAR = -1e30


def owner_place():
    return lax.axis_index("fsdp")


def core_place():
    return lax.rem(lax.axis_index("replica"), 2)


def chip_bit(bit):
    return lax.rem(lax.div(lax.axis_index("replica"), 2 << bit), 2)


def full_rows(mine_ref, peer_ref):
    first = owner_place() == 0
    mine, peer = mine_ref[...], peer_ref[...]
    return (jnp.where(first, mine, peer), jnp.where(first, peer, mine), mine + peer)


def row_marks(lens_ref, rows):
    end_one, end_two = lens_ref[0, 0], lens_ref[0, 0] + lens_ref[0, 1]
    position = lax.broadcasted_iota(jnp.int32, (rows, 1), 0)
    start = jnp.where(position >= end_two, end_two, jnp.where(position >= end_one, end_one, 0))
    return (position, start)


def kept_pairs(start, rows):
    key = lax.broadcasted_iota(jnp.int32, (rows, rows), 1)
    query = lax.broadcasted_iota(jnp.int32, (rows, rows), 0)
    return (key <= query) & (key >= start)


def channel_row(low, high, row, tile):
    half = low.shape[1] // LANES
    source = low if tile < half else high
    at = (tile if tile < half else tile - half) * LANES
    return source[row : row + 1, at : at + LANES]


def exact_dot(left, right):
    return jnp.dot(
        left, right, precision=lax.Precision.HIGHEST, preferred_element_type=jnp.float32
    )


def pair_operand(values, lane):
    zero = jnp.zeros_like(values)
    return jnp.concatenate(
        [jnp.where(lane < LANES // 2, values, zero), jnp.where(lane < LANES // 2, zero, values)],
        axis=0,
    )


def forward_body(lens_ref, own_ref, got_ref, mine_ref, peer_ref, xbc_ref, conv_ref, mixed_ref, rates_ref):
    rows, channels = conv_ref.shape
    tiles = channels // LANES
    pairs = tiles - 2
    heads = 2 * pairs
    taps = 4
    low, high, both = full_rows(mine_ref, peer_ref)
    position, start = row_marks(lens_ref, rows)
    usable = [position - (taps - 1 - k) >= start for k in range(taps)]
    lane = lax.broadcasted_iota(jnp.int32, (1, LANES), 1)
    bias = both[6:7, 0:heads]
    decay = both[6:7, LANES : LANES + heads]
    skip = both[6:7, 2 * LANES : 2 * LANES + heads]
    tail = slice(channels, channels + heads)
    rate = own_ref[:, tail] + got_ref[:, tail].astype(jnp.float32) + bias
    step = jnp.maximum(rate, 0.0) + jnp.log1p(jnp.exp(-jnp.abs(rate)))
    rate_sigmoid = jax.nn.sigmoid(rate)
    lower = jnp.where(
        lax.broadcasted_iota(jnp.int32, (rows, rows), 1)
        <= lax.broadcasted_iota(jnp.int32, (rows, rows), 0),
        1.0,
        0.0,
    ).astype(jnp.float32)
    cum = exact_dot(lower, step * -jnp.exp(decay))
    rates_ref[0] = step
    rates_ref[1] = cum
    rates_ref[2] = rate_sigmoid
    step_t, cum_t = step.T, cum.T
    mask = kept_pairs(start, rows)

    def active_tile(tile):
        at = tile * LANES
        xbc = own_ref[:, at : at + LANES] + got_ref[:, at : at + LANES].astype(jnp.float32)
        xbc_ref[:, at : at + LANES] = xbc
        conv = channel_row(low, high, 4, tile) + channel_row(low, high, taps - 1, tile) * xbc
        for k in range(taps - 1):
            shifted = pltpu.roll(xbc, taps - 1 - k, 0)
            conv = conv + channel_row(low, high, k, tile) * jnp.where(usable[k], shifted, 0.0)
        conv_ref[:, at : at + LANES] = conv
        return conv * jax.nn.sigmoid(conv)

    keys = active_tile(tiles - 2).astype(jnp.bfloat16)
    queries = active_tile(tiles - 1).astype(jnp.bfloat16)
    inner = lax.dot_general(
        queries, keys, (((1,), (1,)), ((), ())), preferred_element_type=jnp.float32
    )
    for pair in range(pairs):
        act = active_tile(pair)
        mixing = []
        for h in (2 * pair, 2 * pair + 1):
            spread = jnp.where(mask, cum[:, h : h + 1] - cum_t[h : h + 1, :], FAR)
            mixing.append((inner * jnp.exp(spread) * step_t[h : h + 1, :]).astype(jnp.bfloat16))
        scan = jnp.dot(
            jnp.concatenate(mixing, axis=1),
            pair_operand(act.astype(jnp.bfloat16), lane),
            preferred_element_type=jnp.float32,
        )
        gain = jnp.where(
            lane < LANES // 2, skip[:, 2 * pair : 2 * pair + 1], skip[:, 2 * pair + 1 : 2 * pair + 2]
        )
        mixed_ref[:, pair * LANES : (pair + 1) * LANES] = scan + gain * act


def gate_body(mixed_ref, own_ref, got_ref, q_own_ref, q_got_ref, mine_ref, peer_ref, keep_ref, send_ref, dkeep_ref, dsend_ref, dmixed_ref, gain_grad_ref, out_ref, dgate_ref):
    rows, inner_width = mixed_ref.shape
    half = inner_width // 2
    owner, core = owner_place(), core_place()
    first = owner == 0
    low, high, _ = full_rows(mine_ref, peer_ref)
    width = 2 * LANES
    tiles = inner_width // width

    def cut(tile):
        return slice(tile * width, (tile + 1) * width)

    def gate_of(tile):
        gate = own_ref[:, cut(tile)] + got_ref[:, cut(tile)].astype(jnp.float32)
        return (gate, jax.nn.sigmoid(gate))

    def half_cut(tile):
        at = tile * width % half
        return slice(at, at + width)

    def gain_of(tile):
        return (low if tile * width < half else high)[5:6, half_cut(tile)]

    def q_of(tile):
        own = q_own_ref[:, half_cut(tile)]
        got = q_got_ref[:, half_cut(tile)].astype(jnp.float32)
        return jnp.where(first == (tile * width < half), own, got)

    squares = jnp.zeros((rows, 1), jnp.float32)
    cross = jnp.zeros((rows, 1), jnp.float32)
    for tile in range(tiles):
        gate, sigmoid = gate_of(tile)
        gated = mixed_ref[:, cut(tile)] * (gate * sigmoid)
        squares = squares + jnp.sum(gated * gated, axis=1, keepdims=True)
        cross = cross + jnp.sum(q_of(tile) * gain_of(tile) * gated, axis=1, keepdims=True)
    inverse = lax.rsqrt(squares / inner_width + EPSILON)
    mean_cross = cross * inverse / inner_width
    for tile in range(tiles):
        gate, sigmoid = gate_of(tile)
        silu = gate * sigmoid
        mixed = mixed_ref[:, cut(tile)]
        normed = mixed * silu * inverse
        gain = gain_of(tile)
        out = (normed * gain).astype(jnp.bfloat16)
        out_ref[tile * width // half, :, half_cut(tile)] = out
        q = q_of(tile)
        gain_grad_ref[:, cut(tile)] = jnp.sum(q * normed, axis=0, keepdims=True)
        dgated = inverse * (q * gain - normed * mean_cross)
        dmixed_ref[:, cut(tile)] = dgated * silu
        dgate_ref[tile * width // half, :, half_cut(tile)] = (
            dgated * mixed * (sigmoid * (1.0 + gate * (1.0 - sigmoid)))
        ).astype(jnp.bfloat16)
    keep_ref[...] = out_ref[owner]
    send_ref[...] = out_ref[1 - owner]
    dkeep_ref[...] = dgate_ref[core]
    dsend_ref[...] = dgate_ref[1 - core]


def backward_body(lens_ref, dmixed_ref, xbc_ref, conv_ref, rates_ref, mine_ref, peer_ref, gain_grad_ref, keep_ref, send_ref, small_keep_ref, small_send_ref, rest_ref, small_ref):
    rows, channels = conv_ref.shape
    tiles = channels // LANES
    pairs = tiles - 2
    heads = 2 * pairs
    taps = 4
    half_tiles = tiles // 2
    small_ref[...] = jnp.zeros(small_ref.shape, jnp.float32)
    low, high, both = full_rows(mine_ref, peer_ref)
    position, start = row_marks(lens_ref, rows)
    usable = [position - (taps - 1 - k) >= start for k in range(taps)]
    lane = lax.broadcasted_iota(jnp.int32, (1, LANES), 1)
    decay = both[6:7, LANES : LANES + heads]
    skip = both[6:7, 2 * LANES : 2 * LANES + heads]
    step, cum, rate_sigmoid = rates_ref[0], rates_ref[1], rates_ref[2]
    step_t, cum_t = step.T, cum.T
    mask = kept_pairs(start, rows)

    def cut(tile):
        return slice(tile * LANES, (tile + 1) * LANES)

    def act_of(tile):
        conv = conv_ref[:, cut(tile)]
        sigmoid = jax.nn.sigmoid(conv)
        return (conv * sigmoid, sigmoid * (1.0 + conv * (1.0 - sigmoid)))

    def finish_tile(tile, dconv):
        owner, at = tile // half_tiles, tile % half_tiles * LANES
        xbc = xbc_ref[:, cut(tile)]
        small_ref[owner, 4:5, at : at + LANES] = jnp.sum(dconv, axis=0, keepdims=True)
        small_ref[owner, taps - 1 : taps, at : at + LANES] = jnp.sum(
            dconv * xbc, axis=0, keepdims=True
        )
        total = channel_row(low, high, taps - 1, tile) * dconv
        for k in range(taps - 1):
            behind = taps - 1 - k
            kept = jnp.where(usable[k], dconv, 0.0)
            small_ref[owner, k : k + 1, at : at + LANES] = jnp.sum(
                kept * pltpu.roll(xbc, behind, 0), axis=0, keepdims=True
            )
            total = total + channel_row(low, high, k, tile) * pltpu.roll(kept, rows - behind, 0)
        rest_ref[owner, :, at : at + LANES] = total.astype(jnp.bfloat16)

    keys_act, keys_slope = act_of(tiles - 2)
    queries_act, queries_slope = act_of(tiles - 1)
    keys, queries = keys_act.astype(jnp.bfloat16), queries_act.astype(jnp.bfloat16)
    inner = lax.dot_general(
        queries, keys, (((1,), (1,)), ((), ())), preferred_element_type=jnp.float32
    )
    dinner = jnp.zeros((rows, rows), jnp.float32)
    dstep_rows = []
    dcum = jnp.zeros((rows, heads), jnp.float32)
    skip_grad = jnp.zeros((1, heads), jnp.float32)
    head_lane = lax.broadcasted_iota(jnp.int32, (1, heads), 1)
    for pair in range(pairs):
        act, slope = act_of(pair)
        dmixed = dmixed_ref[:, cut(pair)]
        dscan = dmixed.astype(jnp.bfloat16)
        operand = pair_operand(act.astype(jnp.bfloat16), lane)
        dmixing = lax.dot_general(
            dscan, operand, (((1,), (1,)), ((), ())), preferred_element_type=jnp.float32
        )
        direct = jnp.sum(dmixed * act, axis=0, keepdims=True)
        mixing = []
        for j in range(2):
            h = 2 * pair + j
            spread = jnp.where(mask, cum[:, h : h + 1] - cum_t[h : h + 1, :], FAR)
            decays = jnp.exp(spread)
            step_row = step_t[h : h + 1, :]
            weight = inner * decays
            mixing.append((weight * step_row).astype(jnp.bfloat16))
            grad = dmixing[:, j * rows : (j + 1) * rows]
            dinner = dinner + grad * decays * step_row
            term = grad * weight
            dstep_rows.append(jnp.sum(term, axis=0, keepdims=True))
            dcum = dcum + jnp.where(
                head_lane == h, jnp.sum(term * step_row, axis=1, keepdims=True), 0.0
            )
            in_head = (lane < LANES // 2) if j == 0 else (lane >= LANES // 2)
            skip_grad = skip_grad + jnp.where(
                head_lane == h,
                jnp.sum(jnp.where(in_head, direct, 0.0), axis=1, keepdims=True),
                0.0,
            )
        dinput = lax.dot_general(
            jnp.concatenate(mixing, axis=1),
            dscan,
            (((0,), (0,)), ((), ())),
            preferred_element_type=jnp.float32,
        )
        gain = jnp.where(
            lane < LANES // 2, skip[:, 2 * pair : 2 * pair + 1], skip[:, 2 * pair + 1 : 2 * pair + 2]
        )
        dact = jnp.where(lane < LANES // 2, dinput[:rows], dinput[rows:]) + gain * dmixed
        finish_tile(pair, dact * slope)
    dinner_low = dinner.astype(jnp.bfloat16)
    dqueries = jnp.dot(dinner_low, keys, preferred_element_type=jnp.float32)
    dkeys = lax.dot_general(
        dinner_low, queries, (((0,), (0,)), ((), ())), preferred_element_type=jnp.float32
    )
    finish_tile(tiles - 2, dkeys * keys_slope)
    finish_tile(tiles - 1, dqueries * queries_slope)
    dstep_t = jnp.concatenate(dstep_rows, axis=0)
    dstep = dstep_t.T
    dcum = dcum - step * dstep
    upper = jnp.where(
        lax.broadcasted_iota(jnp.int32, (rows, rows), 1)
        >= lax.broadcasted_iota(jnp.int32, (rows, rows), 0),
        1.0,
        0.0,
    ).astype(jnp.float32)
    drate = exact_dot(upper, dcum)
    speed = jnp.exp(decay)
    draw = (dstep - drate * speed) * rate_sigmoid
    tail = jnp.concatenate([draw, jnp.zeros((rows, LANES - heads), jnp.float32)], axis=1)
    for side in range(2):
        rest_ref[side, :, channels // 2 :] = tail.astype(jnp.bfloat16)
    bias_grad = jnp.sum(draw, axis=0, keepdims=True)
    decay_grad = jnp.sum(-drate * step * speed, axis=0, keepdims=True)
    half_inner = pairs * LANES // 2
    half_heads = heads // 2
    for owner in range(2):
        small_ref[owner, 5:6, 0:half_inner] = gain_grad_ref[
            :, owner * half_inner : (owner + 1) * half_inner
        ]
        for place, item in enumerate((bias_grad, decay_grad, skip_grad)):
            at = place * LANES
            small_ref[owner, 6:7, at : at + half_heads] = item[
                :, owner * half_heads : (owner + 1) * half_heads
            ]
    core, place = core_place(), owner_place()
    keep_ref[...] = rest_ref[core]
    send_ref[...] = rest_ref[1 - core]
    small_keep_ref[...] = small_ref[place]
    small_send_ref[...] = small_ref[1 - place]


def whole(shape, dtype):
    return jax.ShapeDtypeStruct(shape, dtype)


def call(body, out_shape, operands, work, scratch=(), lens=None):
    moved = sum(item.size * item.dtype.itemsize for item in (*operands, *out_shape))
    vmem = pl.BlockSpec(memory_space=pltpu.VMEM)
    in_specs = [vmem for _ in operands]
    if lens is not None:
        operands = (lens, *operands)
        in_specs = [pl.BlockSpec(memory_space=pltpu.SMEM), *in_specs]
    return pl.pallas_call(
        body,
        out_shape=out_shape,
        in_specs=in_specs,
        out_specs=[vmem for _ in out_shape],
        scratch_shapes=[pltpu.VMEM(item.shape, item.dtype) for item in scratch],
        compiler_params=pltpu.CompilerParams(vmem_limit_bytes=40 << 20),
        cost_estimate=pl.CostEstimate(flops=work, bytes_accessed=moved, transcendentals=0),
    )(*operands)


def unit_rows(tokens):
    values = tokens.astype(jnp.float32)
    return lax.rsqrt(jnp.mean(values * values, axis=-1, keepdims=True) + EPSILON)


def lanes_product(left, right):
    return lax.dot_general(
        left, right, (((1,), (1,)), ((), ())), preferred_element_type=jnp.float32
    )


def rows_product(left, right):
    return lax.dot_general(
        left, right, (((0,), (0,)), ((), ())), preferred_element_type=jnp.float32
    )


def lane_half(size):
    return pl.ds(pl.multiple_of(owner_place() * size, LANES), size)


def half_means(tokens_ref, size):
    return tokens_ref[:, lane_half(size)].astype(jnp.float32) * unit_rows(tokens_ref[...])


def norm_body(first_ref, second_ref, gain_ref, out_first_ref, out_second_ref):
    for tokens_ref, out_ref in ((first_ref, out_first_ref), (second_ref, out_second_ref)):
        means = half_means(tokens_ref, out_ref.shape[1])
        out_ref[...] = (means * gain_ref[...]).astype(jnp.bfloat16)


def project_body(tokens_ref, gain_ref, weight_ref, normed_ref, rest_ref, gate_ref):
    inner_width = gate_ref.shape[1]
    rest_width = weight_ref.shape[0] - inner_width
    normed = (half_means(tokens_ref, normed_ref.shape[1]) * gain_ref[...]).astype(jnp.bfloat16)
    normed_ref[...] = normed
    whole_tiles = rest_width // LANES * LANES
    rest_ref[:, :whole_tiles] = lanes_product(
        normed, weight_ref[inner_width : inner_width + whole_tiles, :]
    ).astype(rest_ref.dtype)
    tail = lanes_product(normed, weight_ref[inner_width + whole_tiles :, :])
    blank = jnp.zeros((tail.shape[0], LANES - tail.shape[1]), jnp.float32)
    rest_ref[:, whole_tiles:] = jnp.concatenate([tail, blank], axis=1).astype(rest_ref.dtype)
    gate_ref[...] = lanes_product(normed, weight_ref[:inner_width, :]).astype(gate_ref.dtype)


def cotangent_body(own_ref, other_ref, weight_ref, q_own_ref, q_send_ref):
    q_send_ref[...] = lanes_product(other_ref[...], weight_ref[...]).astype(q_send_ref.dtype)
    q_own_ref[...] = lanes_product(own_ref[...], weight_ref[...])


def branch_body(keep_ref, got_ref, weight_ref, own_ref, send_ref):
    send_ref[...] = jnp.dot(
        got_ref[...], weight_ref[...], preferred_element_type=jnp.float32
    ).astype(send_ref.dtype)
    own_ref[...] = jnp.dot(keep_ref[...], weight_ref[...], preferred_element_type=jnp.float32)


def input_grad_body(*refs):
    tokens, gates, rests = refs[0:4], refs[4:8], refs[8:12]
    gain_ref, weight_ref = refs[12:14]
    outs, gain_grad_ref = refs[14:18], refs[18]
    core = core_place()
    half_inner = gates[0].shape[1]
    half_channels = rests[0].shape[1] - LANES
    tail = weight_ref.shape[0] - 2 * (half_inner + half_channels)
    gate_rows = pl.ds(pl.multiple_of(core * half_inner, LANES), half_inner)
    rest_rows = pl.ds(
        pl.multiple_of(2 * half_inner + core * half_channels, LANES), half_channels
    )
    gate_weight = weight_ref[gate_rows, :]
    rest_weight = weight_ref[rest_rows, :]
    tail_weight = weight_ref[2 * (half_inner + half_channels) :, :]
    gain = gain_ref[...]
    gain_grad = jnp.zeros_like(gain)
    for tokens_ref, gate_ref, rest_ref, out_ref in zip(tokens, gates, rests, outs):
        dnormed = jnp.dot(gate_ref[...], gate_weight, preferred_element_type=jnp.float32)
        dnormed = dnormed + jnp.dot(
            rest_ref[:, :half_channels], rest_weight, preferred_element_type=jnp.float32
        )
        dtail = jnp.dot(
            rest_ref[:, half_channels : half_channels + tail],
            tail_weight,
            preferred_element_type=jnp.float32,
        )
        dnormed = dnormed + jnp.where(core == 0, dtail, 0.0)
        means = half_means(tokens_ref, gain.shape[1])
        gain_grad = gain_grad + jnp.sum(dnormed * means, axis=0, keepdims=True)
        out_ref[...] = (dnormed * gain).astype(out_ref.dtype)
    gain_grad_ref[...] = gain_grad


def tokens_grad_body(tokens_ref, cotangent_ref, own_ref, sib_ref, far_ref, far_sib_ref, out_ref):
    half = own_ref.shape[1]
    first = owner_place() == 0
    inverse = unit_rows(tokens_ref[...])
    own = own_ref[...] + sib_ref[...].astype(jnp.float32)
    far = far_ref[...].astype(jnp.float32) + far_sib_ref[...].astype(jnp.float32)
    parts = []
    cross = jnp.zeros_like(inverse)
    for side in range(2):
        cut = slice(side * half, (side + 1) * half)
        dmeans = jnp.where(first == (side == 0), own, far)
        means = tokens_ref[:, cut].astype(jnp.float32) * inverse
        cross = cross + jnp.sum(dmeans * means, axis=1, keepdims=True)
        parts.append((cut, dmeans, means))
    for cut, dmeans, means in parts:
        out_ref[:, cut] = cotangent_ref[:, cut].astype(jnp.float32) + inverse * (
            dmeans - means * (cross / (2 * half))
        )


def block_grad_body(parts, right_half, *refs):
    lefts, rights, outs = refs[0:4], refs[4:8], refs[8:]
    width = outs[0].shape[1]
    lanes = slice(None)
    if right_half:
        lanes = pl.ds(pl.multiple_of(core_place() * width, LANES), width)
    right = jnp.concatenate([ref[:, lanes] for ref in rights], axis=0)
    for place, (at, size, order) in enumerate(parts):
        bit = chip_bit(order[0])
        half = size // 2
        for ref, side in ((outs[2 * place], 1 - bit), (outs[2 * place + 1], bit)):
            cut = pl.ds(pl.multiple_of(at + side * half, LANES), half)
            left = jnp.concatenate([left_ref[:, cut] for left_ref in lefts], axis=0)
            ref[...] = rows_product(left, right).astype(ref.dtype)


def sum_step_body(parts, step, *refs):
    count = len(parts)
    kept, got, outs = refs[0:count], refs[count : 2 * count], refs[2 * count :]
    for place, (_, _, order) in enumerate(parts):
        if step == len(order):
            outs[place][...] = (
                kept[place][...] + got[place][...].astype(jnp.float32)
            ).astype(outs[place].dtype)
            continue
        rows = kept[place].shape[0] // 2
        bit = chip_bit(order[step])
        for ref, side in ((outs[2 * place], 1 - bit), (outs[2 * place + 1], bit)):
            cut = pl.ds(pl.multiple_of(side * rows, 16), rows)
            ref[...] = (kept[place][cut, :] + got[place][cut, :].astype(jnp.float32)).astype(
                ref.dtype
            )


def stream_pieces(parts, lefts, rights, width, right_half):
    f32, low = jnp.float32, jnp.bfloat16

    def sizes(step):
        return [
            whole((size >> step, width), dtype) for _, size, _ in parts for dtype in (low, f32)
        ]

    def block(*refs):
        block_grad_body(parts, right_half, *refs)

    now = call(
        block, sizes(1), (*lefts, *rights), 1024 * width * sum(size for _, size, _ in parts)
    )
    depth = len(parts[0][2])
    for step in range(1, depth + 1):
        got = [swap_chip(now[2 * p], order[step - 1]) for p, (_, _, order) in enumerate(parts)]

        def add(*refs, step=step):
            sum_step_body(parts, step, *refs)

        last = [whole((size >> depth, width), low) for _, size, _ in parts]
        now = call(add, sizes(step + 1) if step < depth else last, (*now[1::2], *got), 0)
    out = []
    for chunk, (_, _, order) in zip(now, parts):
        for bit in reversed(order[1:]):
            chunk = jnp.concatenate([chunk, swap_chip(chunk, bit)], axis=0)
        got = swap_chip(chunk, order[0])
        out += [chunk, got, swap_core(chunk), swap_core(got)]
    return out


def write_part(out_ref, base, part, pieces, other, limit=None, tail_at=None):
    at, size, order = part
    half, size = size // 2, size >> 3
    first, second, third = (chip_bit(bit) for bit in order)
    for which in range(2):
        side = first if which == 0 else 1 - first
        mine, sibling = pieces[which], pieces[2 + which]
        for p in range(4):
            middle = second if p < 2 else 1 - second
            last = third if p % 2 == 0 else 1 - third
            rows = slice(p * size, (p + 1) * size)
            value = jnp.where(other, sibling[rows, :], mine[rows, :]).astype(jnp.float32)
            place = at + side * half + (2 * middle + last) * size

            def store():
                out_ref[pl.ds(pl.multiple_of(base + place, 8), size), :] = value

            def store_tail():
                out_ref[tail_at:, :] = value[: out_ref.shape[0] - tail_at]

            if limit is None or at + 2 * half <= limit:
                store()
            else:
                pl.when(place < limit)(store)
            if tail_at is not None and at <= limit < at + 2 * half:
                pl.when(place == limit)(store_tail)


def in_weight_body(gate_parts, rest_parts, *refs):
    out_ref = refs[-1]
    gates, rests = refs[: 4 * len(gate_parts)], refs[4 * len(gate_parts) : -1]
    core = core_place()
    half_inner = sum(size for _, size, _ in gate_parts)
    half_channels = sum(size for _, size, _ in rest_parts) - LANES
    for side in range(2):
        other = core != side
        for place, part in enumerate(gate_parts):
            write_part(out_ref, side * half_inner, part, gates[4 * place : 4 * place + 4], other)
        for place, part in enumerate(rest_parts):
            write_part(
                out_ref,
                2 * half_inner + side * half_channels,
                part,
                rests[4 * place : 4 * place + 4],
                other,
                half_channels,
                2 * (half_inner + half_channels) if side == 0 else None,
            )


def out_weight_body(parts, blocks, *refs):
    side = lax.div(pl.program_id(0), blocks)
    other = core_place() != side
    for place, part in enumerate(parts):
        write_part(refs[-1], 0, part, refs[4 * place : 4 * place + 4], other)


def assemble(body, out, pieces, block):
    blocks = pieces[0].shape[1] // block
    return pl.pallas_call(
        body,
        grid=(out.shape[1] // block,),
        out_shape=out,
        in_specs=[
            pl.BlockSpec((item.shape[0], block), lambda i: (0, lax.rem(i, blocks)))
            for item in pieces
        ],
        out_specs=pl.BlockSpec((out.shape[0], block), lambda i: (0, i)),
        compiler_params=pltpu.CompilerParams(vmem_limit_bytes=48 << 20),
        cost_estimate=pl.CostEstimate(
            flops=out.size, bytes_accessed=out.size * 6, transcendentals=0
        ),
    )(*pieces)


def swap(value, replica_bits, fsdp_bits):
    replicas, owners = lax.axis_size("replica"), lax.axis_size("fsdp")
    pairs = [
        (r * owners + f, (r ^ replica_bits) * owners + (f ^ fsdp_bits))
        for r in range(replicas)
        for f in range(owners)
    ]
    return lax.ppermute(value, AXES, pairs)


def swap_owner(value):
    return swap(value, 0, 1)


def swap_core(value):
    return swap(value, 1, 0)


def swap_chip(value, bit):
    return swap(value, 2 << bit, 0)


def join(place, own, other, axis):
    return jnp.where(
        place == 0,
        jnp.concatenate([own, other], axis=axis),
        jnp.concatenate([other, own], axis=axis),
    )


def part_of(value, place, parts, axis):
    size = value.shape[axis] // parts
    return lax.dynamic_slice_in_dim(value, place * size, size, axis)


def total_over_chips(block):
    chip = lax.axis_index("replica") // 2
    bits = range((lax.axis_size("replica") // 2).bit_length() - 1)
    rows, cols = block.shape
    kept = block.reshape((2,) * len(bits) + (rows >> len(bits), cols))
    for bit in bits:
        mine = (chip >> bit) & 1
        sent = lax.dynamic_index_in_dim(kept, 1 - mine, 0, keepdims=False).astype(jnp.bfloat16)
        got = swap_chip(sent, bit)
        kept = lax.dynamic_index_in_dim(kept, mine, 0, keepdims=False) + got.astype(jnp.float32)
    chunk = kept.astype(jnp.bfloat16)
    for bit in reversed(bits):
        chunk = join((chip >> bit) & 1, chunk, swap_chip(chunk, bit), 0)
    return chunk


def per_device(
    tokens,
    seq_lens,
    norm_gain,
    in_weight,
    conv_weight,
    conv_bias,
    step_bias,
    decay_log,
    skip_gain,
    out_gain,
    out_weight,
    cotangent,
):
    f32, low = jnp.float32, jnp.bfloat16
    owner = lax.axis_index("fsdp")
    core = lax.axis_index("replica") % 2
    chips = lax.axis_size("replica") // 2
    rows, width = tokens.shape
    half_width = width // 2
    half_inner = out_weight.shape[0]
    inner_width = 2 * half_inner
    half_channels = conv_bias.shape[0]
    channels = 2 * half_channels
    half_heads = skip_gain.shape[0]
    heads = 2 * half_heads
    weight = in_weight.T
    gain = norm_gain.astype(f32).reshape(1, -1)

    def row(item):
        item = item.astype(f32).reshape(-1, item.shape[-1])
        return jnp.pad(item, ((0, 0), (0, half_channels - item.shape[-1])))

    def head_row(item):
        item = item.astype(f32)
        there = jnp.zeros_like(item)
        placed = jnp.where(
            owner == 0, jnp.concatenate([item, there]), jnp.concatenate([there, item])
        )
        return jnp.pad(placed, (0, LANES - heads))

    head_rows = jnp.concatenate([head_row(step_bias), head_row(decay_log), head_row(skip_gain)])
    mine = jnp.concatenate(
        [
            row(conv_weight),
            row(conv_bias),
            row(out_gain),
            row(head_rows),
            jnp.zeros((1, half_channels), f32),
        ],
        axis=0,
    )

    def project(source, dtype):
        return call(
            project_body,
            [
                whole((rows, half_width), low),
                whole((rows, channels + LANES), dtype),
                whole((rows, inner_width), dtype),
            ],
            (source, gain, weight),
            2 * rows * half_width * weight.shape[0],
        )

    tokens_far = swap_owner(tokens)
    peer = swap_owner(mine)
    held, _ = lax.optimization_barrier((cotangent, tokens_far))
    cotangent_far = swap_owner(held)
    normed_own, rest_own, gate_own = project(tokens, f32)
    normed_far, rest_send, gate_send = project(tokens_far, low)
    rest_got = swap_owner(rest_send)
    q_own, q_send = call(
        cotangent_body,
        [whole((rows, half_inner), f32), whole((rows, half_inner), low)],
        (cotangent, cotangent_far, out_weight),
        4 * rows * width * half_inner,
    )
    q_got = swap_owner(q_send)
    held, _ = lax.optimization_barrier((gate_send, rest_got))
    gate_got = swap_owner(held)
    tokens_sib, tokens_far_sib = swap_core(tokens), swap_core(tokens_far)
    cotangent_sib, cotangent_far_sib = swap_core(cotangent), swap_core(cotangent_far)
    normed_sib, normed_far_sib = call(
        norm_body,
        [whole((rows, half_width), low)] * 2,
        (tokens_sib, tokens_far_sib, gain),
        0,
    )

    xbc, conv, mixed, rates = call(
        forward_body,
        [
            whole((rows, channels), f32),
            whole((rows, channels), f32),
            whole((rows, inner_width), f32),
            whole((3, rows, heads), f32),
        ],
        (rest_own, rest_got, mine, peer),
        10**9,
        lens=seq_lens,
    )
    out_keep, out_send, dgate, dgate_send, dmixed, gain_grad = call(
        gate_body,
        [
            *[whole((rows, half_inner), low)] * 4,
            whole((rows, inner_width), f32),
            whole((1, inner_width), f32),
        ],
        (mixed, gate_own, gate_got, q_own, q_got, mine, peer),
        10**9,
        scratch=[whole((2, rows, half_inner), low)] * 2,
    )
    out_far = swap_owner(out_send)
    dgate_far, dgate_far_sib = swap_owner(dgate), swap(dgate_send, 1, 1)
    out_sib, dgate_sib = swap_core(out_keep), swap_core(dgate_send)
    out_far_sib = swap_core(out_far)
    drest, drest_send, small_keep, small_send = call(
        backward_body,
        [
            *[whole((rows, half_channels + LANES), low)] * 2,
            *[whole((8, half_channels), f32)] * 2,
        ],
        (dmixed, xbc, conv, rates, mine, peer, gain_grad),
        10**9,
        scratch=[
            whole((2, rows, half_channels + LANES), low),
            whole((2, 8, half_channels), f32),
        ],
        lens=seq_lens,
    )
    drest_far, drest_far_sib = swap_owner(drest), swap(drest_send, 1, 1)
    drest_sib = swap_core(drest_send)

    tokens_all = (tokens, tokens_far, tokens_sib, tokens_far_sib)
    normed_all = (normed_own, normed_far, normed_sib, normed_far_sib)
    cotangent_all = (cotangent, cotangent_far, cotangent_sib, cotangent_far_sib)
    out_all = (out_keep, out_far, out_sib, out_far_sib)
    dgate_all = (dgate, dgate_far, dgate_sib, dgate_far_sib)
    drest_all = (drest, drest_far, drest_sib, drest_far_sib)
    if chips == 8:
        out_parts = ((0, half_inner, (0, 1, 2)),)
        gate_parts = ((0, half_inner, (1, 0, 2)),)
        cut = (half_channels + LANES) * 3 // 5 // LANES * LANES
        rest_parts = ((0, cut, (0, 1, 2)), (cut, half_channels + LANES - cut, (1, 0, 2)))
        out_pieces = stream_pieces(out_parts, out_all, cotangent_all, half_width, True)
        gate_pieces = stream_pieces(gate_parts, dgate_all, normed_all, half_width, False)
        rest_pieces = stream_pieces(rest_parts, drest_all, normed_all, half_width, False)

        def in_weight_rows(*refs):
            in_weight_body(gate_parts, rest_parts, *refs)

        def out_weight_lanes(*refs):
            out_weight_body(out_parts, 2, *refs)

        in_weight_grad = assemble(
            in_weight_rows, whole(weight.shape, f32), [*gate_pieces, *rest_pieces], LANES
        ).T
        out_weight_grad = assemble(
            out_weight_lanes, whole(out_weight.shape, f32), out_pieces, half_width // 2
        )
    else:

        def total_of(left, right):
            return total_over_chips(
                rows_product(jnp.concatenate(left, axis=0), jnp.concatenate(right, axis=0))
            )

        out_total = total_of(
            out_all, [part_of(item, core, 2, 1) for item in cotangent_all]
        )
        gate_total = total_of(dgate_all, normed_all)
        rest_total = total_of(drest_all, normed_all)
        rest_sib = swap_core(rest_total)
        out_weight_grad = join(core, out_total, swap_core(out_total), 1).astype(f32)
        in_weight_grad = (
            jnp.concatenate(
                [
                    join(core, gate_total, swap_core(gate_total), 0),
                    join(core, rest_total[:half_channels], rest_sib[:half_channels], 0),
                    rest_total[half_channels : half_channels + heads],
                ],
                axis=0,
            )
            .astype(f32)
            .T
        )

    branch_own, branch_send = call(
        branch_body,
        [whole((rows, width), f32), whole((rows, width), low)],
        (out_keep, out_far, out_weight),
        4 * rows * width * half_inner,
    )
    branch_far = swap_owner(branch_send)
    block_out = (tokens.astype(f32) + branch_own + branch_far.astype(f32)).astype(low)

    own, far_send, sib_send, far_sib_send, norm_grad = call(
        input_grad_body,
        [
            whole((rows, half_width), f32),
            *[whole((rows, half_width), low)] * 3,
            whole((1, half_width), f32),
        ],
        (*tokens_all, *dgate_all, *drest_all, gain, weight),
        4 * rows * width * weight.shape[0],
    )
    (grad_tokens,) = call(
        tokens_grad_body,
        [whole((rows, width), f32)],
        (
            tokens,
            cotangent,
            own,
            swap_core(sib_send),
            swap_owner(far_send),
            swap(far_sib_send, 1, 1),
        ),
        0,
    )

    total = small_keep + swap_owner(small_send)
    total = jnp.concatenate([total[:7], row(norm_grad)], axis=0)
    bit = 1
    while bit < 2 * chips:
        total = total + swap(total, bit, 0)
        bit *= 2
    return (
        block_out,
        grad_tokens,
        total[7, :half_width],
        in_weight_grad,
        total[0:4],
        total[4],
        total[6, 0:half_heads],
        total[6, LANES : LANES + half_heads],
        total[6, 2 * LANES : 2 * LANES + half_heads],
        total[5, :half_inner],
        out_weight_grad,
    )


def solution(mesh):
    placed = (
        P(("replica", "fsdp"), None),
        P(("replica", "fsdp"), None),
        P("fsdp"),
        P("fsdp", None),
        P(None, "fsdp"),
        P("fsdp"),
        P("fsdp"),
        P("fsdp"),
        P("fsdp"),
        P("fsdp"),
        P("fsdp", None),
        P(("replica", "fsdp"), None),
    )
    return jax.shard_map(
        per_device,
        mesh=mesh,
        in_specs=placed,
        out_specs=(
            P(("replica", "fsdp"), None),
            P(("replica", "fsdp"), None),
            P("fsdp"),
            P("fsdp", None),
            P(None, "fsdp"),
            P("fsdp"),
            P("fsdp"),
            P("fsdp"),
            P("fsdp"),
            P("fsdp"),
            P("fsdp", None),
        ),
        check_vma=False,
    )
```

```python
import jax
import jax.numpy as jnp
from jax import lax
from jax.experimental import pallas as pl
from jax.experimental.pallas import tpu as pltpu
from jax.sharding import PartitionSpec as P

EPSILON = 1e-05
AXES = ("replica", "fsdp")
LANES = 128
FAR = -1e30
ORDER = "012n3x0123k0123tb0123p012301os23"


def owner_place():
    return lax.axis_index("fsdp")


def core_place():
    return lax.rem(lax.axis_index("replica"), 2)


def chip_bit(bit):
    return lax.rem(lax.div(lax.axis_index("replica"), 2 << bit), 2)


def full_rows(mine_ref, peer_ref):
    first = owner_place() == 0
    mine, peer = mine_ref[...], peer_ref[...]
    return (jnp.where(first, mine, peer), jnp.where(first, peer, mine), mine + peer)


def row_marks(lens_ref, rows):
    end_one, end_two = lens_ref[0, 0], lens_ref[0, 0] + lens_ref[0, 1]
    position = lax.broadcasted_iota(jnp.int32, (rows, 1), 0)
    start = jnp.where(position >= end_two, end_two, jnp.where(position >= end_one, end_one, 0))
    return (position, start)


def kept_pairs(start, rows):
    key = lax.broadcasted_iota(jnp.int32, (rows, rows), 1)
    query = lax.broadcasted_iota(jnp.int32, (rows, rows), 0)
    return (key <= query) & (key >= start)


def channel_row(low, high, row, tile):
    half = low.shape[1] // LANES
    source = low if tile < half else high
    at = (tile if tile < half else tile - half) * LANES
    return source[row : row + 1, at : at + LANES]


def exact_dot(left, right):
    return jnp.dot(
        left, right, precision=lax.Precision.HIGHEST, preferred_element_type=jnp.float32
    )


def pair_operand(values, lane):
    zero = jnp.zeros_like(values)
    return jnp.concatenate(
        [jnp.where(lane < LANES // 2, values, zero), jnp.where(lane < LANES // 2, zero, values)],
        axis=0,
    )


def forward_body(lens_ref, own_ref, got_ref, mine_ref, peer_ref, xbc_ref, conv_ref, mixed_ref, rates_ref):
    rows, channels = conv_ref.shape
    tiles = channels // LANES
    pairs = tiles - 2
    heads = 2 * pairs
    taps = 4
    low, high, both = full_rows(mine_ref, peer_ref)
    position, start = row_marks(lens_ref, rows)
    usable = [position - (taps - 1 - k) >= start for k in range(taps)]
    lane = lax.broadcasted_iota(jnp.int32, (1, LANES), 1)
    bias = both[6:7, 0:heads]
    decay = both[6:7, LANES : LANES + heads]
    skip = both[6:7, 2 * LANES : 2 * LANES + heads]
    tail = slice(channels, channels + heads)
    rate = own_ref[:, tail] + got_ref[:, tail].astype(jnp.float32) + bias
    step = jnp.maximum(rate, 0.0) + jnp.log1p(jnp.exp(-jnp.abs(rate)))
    rate_sigmoid = jax.nn.sigmoid(rate)
    lower = jnp.where(
        lax.broadcasted_iota(jnp.int32, (rows, rows), 1)
        <= lax.broadcasted_iota(jnp.int32, (rows, rows), 0),
        1.0,
        0.0,
    ).astype(jnp.float32)
    cum = exact_dot(lower, step * -jnp.exp(decay))
    rates_ref[0] = step
    rates_ref[1] = cum
    rates_ref[2] = rate_sigmoid
    step_t, cum_t = step.T, cum.T
    mask = kept_pairs(start, rows)

    def active_tile(tile):
        at = tile * LANES
        xbc = own_ref[:, at : at + LANES] + got_ref[:, at : at + LANES].astype(jnp.float32)
        xbc_ref[:, at : at + LANES] = xbc
        conv = channel_row(low, high, 4, tile) + channel_row(low, high, taps - 1, tile) * xbc
        for k in range(taps - 1):
            shifted = pltpu.roll(xbc, taps - 1 - k, 0)
            conv = conv + channel_row(low, high, k, tile) * jnp.where(usable[k], shifted, 0.0)
        conv_ref[:, at : at + LANES] = conv
        return conv * jax.nn.sigmoid(conv)

    keys = active_tile(tiles - 2).astype(jnp.bfloat16)
    queries = active_tile(tiles - 1).astype(jnp.bfloat16)
    inner = lax.dot_general(
        queries, keys, (((1,), (1,)), ((), ())), preferred_element_type=jnp.float32
    )
    for pair in range(pairs):
        act = active_tile(pair)
        mixing = []
        for h in (2 * pair, 2 * pair + 1):
            spread = jnp.where(mask, cum[:, h : h + 1] - cum_t[h : h + 1, :], FAR)
            mixing.append((inner * jnp.exp(spread) * step_t[h : h + 1, :]).astype(jnp.bfloat16))
        scan = jnp.dot(
            jnp.concatenate(mixing, axis=1),
            pair_operand(act.astype(jnp.bfloat16), lane),
            preferred_element_type=jnp.float32,
        )
        gain = jnp.where(
            lane < LANES // 2, skip[:, 2 * pair : 2 * pair + 1], skip[:, 2 * pair + 1 : 2 * pair + 2]
        )
        mixed_ref[:, pair * LANES : (pair + 1) * LANES] = scan + gain * act


def half_cut(tile, width, half):
    at = tile * width % half
    return slice(at, at + width)


def gate_tile(own_ref, got_ref, cut):
    gate = own_ref[:, cut] + got_ref[:, cut].astype(jnp.float32)
    return (gate, jax.nn.sigmoid(gate))


def gate_out_body(mixed_ref, own_ref, got_ref, mine_ref, peer_ref, keep_ref, send_ref, inverse_ref, out_ref):
    rows, inner_width = mixed_ref.shape
    half = inner_width // 2
    owner = owner_place()
    low, high, _ = full_rows(mine_ref, peer_ref)
    width = 2 * LANES
    cuts = [slice(at, at + width) for at in range(0, inner_width, width)]
    squares = jnp.zeros((rows, 1), jnp.float32)
    for cut in cuts:
        gate, sigmoid = gate_tile(own_ref, got_ref, cut)
        gated = mixed_ref[:, cut] * (gate * sigmoid)
        squares = squares + jnp.sum(gated * gated, axis=1, keepdims=True)
    inverse = lax.rsqrt(squares / inner_width + EPSILON)
    inverse_ref[...] = inverse
    for tile, cut in enumerate(cuts):
        gate, sigmoid = gate_tile(own_ref, got_ref, cut)
        near = half_cut(tile, width, half)
        gain = (low if cut.start < half else high)[5:6, near]
        normed = mixed_ref[:, cut] * (gate * sigmoid) * inverse
        out_ref[cut.start // half, :, near] = (normed * gain).astype(jnp.bfloat16)
    keep_ref[...] = out_ref[owner]
    send_ref[...] = out_ref[1 - owner]


def gate_grad_body(mixed_ref, own_ref, q_own_ref, got_ref, mine_ref, peer_ref, inverse_ref, keep_ref, send_ref, far_send_ref, dmixed_ref, gain_grad_ref, dgate_ref):
    rows, inner_width = mixed_ref.shape
    half = inner_width // 2
    owner, core = owner_place(), core_place()
    low, high, _ = full_rows(mine_ref, peer_ref)
    width = 2 * LANES
    cuts = [slice(at, at + width) for at in range(0, inner_width, width)]
    inverse = inverse_ref[...]

    def operands(tile, cut):
        near = half_cut(tile, width, half)
        in_low = cut.start < half
        gain = (low if in_low else high)[5:6, near]
        far = got_ref[:, inner_width + near.start : inner_width + near.stop]
        q = jnp.where((owner == 0) == in_low, q_own_ref[:, near], far.astype(jnp.float32))
        return (near, gain, q)

    cross = jnp.zeros((rows, 1), jnp.float32)
    for tile, cut in enumerate(cuts):
        _, gain, q = operands(tile, cut)
        gate, sigmoid = gate_tile(own_ref, got_ref, cut)
        cross = cross + jnp.sum(
            q * gain * (mixed_ref[:, cut] * (gate * sigmoid)), axis=1, keepdims=True
        )
    mean_cross = cross * inverse / inner_width
    for tile, cut in enumerate(cuts):
        near, gain, q = operands(tile, cut)
        gate, sigmoid = gate_tile(own_ref, got_ref, cut)
        silu = gate * sigmoid
        mixed = mixed_ref[:, cut]
        normed = mixed * silu * inverse
        gain_grad_ref[:, cut] = jnp.sum(q * normed, axis=0, keepdims=True)
        dgated = inverse * (q * gain - normed * mean_cross)
        dmixed_ref[:, cut] = dgated * silu
        dgate_ref[cut.start // half, :, near] = (
            dgated * mixed * (sigmoid * (1.0 + gate * (1.0 - sigmoid)))
        ).astype(jnp.bfloat16)
    keep_ref[...] = dgate_ref[core]
    send_ref[...] = dgate_ref[1 - core]
    far_send_ref[:rows] = dgate_ref[1 - core]
    far_send_ref[rows:] = dgate_ref[core]


def backward_body(lens_ref, dmixed_ref, xbc_ref, conv_ref, rates_ref, mine_ref, peer_ref, gain_grad_ref, keep_ref, send_ref, small_keep_ref, small_send_ref, rest_ref, small_ref):
    rows, channels = conv_ref.shape
    tiles = channels // LANES
    pairs = tiles - 2
    heads = 2 * pairs
    taps = 4
    half_tiles = tiles // 2
    small_ref[...] = jnp.zeros(small_ref.shape, jnp.float32)
    low, high, both = full_rows(mine_ref, peer_ref)
    position, start = row_marks(lens_ref, rows)
    usable = [position - (taps - 1 - k) >= start for k in range(taps)]
    lane = lax.broadcasted_iota(jnp.int32, (1, LANES), 1)
    decay = both[6:7, LANES : LANES + heads]
    skip = both[6:7, 2 * LANES : 2 * LANES + heads]
    step, cum, rate_sigmoid = rates_ref[0], rates_ref[1], rates_ref[2]
    step_t, cum_t = step.T, cum.T
    mask = kept_pairs(start, rows)

    def cut(tile):
        return slice(tile * LANES, (tile + 1) * LANES)

    def act_of(tile):
        conv = conv_ref[:, cut(tile)]
        sigmoid = jax.nn.sigmoid(conv)
        return (conv * sigmoid, sigmoid * (1.0 + conv * (1.0 - sigmoid)))

    def finish_tile(tile, dconv):
        owner, at = tile // half_tiles, tile % half_tiles * LANES
        xbc = xbc_ref[:, cut(tile)]
        small_ref[owner, 4:5, at : at + LANES] = jnp.sum(dconv, axis=0, keepdims=True)
        small_ref[owner, taps - 1 : taps, at : at + LANES] = jnp.sum(
            dconv * xbc, axis=0, keepdims=True
        )
        total = channel_row(low, high, taps - 1, tile) * dconv
        for k in range(taps - 1):
            behind = taps - 1 - k
            kept = jnp.where(usable[k], dconv, 0.0)
            small_ref[owner, k : k + 1, at : at + LANES] = jnp.sum(
                kept * pltpu.roll(xbc, behind, 0), axis=0, keepdims=True
            )
            total = total + channel_row(low, high, k, tile) * pltpu.roll(kept, rows - behind, 0)
        rest_ref[owner, :, at : at + LANES] = total.astype(jnp.bfloat16)

    keys_act, keys_slope = act_of(tiles - 2)
    queries_act, queries_slope = act_of(tiles - 1)
    keys, queries = keys_act.astype(jnp.bfloat16), queries_act.astype(jnp.bfloat16)
    inner = lax.dot_general(
        queries, keys, (((1,), (1,)), ((), ())), preferred_element_type=jnp.float32
    )
    dinner = jnp.zeros((rows, rows), jnp.float32)
    dstep_rows = []
    dcum = jnp.zeros((rows, heads), jnp.float32)
    skip_grad = jnp.zeros((1, heads), jnp.float32)
    head_lane = lax.broadcasted_iota(jnp.int32, (1, heads), 1)
    for pair in range(pairs):
        act, slope = act_of(pair)
        dmixed = dmixed_ref[:, cut(pair)]
        dscan = dmixed.astype(jnp.bfloat16)
        operand = pair_operand(act.astype(jnp.bfloat16), lane)
        dmixing = lax.dot_general(
            dscan, operand, (((1,), (1,)), ((), ())), preferred_element_type=jnp.float32
        )
        direct = jnp.sum(dmixed * act, axis=0, keepdims=True)
        mixing = []
        for j in range(2):
            h = 2 * pair + j
            spread = jnp.where(mask, cum[:, h : h + 1] - cum_t[h : h + 1, :], FAR)
            decays = jnp.exp(spread)
            step_row = step_t[h : h + 1, :]
            weight = inner * decays
            mixing.append((weight * step_row).astype(jnp.bfloat16))
            grad = dmixing[:, j * rows : (j + 1) * rows]
            dinner = dinner + grad * decays * step_row
            term = grad * weight
            dstep_rows.append(jnp.sum(term, axis=0, keepdims=True))
            dcum = dcum + jnp.where(
                head_lane == h, jnp.sum(term * step_row, axis=1, keepdims=True), 0.0
            )
            in_head = (lane < LANES // 2) if j == 0 else (lane >= LANES // 2)
            skip_grad = skip_grad + jnp.where(
                head_lane == h,
                jnp.sum(jnp.where(in_head, direct, 0.0), axis=1, keepdims=True),
                0.0,
            )
        dinput = lax.dot_general(
            jnp.concatenate(mixing, axis=1),
            dscan,
            (((0,), (0,)), ((), ())),
            preferred_element_type=jnp.float32,
        )
        gain = jnp.where(
            lane < LANES // 2, skip[:, 2 * pair : 2 * pair + 1], skip[:, 2 * pair + 1 : 2 * pair + 2]
        )
        dact = jnp.where(lane < LANES // 2, dinput[:rows], dinput[rows:]) + gain * dmixed
        finish_tile(pair, dact * slope)
    dinner_low = dinner.astype(jnp.bfloat16)
    dqueries = jnp.dot(dinner_low, keys, preferred_element_type=jnp.float32)
    dkeys = lax.dot_general(
        dinner_low, queries, (((0,), (0,)), ((), ())), preferred_element_type=jnp.float32
    )
    finish_tile(tiles - 2, dkeys * keys_slope)
    finish_tile(tiles - 1, dqueries * queries_slope)
    dstep_t = jnp.concatenate(dstep_rows, axis=0)
    dstep = dstep_t.T
    dcum = dcum - step * dstep
    upper = jnp.where(
        lax.broadcasted_iota(jnp.int32, (rows, rows), 1)
        >= lax.broadcasted_iota(jnp.int32, (rows, rows), 0),
        1.0,
        0.0,
    ).astype(jnp.float32)
    drate = exact_dot(upper, dcum)
    speed = jnp.exp(decay)
    draw = (dstep - drate * speed) * rate_sigmoid
    tail = jnp.concatenate([draw, jnp.zeros((rows, LANES - heads), jnp.float32)], axis=1)
    for side in range(2):
        rest_ref[side, :, channels // 2 :] = tail.astype(jnp.bfloat16)
    bias_grad = jnp.sum(draw, axis=0, keepdims=True)
    decay_grad = jnp.sum(-drate * step * speed, axis=0, keepdims=True)
    half_inner = pairs * LANES // 2
    half_heads = heads // 2
    for owner in range(2):
        small_ref[owner, 5:6, 0:half_inner] = gain_grad_ref[
            :, owner * half_inner : (owner + 1) * half_inner
        ]
        for place, item in enumerate((bias_grad, decay_grad, skip_grad)):
            at = place * LANES
            small_ref[owner, 6:7, at : at + half_heads] = item[
                :, owner * half_heads : (owner + 1) * half_heads
            ]
    core, place = core_place(), owner_place()
    keep_ref[...] = rest_ref[core]
    send_ref[...] = rest_ref[1 - core]
    small_keep_ref[...] = small_ref[place]
    small_send_ref[...] = small_ref[1 - place]


def whole(shape, dtype):
    return jax.ShapeDtypeStruct(shape, dtype)


def call(body, out_shape, operands, scratch=(), lens=None):
    vmem = pl.BlockSpec(memory_space=pltpu.VMEM)
    in_specs = [vmem for _ in operands]
    if lens is not None:
        operands = (lens, *operands)
        in_specs = [pl.BlockSpec(memory_space=pltpu.SMEM), *in_specs]
    return pl.pallas_call(
        body,
        out_shape=out_shape,
        in_specs=in_specs,
        out_specs=[vmem for _ in out_shape],
        scratch_shapes=[pltpu.VMEM(item.shape, item.dtype) for item in scratch],
        compiler_params=pltpu.CompilerParams(vmem_limit_bytes=40 << 20),
        name=body.__name__,
        cost_estimate=pl.CostEstimate(flops=1, bytes_accessed=1, transcendentals=0),
    )(*operands)


def unit_rows(tokens):
    values = tokens.astype(jnp.float32)
    return lax.rsqrt(jnp.mean(values * values, axis=-1, keepdims=True) + EPSILON)


def lanes_product(left, right):
    return lax.dot_general(
        left, right, (((1,), (1,)), ((), ())), preferred_element_type=jnp.float32
    )


def rows_product(left, right):
    return lax.dot_general(
        left, right, (((0,), (0,)), ((), ())), preferred_element_type=jnp.float32
    )


def lane_half(size):
    return pl.ds(pl.multiple_of(owner_place() * size, LANES), size)


def half_means(tokens_ref, size):
    return tokens_ref[:, lane_half(size)].astype(jnp.float32) * unit_rows(tokens_ref[...])


def norm_body(first_ref, second_ref, gain_ref, out_first_ref, out_second_ref):
    for tokens_ref, out_ref in ((first_ref, out_first_ref), (second_ref, out_second_ref)):
        means = half_means(tokens_ref, out_ref.shape[1])
        out_ref[...] = (means * gain_ref[...]).astype(jnp.bfloat16)


def project_rest(normed, weight_ref, rest_ref, inner_width):
    rest_width = weight_ref.shape[0] - inner_width
    whole_tiles = rest_width // LANES * LANES
    rest_ref[:, :whole_tiles] = lanes_product(
        normed, weight_ref[inner_width : inner_width + whole_tiles, :]
    ).astype(rest_ref.dtype)
    tail = lanes_product(normed, weight_ref[inner_width + whole_tiles :, :])
    blank = jnp.zeros((tail.shape[0], LANES - tail.shape[1]), jnp.float32)
    rest_ref[:, whole_tiles:] = jnp.concatenate([tail, blank], axis=1).astype(rest_ref.dtype)


def project_own_body(tokens_ref, cotangent_ref, gain_ref, weight_ref, out_weight_ref, normed_ref, rest_ref, gate_ref, q_ref):
    inner_width = gate_ref.shape[1]
    normed = (half_means(tokens_ref, normed_ref.shape[1]) * gain_ref[...]).astype(jnp.bfloat16)
    normed_ref[...] = normed
    project_rest(normed, weight_ref, rest_ref, inner_width)
    gate_ref[...] = lanes_product(normed, weight_ref[:inner_width, :])
    q_ref[...] = lanes_product(cotangent_ref[...], out_weight_ref[...])


def project_far_body(inner_width, tokens_ref, gain_ref, weight_ref, normed_ref, rest_ref):
    normed = (half_means(tokens_ref, normed_ref.shape[1]) * gain_ref[...]).astype(jnp.bfloat16)
    normed_ref[...] = normed
    project_rest(normed, weight_ref, rest_ref, inner_width)


def gate_far_body(normed_ref, cotangent_ref, weight_ref, out_weight_ref, send_ref):
    inner_width = send_ref.shape[1] - out_weight_ref.shape[0]
    send_ref[:, :inner_width] = lanes_product(
        normed_ref[...], weight_ref[:inner_width, :]
    ).astype(send_ref.dtype)
    send_ref[:, inner_width:] = lanes_product(
        cotangent_ref[...], out_weight_ref[...]
    ).astype(send_ref.dtype)


def branch_body(keep_ref, got_ref, weight_ref, own_ref, send_ref):
    send_ref[...] = jnp.dot(
        got_ref[: send_ref.shape[0], :], weight_ref[...], preferred_element_type=jnp.float32
    ).astype(send_ref.dtype)
    own_ref[...] = jnp.dot(keep_ref[...], weight_ref[...], preferred_element_type=jnp.float32)


def input_grad_body(*refs):
    tokens, gates, rests = refs[0:4], refs[4:8], refs[8:12]
    gain_ref, weight_ref = refs[12:14]
    rows = tokens[0].shape[0]
    gate_starts = (0, rows, 0, 0)
    own_ref, far_ref, sib_ref, gain_grad_ref = refs[14:18]
    outs = (
        own_ref,
        far_ref.at[0:rows],
        sib_ref,
        far_ref.at[rows:],
    )
    core = core_place()
    half_inner = gates[0].shape[1]
    half_channels = rests[0].shape[1] - LANES
    tail = weight_ref.shape[0] - 2 * (half_inner + half_channels)
    gate_rows = pl.ds(pl.multiple_of(core * half_inner, LANES), half_inner)
    rest_rows = pl.ds(
        pl.multiple_of(2 * half_inner + core * half_channels, LANES), half_channels
    )
    gate_weight = weight_ref[gate_rows, :]
    rest_weight = weight_ref[rest_rows, :]
    tail_weight = weight_ref[2 * (half_inner + half_channels) :, :]
    gain = gain_ref[...]
    gain_grad = jnp.zeros_like(gain)
    for tokens_ref, gate_ref, at, rest_ref, out_ref in zip(
        tokens, gates, gate_starts, rests, outs
    ):
        dnormed = jnp.dot(
            gate_ref[at : at + rows, :], gate_weight, preferred_element_type=jnp.float32
        )
        dnormed = dnormed + jnp.dot(
            rest_ref[:, :half_channels], rest_weight, preferred_element_type=jnp.float32
        )
        dtail = jnp.dot(
            rest_ref[:, half_channels : half_channels + tail],
            tail_weight,
            preferred_element_type=jnp.float32,
        )
        dnormed = dnormed + jnp.where(core == 0, dtail, 0.0)
        means = half_means(tokens_ref, gain.shape[1])
        gain_grad = gain_grad + jnp.sum(dnormed * means, axis=0, keepdims=True)
        out_ref[...] = (dnormed * gain).astype(out_ref.dtype)
    gain_grad_ref[...] = gain_grad


def tokens_grad_body(tokens_ref, cotangent_ref, own_ref, far_ref, sib_ref, out_ref):
    rows, half = own_ref.shape
    first = owner_place() == 0
    inverse = unit_rows(tokens_ref[...])
    own = own_ref[...] + sib_ref[:rows].astype(jnp.float32)
    far = far_ref[:rows].astype(jnp.float32) + sib_ref[rows:].astype(jnp.float32)
    parts = []
    cross = jnp.zeros_like(inverse)
    for side in range(2):
        cut = slice(side * half, (side + 1) * half)
        dmeans = jnp.where(first == (side == 0), own, far)
        means = tokens_ref[:, cut].astype(jnp.float32) * inverse
        cross = cross + jnp.sum(dmeans * means, axis=1, keepdims=True)
        parts.append((cut, dmeans, means))
    for cut, dmeans, means in parts:
        out_ref[:, cut] = cotangent_ref[:, cut].astype(jnp.float32) + inverse * (
            dmeans - means * (cross / (2 * half))
        )


def left_lanes(lefts, starts, rows, at, size):
    cut = pl.ds(pl.multiple_of(at, LANES), size)
    return jnp.concatenate(
        [ref[first : first + rows, cut] for ref, first in zip(lefts, starts)], axis=0
    )


def block_grad_body(part, starts, right_half, *refs):
    lefts, rights, (send_ref, keep_ref) = refs[0:4], refs[4:8], refs[8:]
    rows = rights[0].shape[0]
    width = send_ref.shape[1]
    lanes = slice(None)
    if right_half:
        lanes = pl.ds(pl.multiple_of(core_place() * width, LANES), width)
    right = jnp.concatenate([ref[:, lanes] for ref in rights], axis=0)
    at, size, order = part
    bit = chip_bit(order[0])
    half = size // 2
    for ref, side in ((send_ref, 1 - bit), (keep_ref, bit)):
        left = left_lanes(lefts, starts, rows, at + side * half, half)
        ref[...] = rows_product(left, right).astype(ref.dtype)


SMALL_ROWS = 16


def block_small_body(part, starts, *refs):
    lefts, rights, (mine_ref, far_ref, send_ref, keep_ref) = refs[0:4], refs[4:8], refs[8:]
    rows = rights[0].shape[0]
    width = send_ref.shape[1]
    right = jnp.concatenate([ref[...] for ref in rights], axis=0)
    total = mine_ref[...] + far_ref[...]
    count, wide = total.shape
    blank = jnp.zeros((SMALL_ROWS - count, width), jnp.float32)
    smalls = []
    for quarter in range(4):
        piece = total[:, quarter * width : min(wide, (quarter + 1) * width)]
        if piece.shape[1] < width:
            rest = jnp.zeros((count, width - piece.shape[1]), jnp.float32)
            piece = jnp.concatenate([piece, rest], axis=1) if piece.shape[1] else rest
        smalls.append(jnp.concatenate([piece, blank], axis=0))
    heads = total[6:7, :width]
    high = heads.astype(jnp.bfloat16).astype(jnp.float32)
    row = lax.broadcasted_iota(jnp.int32, (SMALL_ROWS, 1), 0)
    chip = lax.div(lax.axis_index("replica"), 2)
    smalls[3] = jnp.where(row == chip, high, 0.0) + jnp.where(
        row == chip + SMALL_ROWS // 2, heads - high, 0.0
    )
    at, size, order = part
    bit = chip_bit(order[0])
    quarter = size // 4
    for ref, side in ((send_ref, 1 - bit), (keep_ref, bit)):
        left = left_lanes(lefts, starts, rows, at + side * 2 * quarter, 2 * quarter)
        block = rows_product(left, right)
        for q in range(2):
            base = q * (quarter + SMALL_ROWS)
            ref[base : base + quarter, :] = block[q * quarter : (q + 1) * quarter].astype(
                ref.dtype
            )
            ref[base + quarter : base + quarter + SMALL_ROWS, :] = jnp.where(
                side == 0, smalls[q], smalls[2 + q]
            ).astype(ref.dtype)


def block_norm_body(part, starts, norm_row, *refs):
    lefts, rights, (norm_ref, send_ref, keep_ref) = refs[0:4], refs[4:8], refs[8:]
    rows = rights[0].shape[0]
    right = jnp.concatenate([ref[...] for ref in rights], axis=0)
    at, size, order = part
    bit = chip_bit(order[0])
    half = size // 2
    row = lax.broadcasted_iota(jnp.int32, (half, 1), 0)
    for ref, side in ((send_ref, 1 - bit), (keep_ref, bit)):
        left = left_lanes(lefts, starts, rows, at + side * half, half)
        block = rows_product(left, right)
        here = (row + (at + side * half)) == norm_row
        ref[...] = jnp.where(here, norm_ref[...], block).astype(ref.dtype)


def halve_body(bit, keep_ref, got_ref, send_ref, out_ref):
    rows = send_ref.shape[0]
    bit = chip_bit(bit)
    for ref, side in ((send_ref, 1 - bit), (out_ref, bit)):
        cut = pl.ds(pl.multiple_of(side * rows, 16), rows)
        ref[...] = (keep_ref[cut, :] + got_ref[cut, :].astype(jnp.float32)).astype(ref.dtype)


def add_body(keep_ref, got_ref, out_ref):
    out_ref[...] = (
        keep_ref[...].astype(jnp.float32) + got_ref[...].astype(jnp.float32)
    ).astype(out_ref.dtype)


def after(value, *earlier):
    return lax.optimization_barrier((value, *earlier))[0]


class PartSum:
    def __init__(self, order, make_block, early=False):
        self.order, self.make_block, self.early = order, make_block, early
        self.steps = 0
        self.pieces = None

    def advance(self, token):
        f32, low = jnp.float32, jnp.bfloat16
        step = self.steps
        self.steps += 1
        if step == 0:
            send, self.keep = self.make_block(token)
            bit = self.order[0]
        elif step == 1:
            keep = after(self.keep, token)
            shape = (keep.shape[0] // 2, keep.shape[1])

            def halve(*refs):
                halve_body(self.order[1], *refs)

            send, self.keep = call(
                halve, [whole(shape, low), whole(shape, f32)], (keep, self.got)
            )
            bit = self.order[1]
        elif step < 4:
            keep = after(self.keep, token)
            (send,) = call(add_body, [whole(keep.shape, low)], (keep, self.got))
            self.keep = send
            bit = self.order[2] if step == 2 else self.order[1]
        elif step == 4:
            send = jnp.concatenate([after(self.keep, token), self.got], axis=0)
            self.keep = send
            if self.early:
                self.sibling = swap_core(send)
            bit = self.order[0]
        else:
            got = after(self.got, token)
            sibling = after(self.sibling, got) if self.early else swap_core(self.keep)
            self.pieces = [self.keep, got, sibling, swap_core(got)]
            return got
        self.got = swap_chip(send, bit)
        return send


def part_quarters(order, pieces):
    first, second = chip_bit(order[0]), chip_bit(order[1])
    for which in range(2):
        side = first if which == 0 else 1 - first
        mine, sibling = pieces[which], pieces[2 + which]
        size = mine.shape[0] // 2
        for p in range(2):
            quarter = 2 * side + (second if p == 0 else 1 - second)
            yield quarter, mine, sibling, p * size


def write_part(out_ref, base, part, pieces, other):
    at, size, order = part
    size = size // 4
    for quarter, mine, sibling, row in part_quarters(order, pieces):
        rows = slice(row, row + size)
        value = jnp.where(other, sibling[rows, :], mine[rows, :]).astype(jnp.float32)
        out_ref[pl.ds(pl.multiple_of(base + at + quarter * size, 8), size), :] = value


def in_weight_body(gate_part, rest_parts, *refs):
    (out_ref, norm_ref), refs = refs[-2:], refs[:-2]
    gates, rests = refs[0:4], refs[4:]
    core = core_place()
    half_inner = gate_part[1]
    last_at, last_size, last_order = rest_parts[1]
    half_channels = last_at + last_size - LANES
    tail_at = 2 * (half_inner + half_channels)
    tail = out_ref.shape[0] - tail_at
    for side in range(2):
        other = core != side
        base = 2 * half_inner + side * half_channels
        write_part(out_ref, side * half_inner, gate_part, gates, other)
        write_part(out_ref, base, rest_parts[0], rests[0:4], other)
        size = last_size // 4
        for quarter, mine, sibling, row in part_quarters(last_order, rests[4:8]):
            rows = slice(row, row + size)
            value = jnp.where(other, sibling[rows, :], mine[rows, :]).astype(jnp.float32)

            @pl.when(quarter < 3)
            def _():
                place = base + last_at + quarter * size
                out_ref[pl.ds(pl.multiple_of(place, 8), size), :] = value

            if side == 0:

                @pl.when(quarter == 3)
                def _():
                    out_ref[tail_at:, :] = value[:tail]
                    both = mine[rows, :].astype(jnp.float32) + sibling[rows, :].astype(
                        jnp.float32
                    )
                    norm_ref[...] = both[tail : tail + norm_ref.shape[0]]


def small_body(order, *refs):
    pieces, out_ref = refs[:-1], refs[-1]
    count, wide = out_ref.shape[0] // 2, out_ref.shape[1]
    width = pieces[0].shape[1]
    for quarter, mine, sibling, row in part_quarters(order, pieces):
        size = mine.shape[0] // 2
        rows = slice(row + size - SMALL_ROWS, row + size)
        both = mine[rows, :].astype(jnp.float32) + sibling[rows, :].astype(jnp.float32)
        for place in range((wide + width - 1) // width):
            lanes = slice(place * width, min(wide, (place + 1) * width))

            @pl.when(quarter == place)
            def _():
                out_ref[:count, lanes] = both[:count, : lanes.stop - lanes.start]

        @pl.when(quarter == 3)
        def _():
            out_ref[count : count + 1, :width] = jnp.sum(both, axis=0, keepdims=True)


def out_weight_body(part, blocks, *refs):
    side = lax.div(pl.program_id(0), blocks)
    write_part(refs[-1], 0, part, refs[:-1], core_place() != side)


def assemble(body, outs, pieces, block):
    blocks = pieces[0].shape[1] // block
    return pl.pallas_call(
        body,
        grid=(outs[0].shape[1] // block,),
        out_shape=outs,
        in_specs=[
            pl.BlockSpec((item.shape[0], block), lambda i: (0, lax.rem(i, blocks)))
            for item in pieces
        ],
        out_specs=[pl.BlockSpec((out.shape[0], block), lambda i: (0, i)) for out in outs],
        compiler_params=pltpu.CompilerParams(vmem_limit_bytes=48 << 20),
        name=body.__name__,
        cost_estimate=pl.CostEstimate(flops=1, bytes_accessed=1, transcendentals=0),
    )(*pieces)


def swap(value, replica_bits, fsdp_bits):
    replicas, owners = lax.axis_size("replica"), lax.axis_size("fsdp")
    pairs = [
        (r * owners + f, (r ^ replica_bits) * owners + (f ^ fsdp_bits))
        for r in range(replicas)
        for f in range(owners)
    ]
    return lax.ppermute(value, AXES, pairs)


def swap_owner(value):
    return swap(value, 0, 1)


def swap_core(value):
    return swap(value, 1, 0)


def swap_chip(value, bit):
    return swap(value, 2 << bit, 0)


def join(place, own, other, axis):
    return jnp.where(
        place == 0,
        jnp.concatenate([own, other], axis=axis),
        jnp.concatenate([other, own], axis=axis),
    )


def part_of(value, place, parts, axis):
    size = value.shape[axis] // parts
    return lax.dynamic_slice_in_dim(value, place * size, size, axis)


def total_over_chips(block):
    chip = lax.axis_index("replica") // 2
    bits = range((lax.axis_size("replica") // 2).bit_length() - 1)
    rows, cols = block.shape
    kept = block.reshape((2,) * len(bits) + (rows >> len(bits), cols))
    for bit in bits:
        mine = (chip >> bit) & 1
        sent = lax.dynamic_index_in_dim(kept, 1 - mine, 0, keepdims=False).astype(jnp.bfloat16)
        got = swap_chip(sent, bit)
        kept = lax.dynamic_index_in_dim(kept, mine, 0, keepdims=False) + got.astype(jnp.float32)
    chunk = kept.astype(jnp.bfloat16)
    for bit in reversed(bits):
        chunk = join((chip >> bit) & 1, chunk, swap_chip(chunk, bit), 0)
    return chunk


def per_device(
    tokens,
    seq_lens,
    norm_gain,
    in_weight,
    conv_weight,
    conv_bias,
    step_bias,
    decay_log,
    skip_gain,
    out_gain,
    out_weight,
    cotangent,
):
    f32, low = jnp.float32, jnp.bfloat16
    owner = lax.axis_index("fsdp")
    core = lax.axis_index("replica") % 2
    chips = lax.axis_size("replica") // 2
    rows, width = tokens.shape
    half_width = width // 2
    half_inner = out_weight.shape[0]
    inner_width = 2 * half_inner
    half_channels = conv_bias.shape[0]
    channels = 2 * half_channels
    half_heads = skip_gain.shape[0]
    heads = 2 * half_heads
    weight = in_weight.T
    gain = norm_gain.astype(f32).reshape(1, -1)

    tokens_far = swap_owner(tokens)
    cotangent_far = swap_owner(cotangent)
    def project_far(*refs):
        project_far_body(inner_width, *refs)

    normed_far, rest_send = call(
        project_far,
        [whole((rows, half_width), low), whole((rows, channels + LANES), f32)],
        (after(tokens_far, cotangent_far), gain, weight),
    )
    rest_got = swap_owner(rest_send)
    normed_own, rest_own, gate_own, q_own = call(
        project_own_body,
        [
            whole((rows, half_width), low),
            whole((rows, channels + LANES), f32),
            whole((rows, inner_width), f32),
            whole((rows, half_inner), f32),
        ],
        (after(tokens, rest_send), cotangent, gain, weight, out_weight),
    )
    (gate_send,) = call(
        gate_far_body,
        [whole((rows, inner_width + half_inner), low)],
        (normed_far, cotangent_far, weight, out_weight),
    )
    conv_weight, conv_bias, step_bias, decay_log, skip_gain, out_gain = after(
        (conv_weight, conv_bias, step_bias, decay_log, skip_gain, out_gain), gate_send
    )

    def row(item):
        item = item.astype(f32).reshape(-1, item.shape[-1])
        return jnp.pad(item, ((0, 0), (0, half_channels - item.shape[-1])))

    def head_row(item):
        item = item.astype(f32)
        there = jnp.zeros_like(item)
        placed = jnp.where(
            owner == 0, jnp.concatenate([item, there]), jnp.concatenate([there, item])
        )
        return jnp.pad(placed, (0, LANES - heads))

    head_rows = jnp.concatenate([head_row(step_bias), head_row(decay_log), head_row(skip_gain)])
    mine = jnp.concatenate(
        [
            row(conv_weight),
            row(conv_bias),
            row(out_gain),
            row(head_rows),
            jnp.zeros((1, half_channels), f32),
        ],
        axis=0,
    )
    peer = swap_owner(mine)
    gate_got = swap_owner(after(gate_send, rest_got, peer))
    tokens_sib, tokens_far_sib = swap_core(tokens), swap_core(tokens_far)
    cotangent_sib, cotangent_far_sib = swap_core(cotangent), swap_core(cotangent_far)
    normed_sib, normed_far_sib = call(
        norm_body,
        [whole((rows, half_width), low)] * 2,
        (tokens_sib, tokens_far_sib, gain),
    )

    xbc, conv, mixed, rates = call(
        forward_body,
        [
            whole((rows, channels), f32),
            whole((rows, channels), f32),
            whole((rows, inner_width), f32),
            whole((3, rows, heads), f32),
        ],
        (rest_own, rest_got, mine, peer),
        lens=seq_lens,
    )
    out_keep, out_send, inverse = call(
        gate_out_body,
        [*[whole((rows, half_inner), low)] * 2, whole((rows, 1), f32)],
        (mixed, gate_own, gate_got, mine, peer),
        scratch=[whole((2, rows, half_inner), low)],
    )
    out_far, out_sib = swap_owner(out_send), swap_core(out_keep)
    dgate, dgate_send, far_send, dmixed, gain_grad = call(
        gate_grad_body,
        [
            *[whole((rows, half_inner), low)] * 2,
            whole((2 * rows, half_inner), low),
            whole((rows, inner_width), f32),
            whole((1, inner_width), f32),
        ],
        (
            after(mixed, normed_sib, normed_far_sib, cotangent_sib, cotangent_far_sib),
            gate_own,
            q_own,
            gate_got,
            mine,
            peer,
            inverse,
        ),
        scratch=[whole((2, rows, half_inner), low)],
    )
    far, dgate_sib = swap_owner(far_send), swap_core(dgate_send)
    drest, drest_send, small_keep, small_send = call(
        backward_body,
        [
            *[whole((rows, half_channels + LANES), low)] * 2,
            *[whole((8, half_channels), f32)] * 2,
        ],
        (dmixed, xbc, conv, rates, mine, peer, gain_grad),
        scratch=[
            whole((2, rows, half_channels + LANES), low),
            whole((2, 8, half_channels), f32),
        ],
        lens=seq_lens,
    )
    small_far = swap_owner(small_send)
    out_far_sib = swap_core(after(out_far, drest))
    drest_far, drest_far_sib = swap_owner(drest), swap(drest_send, 1, 1)
    drest_sib = swap_core(drest_send)

    tokens_all = (tokens, tokens_far, tokens_sib, tokens_far_sib)
    normed_all = (normed_own, normed_far, normed_sib, normed_far_sib)
    cotangent_all = (cotangent, cotangent_far, cotangent_sib, cotangent_far_sib)
    drest_all = (drest, drest_far, drest_sib, drest_far_sib)
    out_all = (out_keep, out_far, out_sib, out_far_sib)
    out_starts, gate_starts, rest_starts = (0,) * 4, (0, rows, 0, 0), (0,) * 4
    state = {}
    if chips == 8:
        cut = (half_channels + LANES) * 3 // 5 // LANES * LANES
        out_part = (0, half_inner, (0, 1, 2))
        gate_part = (0, half_inner, (1, 0, 2))
        rest_parts = ((0, cut, (0, 1, 2)), (cut, half_channels + LANES - cut, (1, 0, 2)))
        norm_row = half_channels + heads

        def maker(body, part, given, size, extra=(), early=False):
            lefts, starts, rights = given

            def make(token):
                def block_grad(*refs):
                    body(part, starts, *refs)

                if lefts is None:
                    state["far_sib"] = swap_core(after(far, token))
                    sources = (dgate, far, dgate_sib, state["far_sib"])
                else:
                    sources = lefts
                tied = sources if token is None else (after(sources[0], token), *sources[1:])
                more = [item() for item in extra]
                sizes = [whole((size // 2, half_width), dtype) for dtype in (low, f32)]
                return call(block_grad, sizes, (*tied, *rights, *more))

            return PartSum(part[2], make, early)

        def out_block(part, starts, *refs):
            block_grad_body(part, starts, True, *refs)

        def rest_block(part, starts, *refs):
            block_grad_body(part, starts, False, *refs)

        def norm_block(part, starts, *refs):
            block_norm_body(part, starts, norm_row, *refs)

        gate_sources = (None, gate_starts, normed_all)
        rest_sources = (drest_all, rest_starts, normed_all)
        sums = (
            maker(out_block, out_part, (out_all, out_starts, cotangent_all), half_inner),
            maker(
                block_small_body,
                gate_part,
                gate_sources,
                half_inner + 4 * SMALL_ROWS,
                (lambda: small_keep, lambda: small_far),
            ),
            maker(rest_block, rest_parts[0], rest_sources, rest_parts[0][1], early=True),
            maker(
                norm_block,
                rest_parts[1],
                rest_sources,
                rest_parts[1][1],
                (lambda: state["norm_grad"],),
                early=True,
            ),
        )
        token = None
    else:
        token = drest

        def total_of(left, starts, right):
            left = [item[first : first + rows] for item, first in zip(left, starts)]
            return total_over_chips(
                rows_product(jnp.concatenate(left, axis=0), jnp.concatenate(right, axis=0))
            )

        out_total = total_of(
            out_all,
            out_starts,
            [part_of(item, core, 2, 1) for item in cotangent_all],
        )
        state["far_sib"] = swap_core(far)
        dgate_all = (dgate, far, dgate_sib, state["far_sib"])
        gate_total = total_of(dgate_all, gate_starts, normed_all)
        rest_total = total_of(drest_all, rest_starts, normed_all)
        rest_sib = swap_core(rest_total)
        out_weight_grad = join(core, out_total, swap_core(out_total), 1).astype(f32)
        in_weight_grad = (
            jnp.concatenate(
                [
                    join(core, gate_total, swap_core(gate_total), 0),
                    join(core, rest_total[:half_channels], rest_sib[:half_channels], 0),
                    rest_total[half_channels : half_channels + heads],
                ],
                axis=0,
            )
            .astype(f32)
            .T
        )

    def out_projection(token):
        own, send = call(
            branch_body,
            [whole((rows, width), f32), whole((rows, width), low)],
            (after(out_keep, token), out_far, out_weight),
        )
        state["branch"] = (own, swap_owner(send))
        return send

    def block_sum(token):
        own, far = state["branch"]
        state["block_out"] = (
            tokens.astype(f32) + after(own, token) + far.astype(f32)
        ).astype(low)
        return state["block_out"]

    def input_norm(token):
        state["dmeans"] = call(
            input_grad_body,
            [
                whole((rows, half_width), f32),
                whole((2 * rows, half_width), low),
                whole((rows, half_width), low),
                whole((1, half_width), f32),
            ],
            (
                *tokens_all,
                after(dgate, token),
                far,
                dgate_sib,
                state["far_sib"],
                *drest_all,
                gain,
                weight,
            ),
        )
        state["norm_grad"] = state["dmeans"][3]
        return state["norm_grad"]

    def means_far(token):
        send = after(state["dmeans"][1], token)
        state["means_far"] = swap_owner(send)
        return send

    def means_sib(token):
        far = after(state["means_far"], token)
        send = jnp.concatenate([state["dmeans"][2], far[rows:]], axis=0)
        state["means_sib"] = swap_core(send)
        return send

    def tokens_grad(token):
        (state["grad_tokens"],) = call(
            tokens_grad_body,
            [whole((rows, width), f32)],
            (
                tokens,
                cotangent,
                after(state["dmeans"][0], token),
                state["means_far"],
                state["means_sib"],
            ),
        )
        return state["grad_tokens"]

    def small_results(total, row):
        return (
            total[0:4],
            total[4],
            total[row, 0:half_heads],
            total[row, LANES : LANES + half_heads],
            total[row, 2 * LANES : 2 * LANES + half_heads],
            total[5, :half_inner],
        )

    def small_assembly(token):
        def small_rows(*refs):
            small_body(gate_part[2], *refs)

        pieces = sums[1].pieces
        (total,) = call(
            small_rows,
            [whole((16, half_channels), f32)],
            (after(pieces[0], token), *pieces[1:]),
        )
        state["smalls"] = small_results(total, 8)
        return state["smalls"][1]

    def out_assembly(token):
        def out_weight_lanes(*refs):
            out_weight_body(out_part, 2, *refs)

        pieces = sums[0].pieces
        (state["out_weight"],) = assemble(
            out_weight_lanes,
            [whole(out_weight.shape, f32)],
            [after(pieces[0], token), *pieces[1:]],
            half_width // 2,
        )
        return state["out_weight"]

    if chips == 8:
        steps = {
            "n": input_norm,
            "x": means_far,
            "k": means_sib,
            "t": tokens_grad,
            "b": out_projection,
            "p": block_sum,
            "s": small_assembly,
            "o": out_assembly,
        }
        for mark in ORDER:
            step = steps[mark] if mark in steps else sums[int(mark)].advance
            token = step(token)

        def in_weight_rows(*refs):
            in_weight_body(gate_part, rest_parts, *refs)

        pieces = [piece for part in sums[1:] for piece in part.pieces]
        in_weight_rows_grad, norm_rows = assemble(
            in_weight_rows,
            [whole(weight.shape, f32), whole((8, half_width), f32)],
            [after(pieces[0], token), *pieces[1:]],
            LANES,
        )
        in_weight_grad = in_weight_rows_grad.T
        out_weight_grad = state["out_weight"]
        norm_gain_grad = norm_rows[0]
    else:
        for step in (out_projection, block_sum, input_norm, means_far, means_sib, tokens_grad):
            step(token)
        total = jnp.concatenate(
            [(small_keep + small_far)[:7], row(state["norm_grad"])], axis=0
        )
        bits = 1
        while bits < 2 * chips:
            total = total + swap(total, bits, 0)
            bits *= 2
        norm_gain_grad = total[7, :half_width]
        state["smalls"] = small_results(total, 6)
    return (
        state["block_out"],
        state["grad_tokens"],
        norm_gain_grad,
        in_weight_grad,
        *state["smalls"],
        out_weight_grad,
    )


def solution(mesh):
    placed = (
        P(("replica", "fsdp"), None),
        P(("replica", "fsdp"), None),
        P("fsdp"),
        P("fsdp", None),
        P(None, "fsdp"),
        P("fsdp"),
        P("fsdp"),
        P("fsdp"),
        P("fsdp"),
        P("fsdp"),
        P("fsdp", None),
        P(("replica", "fsdp"), None),
    )
    return jax.shard_map(
        per_device,
        mesh=mesh,
        in_specs=placed,
        out_specs=(
            P(("replica", "fsdp"), None),
            P(("replica", "fsdp"), None),
            P("fsdp"),
            P("fsdp", None),
            P(None, "fsdp"),
            P("fsdp"),
            P("fsdp"),
            P("fsdp"),
            P("fsdp"),
            P("fsdp"),
            P("fsdp", None),
        ),
        check_vma=False,
    )
```

```python
import jax
import jax.numpy as jnp
from jax import lax
from jax.experimental import pallas as pl
from jax.experimental.pallas import tpu as pltpu
from jax.sharding import PartitionSpec as P

EPSILON = 1e-05
AXES = ("replica", "fsdp")
LANES = 128
FAR = -1e30
ORDER = "012n3x0123k0123tb0123p012301os23"


def owner_place():
    return lax.axis_index("fsdp")


def core_place():
    return lax.rem(lax.axis_index("replica"), 2)


def chip_bit(bit):
    return lax.rem(lax.div(lax.axis_index("replica"), 2 << bit), 2)


def full_rows(mine_ref, peer_ref):
    first = owner_place() == 0
    mine, peer = mine_ref[...], peer_ref[...]
    return (jnp.where(first, mine, peer), jnp.where(first, peer, mine), mine + peer)


def row_marks(lens_ref, rows):
    end_one, end_two = lens_ref[0, 0], lens_ref[0, 0] + lens_ref[0, 1]
    position = lax.broadcasted_iota(jnp.int32, (rows, 1), 0)
    start = jnp.where(position >= end_two, end_two, jnp.where(position >= end_one, end_one, 0))
    return (position, start)


def kept_pairs(start, rows):
    key = lax.broadcasted_iota(jnp.int32, (rows, rows), 1)
    query = lax.broadcasted_iota(jnp.int32, (rows, rows), 0)
    return (key <= query) & (key >= start)


def channel_row(low, high, row, tile):
    half = low.shape[1] // LANES
    source = low if tile < half else high
    at = (tile if tile < half else tile - half) * LANES
    return source[row : row + 1, at : at + LANES]


def exact_dot(left, right):
    return jnp.dot(
        left, right, precision=lax.Precision.HIGHEST, preferred_element_type=jnp.float32
    )


def pair_operand(values, lane):
    zero = jnp.zeros_like(values)
    return jnp.concatenate(
        [jnp.where(lane < LANES // 2, values, zero), jnp.where(lane < LANES // 2, zero, values)],
        axis=0,
    )


def forward_body(lens_ref, own_ref, wide_ref, got_ref, mine_ref, peer_ref, xbc_ref, conv_ref, mixed_ref, rates_ref):
    rows, channels = conv_ref.shape
    tiles = channels // LANES
    pairs = tiles - 2
    heads = 2 * pairs
    taps = 4
    low, high, both = full_rows(mine_ref, peer_ref)
    position, start = row_marks(lens_ref, rows)
    usable = [position - (taps - 1 - k) >= start for k in range(taps)]
    lane = lax.broadcasted_iota(jnp.int32, (1, LANES), 1)
    bias = both[6:7, 0:heads]
    decay = both[6:7, LANES : LANES + heads]
    skip = both[6:7, 2 * LANES : 2 * LANES + heads]
    tail = slice(channels, channels + heads)
    wide = wide_ref.shape[1]
    rate = own_ref[:, tail] + got_ref[:, channels - wide : channels - wide + heads] + bias
    step = jnp.maximum(rate, 0.0) + jnp.log1p(jnp.exp(-jnp.abs(rate)))
    rate_sigmoid = jax.nn.sigmoid(rate)
    lower = jnp.where(
        lax.broadcasted_iota(jnp.int32, (rows, rows), 1)
        <= lax.broadcasted_iota(jnp.int32, (rows, rows), 0),
        1.0,
        0.0,
    ).astype(jnp.float32)
    cum = exact_dot(lower, step * -jnp.exp(decay))
    rates_ref[0] = step
    rates_ref[1] = cum
    rates_ref[2] = rate_sigmoid
    step_t, cum_t = step.T, cum.T
    mask = kept_pairs(start, rows)

    def active_tile(tile):
        at = tile * LANES
        if at < wide:
            far = wide_ref[:, at : at + LANES].astype(jnp.float32)
        else:
            far = got_ref[:, at - wide : at - wide + LANES]
        xbc = own_ref[:, at : at + LANES] + far
        xbc_ref[:, at : at + LANES] = xbc
        conv = channel_row(low, high, 4, tile) + channel_row(low, high, taps - 1, tile) * xbc
        for k in range(taps - 1):
            shifted = pltpu.roll(xbc, taps - 1 - k, 0)
            conv = conv + channel_row(low, high, k, tile) * jnp.where(usable[k], shifted, 0.0)
        conv_ref[:, at : at + LANES] = conv
        return conv * jax.nn.sigmoid(conv)

    keys = active_tile(tiles - 2).astype(jnp.bfloat16)
    queries = active_tile(tiles - 1).astype(jnp.bfloat16)
    inner = lax.dot_general(
        queries, keys, (((1,), (1,)), ((), ())), preferred_element_type=jnp.float32
    )
    for pair in range(pairs):
        act = active_tile(pair)
        mixing = []
        for h in (2 * pair, 2 * pair + 1):
            spread = jnp.where(mask, cum[:, h : h + 1] - cum_t[h : h + 1, :], FAR)
            mixing.append((inner * jnp.exp(spread) * step_t[h : h + 1, :]).astype(jnp.bfloat16))
        scan = jnp.dot(
            jnp.concatenate(mixing, axis=1),
            pair_operand(act.astype(jnp.bfloat16), lane),
            preferred_element_type=jnp.float32,
        )
        gain = jnp.where(
            lane < LANES // 2, skip[:, 2 * pair : 2 * pair + 1], skip[:, 2 * pair + 1 : 2 * pair + 2]
        )
        mixed_ref[:, pair * LANES : (pair + 1) * LANES] = scan + gain * act


def half_cut(tile, width, half):
    at = tile * width % half
    return slice(at, at + width)


def gate_tile(own_ref, got_ref, cut):
    gate = own_ref[:, cut] + got_ref[:, cut].astype(jnp.float32)
    return (gate, jax.nn.sigmoid(gate))


def gate_out_body(mixed_ref, own_ref, got_ref, mine_ref, peer_ref, keep_ref, send_ref, inverse_ref, out_ref):
    rows, inner_width = mixed_ref.shape
    half = inner_width // 2
    owner = owner_place()
    low, high, _ = full_rows(mine_ref, peer_ref)
    width = 2 * LANES
    cuts = [slice(at, at + width) for at in range(0, inner_width, width)]
    squares = jnp.zeros((rows, 1), jnp.float32)
    for cut in cuts:
        gate, sigmoid = gate_tile(own_ref, got_ref, cut)
        gated = mixed_ref[:, cut] * (gate * sigmoid)
        squares = squares + jnp.sum(gated * gated, axis=1, keepdims=True)
    inverse = lax.rsqrt(squares / inner_width + EPSILON)
    inverse_ref[...] = inverse
    for tile, cut in enumerate(cuts):
        gate, sigmoid = gate_tile(own_ref, got_ref, cut)
        near = half_cut(tile, width, half)
        gain = (low if cut.start < half else high)[5:6, near]
        normed = mixed_ref[:, cut] * (gate * sigmoid) * inverse
        out_ref[cut.start // half, :, near] = (normed * gain).astype(jnp.bfloat16)
    keep_ref[...] = out_ref[owner]
    send_ref[...] = out_ref[1 - owner]


def gate_grad_body(mixed_ref, own_ref, q_own_ref, got_ref, mine_ref, peer_ref, inverse_ref, keep_ref, send_ref, far_send_ref, dmixed_ref, gain_grad_ref, dgate_ref):
    rows, inner_width = mixed_ref.shape
    half = inner_width // 2
    owner, core = owner_place(), core_place()
    low, high, _ = full_rows(mine_ref, peer_ref)
    width = 2 * LANES
    cuts = [slice(at, at + width) for at in range(0, inner_width, width)]
    inverse = inverse_ref[...]

    def operands(tile, cut):
        near = half_cut(tile, width, half)
        in_low = cut.start < half
        gain = (low if in_low else high)[5:6, near]
        far = got_ref[:, inner_width + near.start : inner_width + near.stop]
        q = jnp.where((owner == 0) == in_low, q_own_ref[:, near], far.astype(jnp.float32))
        return (near, gain, q)

    cross = jnp.zeros((rows, 1), jnp.float32)
    for tile, cut in enumerate(cuts):
        _, gain, q = operands(tile, cut)
        gate, sigmoid = gate_tile(own_ref, got_ref, cut)
        cross = cross + jnp.sum(
            q * gain * (mixed_ref[:, cut] * (gate * sigmoid)), axis=1, keepdims=True
        )
    mean_cross = cross * inverse / inner_width
    for tile, cut in enumerate(cuts):
        near, gain, q = operands(tile, cut)
        gate, sigmoid = gate_tile(own_ref, got_ref, cut)
        silu = gate * sigmoid
        mixed = mixed_ref[:, cut]
        normed = mixed * silu * inverse
        gain_grad_ref[:, cut] = jnp.sum(q * normed, axis=0, keepdims=True)
        dgated = inverse * (q * gain - normed * mean_cross)
        dmixed_ref[:, cut] = dgated * silu
        dgate_ref[cut.start // half, :, near] = (
            dgated * mixed * (sigmoid * (1.0 + gate * (1.0 - sigmoid)))
        ).astype(jnp.bfloat16)
    keep_ref[...] = dgate_ref[core]
    send_ref[...] = dgate_ref[1 - core]
    far_send_ref[:rows] = dgate_ref[1 - core]
    far_send_ref[rows:] = dgate_ref[core]


def backward_body(lens_ref, dmixed_ref, xbc_ref, conv_ref, rates_ref, mine_ref, peer_ref, gain_grad_ref, keep_ref, send_ref, small_keep_ref, small_send_ref, rest_ref, small_ref):
    rows, channels = conv_ref.shape
    tiles = channels // LANES
    pairs = tiles - 2
    heads = 2 * pairs
    taps = 4
    half_tiles = tiles // 2
    small_ref[...] = jnp.zeros(small_ref.shape, jnp.float32)
    low, high, both = full_rows(mine_ref, peer_ref)
    position, start = row_marks(lens_ref, rows)
    usable = [position - (taps - 1 - k) >= start for k in range(taps)]
    lane = lax.broadcasted_iota(jnp.int32, (1, LANES), 1)
    decay = both[6:7, LANES : LANES + heads]
    skip = both[6:7, 2 * LANES : 2 * LANES + heads]
    step, cum, rate_sigmoid = rates_ref[0], rates_ref[1], rates_ref[2]
    step_t, cum_t = step.T, cum.T
    mask = kept_pairs(start, rows)

    def cut(tile):
        return slice(tile * LANES, (tile + 1) * LANES)

    def act_of(tile):
        conv = conv_ref[:, cut(tile)]
        sigmoid = jax.nn.sigmoid(conv)
        return (conv * sigmoid, sigmoid * (1.0 + conv * (1.0 - sigmoid)))

    def finish_tile(tile, dconv):
        owner, at = tile // half_tiles, tile % half_tiles * LANES
        xbc = xbc_ref[:, cut(tile)]
        small_ref[owner, 4:5, at : at + LANES] = jnp.sum(dconv, axis=0, keepdims=True)
        small_ref[owner, taps - 1 : taps, at : at + LANES] = jnp.sum(
            dconv * xbc, axis=0, keepdims=True
        )
        total = channel_row(low, high, taps - 1, tile) * dconv
        for k in range(taps - 1):
            behind = taps - 1 - k
            kept = jnp.where(usable[k], dconv, 0.0)
            small_ref[owner, k : k + 1, at : at + LANES] = jnp.sum(
                kept * pltpu.roll(xbc, behind, 0), axis=0, keepdims=True
            )
            total = total + channel_row(low, high, k, tile) * pltpu.roll(kept, rows - behind, 0)
        rest_ref[owner, :, at : at + LANES] = total.astype(jnp.bfloat16)

    keys_act, keys_slope = act_of(tiles - 2)
    queries_act, queries_slope = act_of(tiles - 1)
    keys, queries = keys_act.astype(jnp.bfloat16), queries_act.astype(jnp.bfloat16)
    inner = lax.dot_general(
        queries, keys, (((1,), (1,)), ((), ())), preferred_element_type=jnp.float32
    )
    dinner = jnp.zeros((rows, rows), jnp.float32)
    dstep_rows = []
    dcum = jnp.zeros((rows, heads), jnp.float32)
    skip_grad = jnp.zeros((1, heads), jnp.float32)
    head_lane = lax.broadcasted_iota(jnp.int32, (1, heads), 1)
    for pair in range(pairs):
        act, slope = act_of(pair)
        dmixed = dmixed_ref[:, cut(pair)]
        dscan = dmixed.astype(jnp.bfloat16)
        operand = pair_operand(act.astype(jnp.bfloat16), lane)
        dmixing = lax.dot_general(
            dscan, operand, (((1,), (1,)), ((), ())), preferred_element_type=jnp.float32
        )
        direct = jnp.sum(dmixed * act, axis=0, keepdims=True)
        mixing = []
        for j in range(2):
            h = 2 * pair + j
            spread = jnp.where(mask, cum[:, h : h + 1] - cum_t[h : h + 1, :], FAR)
            decays = jnp.exp(spread)
            step_row = step_t[h : h + 1, :]
            weight = inner * decays
            mixing.append((weight * step_row).astype(jnp.bfloat16))
            grad = dmixing[:, j * rows : (j + 1) * rows]
            dinner = dinner + grad * decays * step_row
            term = grad * weight
            dstep_rows.append(jnp.sum(term, axis=0, keepdims=True))
            dcum = dcum + jnp.where(
                head_lane == h, jnp.sum(term * step_row, axis=1, keepdims=True), 0.0
            )
            in_head = (lane < LANES // 2) if j == 0 else (lane >= LANES // 2)
            skip_grad = skip_grad + jnp.where(
                head_lane == h,
                jnp.sum(jnp.where(in_head, direct, 0.0), axis=1, keepdims=True),
                0.0,
            )
        dinput = lax.dot_general(
            jnp.concatenate(mixing, axis=1),
            dscan,
            (((0,), (0,)), ((), ())),
            preferred_element_type=jnp.float32,
        )
        gain = jnp.where(
            lane < LANES // 2, skip[:, 2 * pair : 2 * pair + 1], skip[:, 2 * pair + 1 : 2 * pair + 2]
        )
        dact = jnp.where(lane < LANES // 2, dinput[:rows], dinput[rows:]) + gain * dmixed
        finish_tile(pair, dact * slope)
    dinner_low = dinner.astype(jnp.bfloat16)
    dqueries = jnp.dot(dinner_low, keys, preferred_element_type=jnp.float32)
    dkeys = lax.dot_general(
        dinner_low, queries, (((0,), (0,)), ((), ())), preferred_element_type=jnp.float32
    )
    finish_tile(tiles - 2, dkeys * keys_slope)
    finish_tile(tiles - 1, dqueries * queries_slope)
    dstep_t = jnp.concatenate(dstep_rows, axis=0)
    dstep = dstep_t.T
    dcum = dcum - step * dstep
    upper = jnp.where(
        lax.broadcasted_iota(jnp.int32, (rows, rows), 1)
        >= lax.broadcasted_iota(jnp.int32, (rows, rows), 0),
        1.0,
        0.0,
    ).astype(jnp.float32)
    drate = exact_dot(upper, dcum)
    speed = jnp.exp(decay)
    draw = (dstep - drate * speed) * rate_sigmoid
    tail = jnp.concatenate([draw, jnp.zeros((rows, LANES - heads), jnp.float32)], axis=1)
    for side in range(2):
        rest_ref[side, :, channels // 2 :] = tail.astype(jnp.bfloat16)
    bias_grad = jnp.sum(draw, axis=0, keepdims=True)
    decay_grad = jnp.sum(-drate * step * speed, axis=0, keepdims=True)
    half_inner = pairs * LANES // 2
    half_heads = heads // 2
    for owner in range(2):
        small_ref[owner, 5:6, 0:half_inner] = gain_grad_ref[
            :, owner * half_inner : (owner + 1) * half_inner
        ]
        for place, item in enumerate((bias_grad, decay_grad, skip_grad)):
            at = place * LANES
            small_ref[owner, 6:7, at : at + half_heads] = item[
                :, owner * half_heads : (owner + 1) * half_heads
            ]
    core, place = core_place(), owner_place()
    keep_ref[...] = rest_ref[core]
    send_ref[...] = rest_ref[1 - core]
    small_keep_ref[...] = small_ref[place]
    small_send_ref[...] = small_ref[1 - place]


def whole(shape, dtype):
    return jax.ShapeDtypeStruct(shape, dtype)


def call(body, out_shape, operands, scratch=(), lens=None):
    vmem = pl.BlockSpec(memory_space=pltpu.VMEM)
    in_specs = [vmem for _ in operands]
    if lens is not None:
        operands = (lens, *operands)
        in_specs = [pl.BlockSpec(memory_space=pltpu.SMEM), *in_specs]
    return pl.pallas_call(
        body,
        out_shape=out_shape,
        in_specs=in_specs,
        out_specs=[vmem for _ in out_shape],
        scratch_shapes=[pltpu.VMEM(item.shape, item.dtype) for item in scratch],
        compiler_params=pltpu.CompilerParams(vmem_limit_bytes=40 << 20),
        name=body.__name__,
        cost_estimate=pl.CostEstimate(flops=1, bytes_accessed=1, transcendentals=0),
    )(*operands)


def unit_rows(tokens):
    values = tokens.astype(jnp.float32)
    return lax.rsqrt(jnp.mean(values * values, axis=-1, keepdims=True) + EPSILON)


def lanes_product(left, right):
    return lax.dot_general(
        left, right, (((1,), (1,)), ((), ())), preferred_element_type=jnp.float32
    )


def rows_product(left, right):
    return lax.dot_general(
        left, right, (((0,), (0,)), ((), ())), preferred_element_type=jnp.float32
    )


def lane_half(size):
    return pl.ds(pl.multiple_of(owner_place() * size, LANES), size)


def half_means(tokens_ref, size):
    return tokens_ref[:, lane_half(size)].astype(jnp.float32) * unit_rows(tokens_ref[...])


def norm_body(first_ref, second_ref, gain_ref, out_first_ref, out_second_ref):
    for tokens_ref, out_ref in ((first_ref, out_first_ref), (second_ref, out_second_ref)):
        means = half_means(tokens_ref, out_ref.shape[1])
        out_ref[...] = (means * gain_ref[...]).astype(jnp.bfloat16)


def project_rest(normed, weight_ref, rest_ref, inner_width):
    rest_width = weight_ref.shape[0] - inner_width
    whole_tiles = rest_width // LANES * LANES
    rest_ref[:, :whole_tiles] = lanes_product(
        normed, weight_ref[inner_width : inner_width + whole_tiles, :]
    ).astype(rest_ref.dtype)
    tail = lanes_product(normed, weight_ref[inner_width + whole_tiles :, :])
    blank = jnp.zeros((tail.shape[0], LANES - tail.shape[1]), jnp.float32)
    rest_ref[:, whole_tiles:] = jnp.concatenate([tail, blank], axis=1).astype(rest_ref.dtype)


def project_own_body(tokens_ref, cotangent_ref, gain_ref, weight_ref, out_weight_ref, normed_ref, rest_ref, gate_ref, q_ref):
    inner_width = gate_ref.shape[1]
    normed = (half_means(tokens_ref, normed_ref.shape[1]) * gain_ref[...]).astype(jnp.bfloat16)
    normed_ref[...] = normed
    project_rest(normed, weight_ref, rest_ref, inner_width)
    gate_ref[...] = lanes_product(normed, weight_ref[:inner_width, :])
    q_ref[...] = lanes_product(cotangent_ref[...], out_weight_ref[...])


def project_far_body(inner_width, tokens_ref, gain_ref, weight_ref, normed_ref, wide_ref, rest_ref):
    normed = (half_means(tokens_ref, normed_ref.shape[1]) * gain_ref[...]).astype(jnp.bfloat16)
    normed_ref[...] = normed
    wide = wide_ref.shape[1]
    wide_ref[...] = lanes_product(
        normed, weight_ref[inner_width : inner_width + wide, :]
    ).astype(wide_ref.dtype)
    project_rest(normed, weight_ref, rest_ref, inner_width + wide)


def gate_far_body(normed_ref, cotangent_ref, weight_ref, out_weight_ref, send_ref):
    inner_width = send_ref.shape[1] - out_weight_ref.shape[0]
    send_ref[:, :inner_width] = lanes_product(
        normed_ref[...], weight_ref[:inner_width, :]
    ).astype(send_ref.dtype)
    send_ref[:, inner_width:] = lanes_product(
        cotangent_ref[...], out_weight_ref[...]
    ).astype(send_ref.dtype)


def branch_body(keep_ref, got_ref, weight_ref, own_ref, send_ref):
    send_ref[...] = jnp.dot(
        got_ref[: send_ref.shape[0], :], weight_ref[...], preferred_element_type=jnp.float32
    ).astype(send_ref.dtype)
    own_ref[...] = jnp.dot(keep_ref[...], weight_ref[...], preferred_element_type=jnp.float32)


def input_grad_body(*refs):
    tokens, gates, rests = refs[0:4], refs[4:8], refs[8:12]
    gain_ref, weight_ref = refs[12:14]
    rows = tokens[0].shape[0]
    gate_starts = (0, rows, 0, 0)
    own_ref, far_ref, sib_ref, gain_grad_ref = refs[14:18]
    outs = (
        own_ref,
        far_ref.at[0:rows],
        sib_ref,
        far_ref.at[rows:],
    )
    core = core_place()
    half_inner = gates[0].shape[1]
    half_channels = rests[0].shape[1] - LANES
    tail = weight_ref.shape[0] - 2 * (half_inner + half_channels)
    gate_rows = pl.ds(pl.multiple_of(core * half_inner, LANES), half_inner)
    rest_rows = pl.ds(
        pl.multiple_of(2 * half_inner + core * half_channels, LANES), half_channels
    )
    gate_weight = weight_ref[gate_rows, :]
    rest_weight = weight_ref[rest_rows, :]
    tail_weight = weight_ref[2 * (half_inner + half_channels) :, :]
    gain = gain_ref[...]
    gain_grad = jnp.zeros_like(gain)
    for tokens_ref, gate_ref, at, rest_ref, out_ref in zip(
        tokens, gates, gate_starts, rests, outs
    ):
        dnormed = jnp.dot(
            gate_ref[at : at + rows, :], gate_weight, preferred_element_type=jnp.float32
        )
        dnormed = dnormed + jnp.dot(
            rest_ref[:, :half_channels], rest_weight, preferred_element_type=jnp.float32
        )
        dtail = jnp.dot(
            rest_ref[:, half_channels : half_channels + tail],
            tail_weight,
            preferred_element_type=jnp.float32,
        )
        dnormed = dnormed + jnp.where(core == 0, dtail, 0.0)
        means = half_means(tokens_ref, gain.shape[1])
        gain_grad = gain_grad + jnp.sum(dnormed * means, axis=0, keepdims=True)
        out_ref[...] = (dnormed * gain).astype(out_ref.dtype)
    gain_grad_ref[...] = gain_grad


def tokens_grad_body(tokens_ref, cotangent_ref, own_ref, far_ref, sib_ref, out_ref):
    rows, half = own_ref.shape
    first = owner_place() == 0
    inverse = unit_rows(tokens_ref[...])
    own = own_ref[...] + sib_ref[:rows].astype(jnp.float32)
    far = far_ref[:rows].astype(jnp.float32) + sib_ref[rows:].astype(jnp.float32)
    parts = []
    cross = jnp.zeros_like(inverse)
    for side in range(2):
        cut = slice(side * half, (side + 1) * half)
        dmeans = jnp.where(first == (side == 0), own, far)
        means = tokens_ref[:, cut].astype(jnp.float32) * inverse
        cross = cross + jnp.sum(dmeans * means, axis=1, keepdims=True)
        parts.append((cut, dmeans, means))
    for cut, dmeans, means in parts:
        out_ref[:, cut] = cotangent_ref[:, cut].astype(jnp.float32) + inverse * (
            dmeans - means * (cross / (2 * half))
        )


def left_lanes(lefts, starts, rows, at, size):
    cut = pl.ds(pl.multiple_of(at, LANES), size)
    return jnp.concatenate(
        [ref[first : first + rows, cut] for ref, first in zip(lefts, starts)], axis=0
    )


def block_grad_body(part, starts, right_half, *refs):
    lefts, rights, (send_ref, keep_ref) = refs[0:4], refs[4:8], refs[8:]
    rows = rights[0].shape[0]
    width = send_ref.shape[1]
    lanes = slice(None)
    if right_half:
        lanes = pl.ds(pl.multiple_of(core_place() * width, LANES), width)
    right = jnp.concatenate([ref[:, lanes] for ref in rights], axis=0)
    at, size, order = part
    bit = chip_bit(order[0])
    half = size // 2
    for ref, side in ((send_ref, 1 - bit), (keep_ref, bit)):
        left = left_lanes(lefts, starts, rows, at + side * half, half)
        ref[...] = rows_product(left, right).astype(ref.dtype)


SMALL_ROWS = 16


def block_small_body(part, starts, *refs):
    lefts, rights, (mine_ref, far_ref, send_ref, keep_ref) = refs[0:4], refs[4:8], refs[8:]
    rows = rights[0].shape[0]
    width = send_ref.shape[1]
    right = jnp.concatenate([ref[...] for ref in rights], axis=0)
    total = mine_ref[...] + far_ref[...]
    count, wide = total.shape
    blank = jnp.zeros((SMALL_ROWS - count, width), jnp.float32)
    smalls = []
    for quarter in range(4):
        piece = total[:, quarter * width : min(wide, (quarter + 1) * width)]
        if piece.shape[1] < width:
            rest = jnp.zeros((count, width - piece.shape[1]), jnp.float32)
            piece = jnp.concatenate([piece, rest], axis=1) if piece.shape[1] else rest
        smalls.append(jnp.concatenate([piece, blank], axis=0))
    heads = total[6:7, :width]
    high = heads.astype(jnp.bfloat16).astype(jnp.float32)
    row = lax.broadcasted_iota(jnp.int32, (SMALL_ROWS, 1), 0)
    chip = lax.div(lax.axis_index("replica"), 2)
    smalls[3] = jnp.where(row == chip, high, 0.0) + jnp.where(
        row == chip + SMALL_ROWS // 2, heads - high, 0.0
    )
    at, size, order = part
    bit = chip_bit(order[0])
    quarter = size // 4
    for ref, side in ((send_ref, 1 - bit), (keep_ref, bit)):
        left = left_lanes(lefts, starts, rows, at + side * 2 * quarter, 2 * quarter)
        block = rows_product(left, right)
        for q in range(2):
            base = q * (quarter + SMALL_ROWS)
            ref[base : base + quarter, :] = block[q * quarter : (q + 1) * quarter].astype(
                ref.dtype
            )
            ref[base + quarter : base + quarter + SMALL_ROWS, :] = jnp.where(
                side == 0, smalls[q], smalls[2 + q]
            ).astype(ref.dtype)


def block_norm_body(part, starts, norm_row, *refs):
    lefts, rights, (norm_ref, send_ref, keep_ref) = refs[0:4], refs[4:8], refs[8:]
    rows = rights[0].shape[0]
    right = jnp.concatenate([ref[...] for ref in rights], axis=0)
    at, size, order = part
    bit = chip_bit(order[0])
    half = size // 2
    row = lax.broadcasted_iota(jnp.int32, (half, 1), 0)
    for ref, side in ((send_ref, 1 - bit), (keep_ref, bit)):
        left = left_lanes(lefts, starts, rows, at + side * half, half)
        block = rows_product(left, right)
        here = (row + (at + side * half)) == norm_row
        ref[...] = jnp.where(here, norm_ref[...], block).astype(ref.dtype)


def halve_body(bit, keep_ref, got_ref, send_ref, out_ref):
    rows = send_ref.shape[0]
    bit = chip_bit(bit)
    for ref, side in ((send_ref, 1 - bit), (out_ref, bit)):
        cut = pl.ds(pl.multiple_of(side * rows, 16), rows)
        ref[...] = (keep_ref[cut, :] + got_ref[cut, :].astype(jnp.float32)).astype(ref.dtype)


def add_body(keep_ref, got_ref, out_ref):
    out_ref[...] = (
        keep_ref[...].astype(jnp.float32) + got_ref[...].astype(jnp.float32)
    ).astype(out_ref.dtype)


def after(value, *earlier):
    return lax.optimization_barrier((value, *earlier))[0]


class PartSum:
    def __init__(self, order, make_block, early=False):
        self.order, self.make_block, self.early = order, make_block, early
        self.steps = 0
        self.pieces = None

    def advance(self, token):
        f32, low = jnp.float32, jnp.bfloat16
        step = self.steps
        self.steps += 1
        if step == 0:
            send, self.keep = self.make_block(token)
            bit = self.order[0]
        elif step == 1:
            keep = after(self.keep, token)
            shape = (keep.shape[0] // 2, keep.shape[1])

            def halve(*refs):
                halve_body(self.order[1], *refs)

            send, self.keep = call(
                halve, [whole(shape, low), whole(shape, f32)], (keep, self.got)
            )
            bit = self.order[1]
        elif step < 4:
            keep = after(self.keep, token)
            (send,) = call(add_body, [whole(keep.shape, low)], (keep, self.got))
            self.keep = send
            bit = self.order[2] if step == 2 else self.order[1]
        elif step == 4:
            send = jnp.concatenate([after(self.keep, token), self.got], axis=0)
            self.keep = send
            if self.early:
                self.sibling = swap_core(send)
            bit = self.order[0]
        else:
            got = after(self.got, token)
            sibling = after(self.sibling, got) if self.early else swap_core(self.keep)
            self.pieces = [self.keep, got, sibling, swap_core(got)]
            return got
        self.got = swap_chip(send, bit)
        return send


def part_quarters(order, pieces):
    first, second = chip_bit(order[0]), chip_bit(order[1])
    for which in range(2):
        side = first if which == 0 else 1 - first
        mine, sibling = pieces[which], pieces[2 + which]
        size = mine.shape[0] // 2
        for p in range(2):
            quarter = 2 * side + (second if p == 0 else 1 - second)
            yield quarter, mine, sibling, p * size


def write_part(out_ref, base, part, pieces, other):
    at, size, order = part
    size = size // 4
    for quarter, mine, sibling, row in part_quarters(order, pieces):
        rows = slice(row, row + size)
        value = jnp.where(other, sibling[rows, :], mine[rows, :]).astype(jnp.float32)
        out_ref[pl.ds(pl.multiple_of(base + at + quarter * size, 8), size), :] = value


def in_weight_body(gate_part, rest_parts, *refs):
    (out_ref, norm_ref), refs = refs[-2:], refs[:-2]
    gates, rests = refs[0:4], refs[4:]
    core = core_place()
    half_inner = gate_part[1]
    last_at, last_size, last_order = rest_parts[1]
    half_channels = last_at + last_size - LANES
    tail_at = 2 * (half_inner + half_channels)
    tail = out_ref.shape[0] - tail_at
    for side in range(2):
        other = core != side
        base = 2 * half_inner + side * half_channels
        write_part(out_ref, side * half_inner, gate_part, gates, other)
        write_part(out_ref, base, rest_parts[0], rests[0:4], other)
        size = last_size // 4
        for quarter, mine, sibling, row in part_quarters(last_order, rests[4:8]):
            rows = slice(row, row + size)
            value = jnp.where(other, sibling[rows, :], mine[rows, :]).astype(jnp.float32)

            @pl.when(quarter < 3)
            def _():
                place = base + last_at + quarter * size
                out_ref[pl.ds(pl.multiple_of(place, 8), size), :] = value

            if side == 0:

                @pl.when(quarter == 3)
                def _():
                    out_ref[tail_at:, :] = value[:tail]
                    both = mine[rows, :].astype(jnp.float32) + sibling[rows, :].astype(
                        jnp.float32
                    )
                    norm_ref[...] = both[tail : tail + norm_ref.shape[0]]


def small_body(order, *refs):
    pieces, out_ref = refs[:-1], refs[-1]
    count, wide = out_ref.shape[0] // 2, out_ref.shape[1]
    width = pieces[0].shape[1]
    for quarter, mine, sibling, row in part_quarters(order, pieces):
        size = mine.shape[0] // 2
        rows = slice(row + size - SMALL_ROWS, row + size)
        both = mine[rows, :].astype(jnp.float32) + sibling[rows, :].astype(jnp.float32)
        for place in range((wide + width - 1) // width):
            lanes = slice(place * width, min(wide, (place + 1) * width))

            @pl.when(quarter == place)
            def _():
                out_ref[:count, lanes] = both[:count, : lanes.stop - lanes.start]

        @pl.when(quarter == 3)
        def _():
            out_ref[count : count + 1, :width] = jnp.sum(both, axis=0, keepdims=True)


def out_weight_body(part, blocks, *refs):
    side = lax.div(pl.program_id(0), blocks)
    write_part(refs[-1], 0, part, refs[:-1], core_place() != side)


def assemble(body, outs, pieces, block):
    blocks = pieces[0].shape[1] // block
    return pl.pallas_call(
        body,
        grid=(outs[0].shape[1] // block,),
        out_shape=outs,
        in_specs=[
            pl.BlockSpec((item.shape[0], block), lambda i: (0, lax.rem(i, blocks)))
            for item in pieces
        ],
        out_specs=[pl.BlockSpec((out.shape[0], block), lambda i: (0, i)) for out in outs],
        compiler_params=pltpu.CompilerParams(vmem_limit_bytes=48 << 20),
        name=body.__name__,
        cost_estimate=pl.CostEstimate(flops=1, bytes_accessed=1, transcendentals=0),
    )(*pieces)


def swap(value, replica_bits, fsdp_bits):
    replicas, owners = lax.axis_size("replica"), lax.axis_size("fsdp")
    pairs = [
        (r * owners + f, (r ^ replica_bits) * owners + (f ^ fsdp_bits))
        for r in range(replicas)
        for f in range(owners)
    ]
    return lax.ppermute(value, AXES, pairs)


def swap_owner(value):
    return swap(value, 0, 1)


def swap_core(value):
    return swap(value, 1, 0)


def swap_chip(value, bit):
    return swap(value, 2 << bit, 0)


def join(place, own, other, axis):
    return jnp.where(
        place == 0,
        jnp.concatenate([own, other], axis=axis),
        jnp.concatenate([other, own], axis=axis),
    )


def part_of(value, place, parts, axis):
    size = value.shape[axis] // parts
    return lax.dynamic_slice_in_dim(value, place * size, size, axis)


def total_over_chips(block):
    chip = lax.axis_index("replica") // 2
    bits = range((lax.axis_size("replica") // 2).bit_length() - 1)
    rows, cols = block.shape
    kept = block.reshape((2,) * len(bits) + (rows >> len(bits), cols))
    for bit in bits:
        mine = (chip >> bit) & 1
        sent = lax.dynamic_index_in_dim(kept, 1 - mine, 0, keepdims=False).astype(jnp.bfloat16)
        got = swap_chip(sent, bit)
        kept = lax.dynamic_index_in_dim(kept, mine, 0, keepdims=False) + got.astype(jnp.float32)
    chunk = kept.astype(jnp.bfloat16)
    for bit in reversed(bits):
        chunk = join((chip >> bit) & 1, chunk, swap_chip(chunk, bit), 0)
    return chunk


def per_device(
    tokens,
    seq_lens,
    norm_gain,
    in_weight,
    conv_weight,
    conv_bias,
    step_bias,
    decay_log,
    skip_gain,
    out_gain,
    out_weight,
    cotangent,
):
    f32, low = jnp.float32, jnp.bfloat16
    owner = lax.axis_index("fsdp")
    core = lax.axis_index("replica") % 2
    chips = lax.axis_size("replica") // 2
    rows, width = tokens.shape
    half_width = width // 2
    half_inner = out_weight.shape[0]
    inner_width = 2 * half_inner
    half_channels = conv_bias.shape[0]
    channels = 2 * half_channels
    half_heads = skip_gain.shape[0]
    heads = 2 * half_heads
    weight = in_weight.T
    gain = norm_gain.astype(f32).reshape(1, -1)

    tokens_far = swap_owner(tokens)
    cotangent_far = swap_owner(cotangent)
    def project_far(*refs):
        project_far_body(inner_width, *refs)

    normed_far, wide_send, rest_send = call(
        project_far,
        [
            whole((rows, half_width), low),
            whole((rows, inner_width), low),
            whole((rows, channels + LANES - inner_width), f32),
        ],
        (after(tokens_far, cotangent_far), gain, weight),
    )
    rest_got, wide_got = swap_owner(rest_send), swap_owner(wide_send)
    normed_own, rest_own, gate_own, q_own = call(
        project_own_body,
        [
            whole((rows, half_width), low),
            whole((rows, channels + LANES), f32),
            whole((rows, inner_width), f32),
            whole((rows, half_inner), f32),
        ],
        (after(tokens, rest_send), cotangent, gain, weight, out_weight),
    )
    (gate_send,) = call(
        gate_far_body,
        [whole((rows, inner_width + half_inner), low)],
        (normed_far, cotangent_far, weight, out_weight),
    )
    conv_weight, conv_bias, step_bias, decay_log, skip_gain, out_gain = after(
        (conv_weight, conv_bias, step_bias, decay_log, skip_gain, out_gain), gate_send
    )

    def row(item):
        item = item.astype(f32).reshape(-1, item.shape[-1])
        return jnp.pad(item, ((0, 0), (0, half_channels - item.shape[-1])))

    def head_row(item):
        item = item.astype(f32)
        there = jnp.zeros_like(item)
        placed = jnp.where(
            owner == 0, jnp.concatenate([item, there]), jnp.concatenate([there, item])
        )
        return jnp.pad(placed, (0, LANES - heads))

    head_rows = jnp.concatenate([head_row(step_bias), head_row(decay_log), head_row(skip_gain)])
    mine = jnp.concatenate(
        [
            row(conv_weight),
            row(conv_bias),
            row(out_gain),
            row(head_rows),
            jnp.zeros((1, half_channels), f32),
        ],
        axis=0,
    )
    peer = swap_owner(mine)
    gate_got = swap_owner(after(gate_send, rest_got, wide_got, peer))
    tokens_sib, tokens_far_sib = swap_core(tokens), swap_core(tokens_far)
    cotangent_sib, cotangent_far_sib = swap_core(cotangent), swap_core(cotangent_far)
    normed_sib, normed_far_sib = call(
        norm_body,
        [whole((rows, half_width), low)] * 2,
        (tokens_sib, tokens_far_sib, gain),
    )

    xbc, conv, mixed, rates = call(
        forward_body,
        [
            whole((rows, channels), f32),
            whole((rows, channels), f32),
            whole((rows, inner_width), f32),
            whole((3, rows, heads), f32),
        ],
        (rest_own, wide_got, rest_got, mine, peer),
        lens=seq_lens,
    )
    out_keep, out_send, inverse = call(
        gate_out_body,
        [*[whole((rows, half_inner), low)] * 2, whole((rows, 1), f32)],
        (mixed, gate_own, gate_got, mine, peer),
        scratch=[whole((2, rows, half_inner), low)],
    )
    out_far, out_sib = swap_owner(out_send), swap_core(out_keep)
    dgate, dgate_send, far_send, dmixed, gain_grad = call(
        gate_grad_body,
        [
            *[whole((rows, half_inner), low)] * 2,
            whole((2 * rows, half_inner), low),
            whole((rows, inner_width), f32),
            whole((1, inner_width), f32),
        ],
        (
            after(mixed, normed_sib, normed_far_sib, cotangent_sib, cotangent_far_sib),
            gate_own,
            q_own,
            gate_got,
            mine,
            peer,
            inverse,
        ),
        scratch=[whole((2, rows, half_inner), low)],
    )
    far, dgate_sib = swap_owner(far_send), swap_core(dgate_send)
    drest, drest_send, small_keep, small_send = call(
        backward_body,
        [
            *[whole((rows, half_channels + LANES), low)] * 2,
            *[whole((8, half_channels), f32)] * 2,
        ],
        (dmixed, xbc, conv, rates, mine, peer, gain_grad),
        scratch=[
            whole((2, rows, half_channels + LANES), low),
            whole((2, 8, half_channels), f32),
        ],
        lens=seq_lens,
    )
    small_far = swap_owner(small_send)
    out_far_sib = swap_core(after(out_far, drest))
    drest_far, drest_far_sib = swap_owner(drest), swap(drest_send, 1, 1)
    drest_sib = swap_core(drest_send)

    tokens_all = (tokens, tokens_far, tokens_sib, tokens_far_sib)
    normed_all = (normed_own, normed_far, normed_sib, normed_far_sib)
    cotangent_all = (cotangent, cotangent_far, cotangent_sib, cotangent_far_sib)
    drest_all = (drest, drest_far, drest_sib, drest_far_sib)
    out_all = (out_keep, out_far, out_sib, out_far_sib)
    out_starts, gate_starts, rest_starts = (0,) * 4, (0, rows, 0, 0), (0,) * 4
    state = {}
    if chips == 8:
        cut = (half_channels + LANES) * 3 // 5 // LANES * LANES
        out_part = (0, half_inner, (0, 1, 2))
        gate_part = (0, half_inner, (1, 0, 2))
        rest_parts = ((0, cut, (0, 1, 2)), (cut, half_channels + LANES - cut, (1, 0, 2)))
        norm_row = half_channels + heads

        def maker(body, part, given, size, extra=(), early=False):
            lefts, starts, rights = given

            def make(token):
                def block_grad(*refs):
                    body(part, starts, *refs)

                if lefts is None:
                    state["far_sib"] = swap_core(after(far, token))
                    sources = (dgate, far, dgate_sib, state["far_sib"])
                else:
                    sources = lefts
                tied = sources if token is None else (after(sources[0], token), *sources[1:])
                more = [item() for item in extra]
                sizes = [whole((size // 2, half_width), dtype) for dtype in (low, f32)]
                return call(block_grad, sizes, (*tied, *rights, *more))

            return PartSum(part[2], make, early)

        def out_block(part, starts, *refs):
            block_grad_body(part, starts, True, *refs)

        def rest_block(part, starts, *refs):
            block_grad_body(part, starts, False, *refs)

        def norm_block(part, starts, *refs):
            block_norm_body(part, starts, norm_row, *refs)

        gate_sources = (None, gate_starts, normed_all)
        rest_sources = (drest_all, rest_starts, normed_all)
        sums = (
            maker(out_block, out_part, (out_all, out_starts, cotangent_all), half_inner),
            maker(
                block_small_body,
                gate_part,
                gate_sources,
                half_inner + 4 * SMALL_ROWS,
                (lambda: small_keep, lambda: small_far),
            ),
            maker(rest_block, rest_parts[0], rest_sources, rest_parts[0][1], early=True),
            maker(
                norm_block,
                rest_parts[1],
                rest_sources,
                rest_parts[1][1],
                (lambda: state["norm_grad"],),
                early=True,
            ),
        )
        token = None
    else:
        token = drest

        def total_of(left, starts, right):
            left = [item[first : first + rows] for item, first in zip(left, starts)]
            return total_over_chips(
                rows_product(jnp.concatenate(left, axis=0), jnp.concatenate(right, axis=0))
            )

        out_total = total_of(
            out_all,
            out_starts,
            [part_of(item, core, 2, 1) for item in cotangent_all],
        )
        state["far_sib"] = swap_core(far)
        dgate_all = (dgate, far, dgate_sib, state["far_sib"])
        gate_total = total_of(dgate_all, gate_starts, normed_all)
        rest_total = total_of(drest_all, rest_starts, normed_all)
        rest_sib = swap_core(rest_total)
        out_weight_grad = join(core, out_total, swap_core(out_total), 1).astype(f32)
        in_weight_grad = (
            jnp.concatenate(
                [
                    join(core, gate_total, swap_core(gate_total), 0),
                    join(core, rest_total[:half_channels], rest_sib[:half_channels], 0),
                    rest_total[half_channels : half_channels + heads],
                ],
                axis=0,
            )
            .astype(f32)
            .T
        )

    def out_projection(token):
        own, send = call(
            branch_body,
            [whole((rows, width), f32), whole((rows, width), low)],
            (after(out_keep, token), out_far, out_weight),
        )
        state["branch"] = (own, swap_owner(send))
        return send

    def block_sum(token):
        own, far = state["branch"]
        state["block_out"] = (
            tokens.astype(f32) + after(own, token) + far.astype(f32)
        ).astype(low)
        return state["block_out"]

    def input_norm(token):
        state["dmeans"] = call(
            input_grad_body,
            [
                whole((rows, half_width), f32),
                whole((2 * rows, half_width), low),
                whole((rows, half_width), low),
                whole((1, half_width), f32),
            ],
            (
                *tokens_all,
                after(dgate, token),
                far,
                dgate_sib,
                state["far_sib"],
                *drest_all,
                gain,
                weight,
            ),
        )
        state["norm_grad"] = state["dmeans"][3]
        return state["norm_grad"]

    def means_far(token):
        send = after(state["dmeans"][1], token)
        state["means_far"] = swap_owner(send)
        return send

    def means_sib(token):
        far = after(state["means_far"], token)
        send = jnp.concatenate([state["dmeans"][2], far[rows:]], axis=0)
        state["means_sib"] = swap_core(send)
        return send

    def tokens_grad(token):
        (state["grad_tokens"],) = call(
            tokens_grad_body,
            [whole((rows, width), f32)],
            (
                tokens,
                cotangent,
                after(state["dmeans"][0], token),
                state["means_far"],
                state["means_sib"],
            ),
        )
        return state["grad_tokens"]

    def small_results(total, row):
        return (
            total[0:4],
            total[4],
            total[row, 0:half_heads],
            total[row, LANES : LANES + half_heads],
            total[row, 2 * LANES : 2 * LANES + half_heads],
            total[5, :half_inner],
        )

    def small_assembly(token):
        def small_rows(*refs):
            small_body(gate_part[2], *refs)

        pieces = sums[1].pieces
        (total,) = call(
            small_rows,
            [whole((16, half_channels), f32)],
            (after(pieces[0], token), *pieces[1:]),
        )
        state["smalls"] = small_results(total, 8)
        return state["smalls"][1]

    def out_assembly(token):
        def out_weight_lanes(*refs):
            out_weight_body(out_part, 2, *refs)

        pieces = sums[0].pieces
        (state["out_weight"],) = assemble(
            out_weight_lanes,
            [whole(out_weight.shape, f32)],
            [after(pieces[0], token), *pieces[1:]],
            half_width // 2,
        )
        return state["out_weight"]

    if chips == 8:
        steps = {
            "n": input_norm,
            "x": means_far,
            "k": means_sib,
            "t": tokens_grad,
            "b": out_projection,
            "p": block_sum,
            "s": small_assembly,
            "o": out_assembly,
        }
        for mark in ORDER:
            step = steps[mark] if mark in steps else sums[int(mark)].advance
            token = step(token)

        def in_weight_rows(*refs):
            in_weight_body(gate_part, rest_parts, *refs)

        pieces = [piece for part in sums[1:] for piece in part.pieces]
        in_weight_rows_grad, norm_rows = assemble(
            in_weight_rows,
            [whole(weight.shape, f32), whole((8, half_width), f32)],
            [after(pieces[0], token), *pieces[1:]],
            LANES,
        )
        in_weight_grad = in_weight_rows_grad.T
        out_weight_grad = state["out_weight"]
        norm_gain_grad = norm_rows[0]
    else:
        for step in (out_projection, block_sum, input_norm, means_far, means_sib, tokens_grad):
            step(token)
        total = jnp.concatenate(
            [(small_keep + small_far)[:7], row(state["norm_grad"])], axis=0
        )
        bits = 1
        while bits < 2 * chips:
            total = total + swap(total, bits, 0)
            bits *= 2
        norm_gain_grad = total[7, :half_width]
        state["smalls"] = small_results(total, 6)
    return (
        state["block_out"],
        state["grad_tokens"],
        norm_gain_grad,
        in_weight_grad,
        *state["smalls"],
        out_weight_grad,
    )


def solution(mesh):
    placed = (
        P(("replica", "fsdp"), None),
        P(("replica", "fsdp"), None),
        P("fsdp"),
        P("fsdp", None),
        P(None, "fsdp"),
        P("fsdp"),
        P("fsdp"),
        P("fsdp"),
        P("fsdp"),
        P("fsdp"),
        P("fsdp", None),
        P(("replica", "fsdp"), None),
    )
    return jax.shard_map(
        per_device,
        mesh=mesh,
        in_specs=placed,
        out_specs=(
            P(("replica", "fsdp"), None),
            P(("replica", "fsdp"), None),
            P("fsdp"),
            P("fsdp", None),
            P(None, "fsdp"),
            P("fsdp"),
            P("fsdp"),
            P("fsdp"),
            P("fsdp"),
            P("fsdp"),
            P("fsdp", None),
        ),
        check_vma=False,
    )
```

```python
import jax
import jax.numpy as jnp
from jax import lax
from jax.experimental import pallas as pl
from jax.experimental.pallas import tpu as pltpu
from jax.sharding import PartitionSpec as P

EPSILON = 1e-05
AXES = ("replica", "fsdp")
LANES = 128
FAR = -1e30
ORDER = "01012n3x01k2301t2301b2301p23os23"


def owner_place():
    return lax.axis_index("fsdp")


def core_place():
    return lax.rem(lax.axis_index("replica"), 2)


def chip_bit(bit):
    return lax.rem(lax.div(lax.axis_index("replica"), 2 << bit), 2)


def full_rows(mine_ref, peer_ref):
    first = owner_place() == 0
    mine, peer = mine_ref[...], peer_ref[...]
    return (jnp.where(first, mine, peer), jnp.where(first, peer, mine), mine + peer)


def row_marks(lens_ref, rows):
    end_one, end_two = lens_ref[0, 0], lens_ref[0, 0] + lens_ref[0, 1]
    position = lax.broadcasted_iota(jnp.int32, (rows, 1), 0)
    start = jnp.where(position >= end_two, end_two, jnp.where(position >= end_one, end_one, 0))
    return (position, start)


def kept_pairs(start, rows):
    key = lax.broadcasted_iota(jnp.int32, (rows, rows), 1)
    query = lax.broadcasted_iota(jnp.int32, (rows, rows), 0)
    return (key <= query) & (key >= start)


def channel_row(low, high, row, tile):
    half = low.shape[1] // LANES
    source = low if tile < half else high
    at = (tile if tile < half else tile - half) * LANES
    return source[row : row + 1, at : at + LANES]


def exact_dot(left, right):
    return jnp.dot(
        left, right, precision=lax.Precision.HIGHEST, preferred_element_type=jnp.float32
    )


def pair_operand(values, lane):
    zero = jnp.zeros_like(values)
    return jnp.concatenate(
        [jnp.where(lane < LANES // 2, values, zero), jnp.where(lane < LANES // 2, zero, values)],
        axis=0,
    )


def forward_body(lens_ref, own_ref, wide_ref, got_ref, mine_ref, peer_ref, xbc_ref, conv_ref, mixed_ref, rates_ref):
    rows, channels = conv_ref.shape
    tiles = channels // LANES
    pairs = tiles - 2
    heads = 2 * pairs
    taps = 4
    low, high, both = full_rows(mine_ref, peer_ref)
    position, start = row_marks(lens_ref, rows)
    usable = [position - (taps - 1 - k) >= start for k in range(taps)]
    lane = lax.broadcasted_iota(jnp.int32, (1, LANES), 1)
    bias = both[6:7, 0:heads]
    decay = both[6:7, LANES : LANES + heads]
    skip = both[6:7, 2 * LANES : 2 * LANES + heads]
    tail = slice(channels, channels + heads)
    wide = wide_ref.shape[1]
    rate = own_ref[:, tail] + got_ref[:, channels - wide : channels - wide + heads] + bias
    step = jnp.maximum(rate, 0.0) + jnp.log1p(jnp.exp(-jnp.abs(rate)))
    rate_sigmoid = jax.nn.sigmoid(rate)
    lower = jnp.where(
        lax.broadcasted_iota(jnp.int32, (rows, rows), 1)
        <= lax.broadcasted_iota(jnp.int32, (rows, rows), 0),
        1.0,
        0.0,
    ).astype(jnp.float32)
    cum = exact_dot(lower, step * -jnp.exp(decay))
    rates_ref[0] = step
    rates_ref[1] = cum
    rates_ref[2] = rate_sigmoid
    step_t, cum_t = step.T, cum.T
    mask = kept_pairs(start, rows)

    def active_tile(tile):
        at = tile * LANES
        if at < wide:
            far = wide_ref[:, at : at + LANES].astype(jnp.float32)
        else:
            far = got_ref[:, at - wide : at - wide + LANES]
        xbc = own_ref[:, at : at + LANES] + far
        xbc_ref[:, at : at + LANES] = xbc
        conv = channel_row(low, high, 4, tile) + channel_row(low, high, taps - 1, tile) * xbc
        for k in range(taps - 1):
            shifted = pltpu.roll(xbc, taps - 1 - k, 0)
            conv = conv + channel_row(low, high, k, tile) * jnp.where(usable[k], shifted, 0.0)
        conv_ref[:, at : at + LANES] = conv
        return conv * jax.nn.sigmoid(conv)

    keys = active_tile(tiles - 2).astype(jnp.bfloat16)
    queries = active_tile(tiles - 1).astype(jnp.bfloat16)
    inner = lax.dot_general(
        queries, keys, (((1,), (1,)), ((), ())), preferred_element_type=jnp.float32
    )
    for pair in range(pairs):
        act = active_tile(pair)
        mixing = []
        for h in (2 * pair, 2 * pair + 1):
            spread = jnp.where(mask, cum[:, h : h + 1] - cum_t[h : h + 1, :], FAR)
            mixing.append((inner * jnp.exp(spread) * step_t[h : h + 1, :]).astype(jnp.bfloat16))
        scan = jnp.dot(
            jnp.concatenate(mixing, axis=1),
            pair_operand(act.astype(jnp.bfloat16), lane),
            preferred_element_type=jnp.float32,
        )
        gain = jnp.where(
            lane < LANES // 2, skip[:, 2 * pair : 2 * pair + 1], skip[:, 2 * pair + 1 : 2 * pair + 2]
        )
        mixed_ref[:, pair * LANES : (pair + 1) * LANES] = scan + gain * act


def half_cut(tile, width, half):
    at = tile * width % half
    return slice(at, at + width)


def gate_tile(own_ref, got_ref, cut):
    gate = own_ref[:, cut] + got_ref[:, cut].astype(jnp.float32)
    return (gate, jax.nn.sigmoid(gate))


def gate_out_body(mixed_ref, own_ref, got_ref, mine_ref, peer_ref, keep_ref, send_ref, inverse_ref, out_ref):
    rows, inner_width = mixed_ref.shape
    half = inner_width // 2
    owner = owner_place()
    low, high, _ = full_rows(mine_ref, peer_ref)
    width = 2 * LANES
    cuts = [slice(at, at + width) for at in range(0, inner_width, width)]
    squares = jnp.zeros((rows, 1), jnp.float32)
    for cut in cuts:
        gate, sigmoid = gate_tile(own_ref, got_ref, cut)
        gated = mixed_ref[:, cut] * (gate * sigmoid)
        squares = squares + jnp.sum(gated * gated, axis=1, keepdims=True)
    inverse = lax.rsqrt(squares / inner_width + EPSILON)
    inverse_ref[...] = inverse
    for tile, cut in enumerate(cuts):
        gate, sigmoid = gate_tile(own_ref, got_ref, cut)
        near = half_cut(tile, width, half)
        gain = (low if cut.start < half else high)[5:6, near]
        normed = mixed_ref[:, cut] * (gate * sigmoid) * inverse
        out_ref[cut.start // half, :, near] = (normed * gain).astype(jnp.bfloat16)
    keep_ref[...] = out_ref[owner]
    send_ref[...] = out_ref[1 - owner]


def gate_grad_body(mixed_ref, own_ref, q_own_ref, got_ref, mine_ref, peer_ref, inverse_ref, keep_ref, send_ref, far_send_ref, dmixed_ref, gain_grad_ref, dgate_ref):
    rows, inner_width = mixed_ref.shape
    half = inner_width // 2
    owner, core = owner_place(), core_place()
    low, high, _ = full_rows(mine_ref, peer_ref)
    width = 2 * LANES
    cuts = [slice(at, at + width) for at in range(0, inner_width, width)]
    inverse = inverse_ref[...]

    def operands(tile, cut):
        near = half_cut(tile, width, half)
        in_low = cut.start < half
        gain = (low if in_low else high)[5:6, near]
        far = got_ref[:, inner_width + near.start : inner_width + near.stop]
        q = jnp.where((owner == 0) == in_low, q_own_ref[:, near], far.astype(jnp.float32))
        return (near, gain, q)

    cross = jnp.zeros((rows, 1), jnp.float32)
    for tile, cut in enumerate(cuts):
        _, gain, q = operands(tile, cut)
        gate, sigmoid = gate_tile(own_ref, got_ref, cut)
        cross = cross + jnp.sum(
            q * gain * (mixed_ref[:, cut] * (gate * sigmoid)), axis=1, keepdims=True
        )
    mean_cross = cross * inverse / inner_width
    for tile, cut in enumerate(cuts):
        near, gain, q = operands(tile, cut)
        gate, sigmoid = gate_tile(own_ref, got_ref, cut)
        silu = gate * sigmoid
        mixed = mixed_ref[:, cut]
        normed = mixed * silu * inverse
        gain_grad_ref[:, cut] = jnp.sum(q * normed, axis=0, keepdims=True)
        dgated = inverse * (q * gain - normed * mean_cross)
        dmixed_ref[:, cut] = dgated * silu
        dgate_ref[cut.start // half, :, near] = (
            dgated * mixed * (sigmoid * (1.0 + gate * (1.0 - sigmoid)))
        ).astype(jnp.bfloat16)
    keep_ref[...] = dgate_ref[core]
    send_ref[...] = dgate_ref[1 - core]
    far_send_ref[:rows] = dgate_ref[1 - core]
    far_send_ref[rows:] = dgate_ref[core]


def backward_body(lens_ref, dmixed_ref, xbc_ref, conv_ref, rates_ref, mine_ref, peer_ref, gain_grad_ref, keep_ref, send_ref, small_keep_ref, small_send_ref, rest_ref, small_ref):
    rows, channels = conv_ref.shape
    tiles = channels // LANES
    pairs = tiles - 2
    heads = 2 * pairs
    taps = 4
    half_tiles = tiles // 2
    small_ref[...] = jnp.zeros(small_ref.shape, jnp.float32)
    low, high, both = full_rows(mine_ref, peer_ref)
    position, start = row_marks(lens_ref, rows)
    usable = [position - (taps - 1 - k) >= start for k in range(taps)]
    lane = lax.broadcasted_iota(jnp.int32, (1, LANES), 1)
    decay = both[6:7, LANES : LANES + heads]
    skip = both[6:7, 2 * LANES : 2 * LANES + heads]
    step, cum, rate_sigmoid = rates_ref[0], rates_ref[1], rates_ref[2]
    step_t, cum_t = step.T, cum.T
    mask = kept_pairs(start, rows)

    def cut(tile):
        return slice(tile * LANES, (tile + 1) * LANES)

    def act_of(tile):
        conv = conv_ref[:, cut(tile)]
        sigmoid = jax.nn.sigmoid(conv)
        return (conv * sigmoid, sigmoid * (1.0 + conv * (1.0 - sigmoid)))

    def finish_tile(tile, dconv):
        owner, at = tile // half_tiles, tile % half_tiles * LANES
        xbc = xbc_ref[:, cut(tile)]
        small_ref[owner, 4:5, at : at + LANES] = jnp.sum(dconv, axis=0, keepdims=True)
        small_ref[owner, taps - 1 : taps, at : at + LANES] = jnp.sum(
            dconv * xbc, axis=0, keepdims=True
        )
        total = channel_row(low, high, taps - 1, tile) * dconv
        for k in range(taps - 1):
            behind = taps - 1 - k
            kept = jnp.where(usable[k], dconv, 0.0)
            small_ref[owner, k : k + 1, at : at + LANES] = jnp.sum(
                kept * pltpu.roll(xbc, behind, 0), axis=0, keepdims=True
            )
            total = total + channel_row(low, high, k, tile) * pltpu.roll(kept, rows - behind, 0)
        rest_ref[owner, :, at : at + LANES] = total.astype(jnp.bfloat16)

    keys_act, keys_slope = act_of(tiles - 2)
    queries_act, queries_slope = act_of(tiles - 1)
    keys, queries = keys_act.astype(jnp.bfloat16), queries_act.astype(jnp.bfloat16)
    inner = lax.dot_general(
        queries, keys, (((1,), (1,)), ((), ())), preferred_element_type=jnp.float32
    )
    dinner = jnp.zeros((rows, rows), jnp.float32)
    dstep_rows = []
    dcum = jnp.zeros((rows, heads), jnp.float32)
    skip_grad = jnp.zeros((1, heads), jnp.float32)
    head_lane = lax.broadcasted_iota(jnp.int32, (1, heads), 1)
    for pair in range(pairs):
        act, slope = act_of(pair)
        dmixed = dmixed_ref[:, cut(pair)]
        dscan = dmixed.astype(jnp.bfloat16)
        operand = pair_operand(act.astype(jnp.bfloat16), lane)
        dmixing = lax.dot_general(
            dscan, operand, (((1,), (1,)), ((), ())), preferred_element_type=jnp.float32
        )
        direct = jnp.sum(dmixed * act, axis=0, keepdims=True)
        mixing = []
        for j in range(2):
            h = 2 * pair + j
            spread = jnp.where(mask, cum[:, h : h + 1] - cum_t[h : h + 1, :], FAR)
            decays = jnp.exp(spread)
            step_row = step_t[h : h + 1, :]
            weight = inner * decays
            mixing.append((weight * step_row).astype(jnp.bfloat16))
            grad = dmixing[:, j * rows : (j + 1) * rows]
            dinner = dinner + grad * decays * step_row
            term = grad * weight
            dstep_rows.append(jnp.sum(term, axis=0, keepdims=True))
            dcum = dcum + jnp.where(
                head_lane == h, jnp.sum(term * step_row, axis=1, keepdims=True), 0.0
            )
            in_head = (lane < LANES // 2) if j == 0 else (lane >= LANES // 2)
            skip_grad = skip_grad + jnp.where(
                head_lane == h,
                jnp.sum(jnp.where(in_head, direct, 0.0), axis=1, keepdims=True),
                0.0,
            )
        dinput = lax.dot_general(
            jnp.concatenate(mixing, axis=1),
            dscan,
            (((0,), (0,)), ((), ())),
            preferred_element_type=jnp.float32,
        )
        gain = jnp.where(
            lane < LANES // 2, skip[:, 2 * pair : 2 * pair + 1], skip[:, 2 * pair + 1 : 2 * pair + 2]
        )
        dact = jnp.where(lane < LANES // 2, dinput[:rows], dinput[rows:]) + gain * dmixed
        finish_tile(pair, dact * slope)
    dinner_low = dinner.astype(jnp.bfloat16)
    dqueries = jnp.dot(dinner_low, keys, preferred_element_type=jnp.float32)
    dkeys = lax.dot_general(
        dinner_low, queries, (((0,), (0,)), ((), ())), preferred_element_type=jnp.float32
    )
    finish_tile(tiles - 2, dkeys * keys_slope)
    finish_tile(tiles - 1, dqueries * queries_slope)
    dstep_t = jnp.concatenate(dstep_rows, axis=0)
    dstep = dstep_t.T
    dcum = dcum - step * dstep
    upper = jnp.where(
        lax.broadcasted_iota(jnp.int32, (rows, rows), 1)
        >= lax.broadcasted_iota(jnp.int32, (rows, rows), 0),
        1.0,
        0.0,
    ).astype(jnp.float32)
    drate = exact_dot(upper, dcum)
    speed = jnp.exp(decay)
    draw = (dstep - drate * speed) * rate_sigmoid
    tail = jnp.concatenate([draw, jnp.zeros((rows, LANES - heads), jnp.float32)], axis=1)
    for side in range(2):
        rest_ref[side, :, channels // 2 :] = tail.astype(jnp.bfloat16)
    bias_grad = jnp.sum(draw, axis=0, keepdims=True)
    decay_grad = jnp.sum(-drate * step * speed, axis=0, keepdims=True)
    half_inner = pairs * LANES // 2
    half_heads = heads // 2
    for owner in range(2):
        small_ref[owner, 5:6, 0:half_inner] = gain_grad_ref[
            :, owner * half_inner : (owner + 1) * half_inner
        ]
        for place, item in enumerate((bias_grad, decay_grad, skip_grad)):
            at = place * LANES
            small_ref[owner, 6:7, at : at + half_heads] = item[
                :, owner * half_heads : (owner + 1) * half_heads
            ]
    core, place = core_place(), owner_place()
    keep_ref[...] = rest_ref[core]
    send_ref[...] = rest_ref[1 - core]
    small_keep_ref[...] = small_ref[place]
    small_send_ref[...] = small_ref[1 - place]


def whole(shape, dtype):
    return jax.ShapeDtypeStruct(shape, dtype)


def call(body, out_shape, operands, scratch=(), lens=None):
    vmem = pl.BlockSpec(memory_space=pltpu.VMEM)
    in_specs = [vmem for _ in operands]
    if lens is not None:
        operands = (lens, *operands)
        in_specs = [pl.BlockSpec(memory_space=pltpu.SMEM), *in_specs]
    return pl.pallas_call(
        body,
        out_shape=out_shape,
        in_specs=in_specs,
        out_specs=[vmem for _ in out_shape],
        scratch_shapes=[pltpu.VMEM(item.shape, item.dtype) for item in scratch],
        compiler_params=pltpu.CompilerParams(vmem_limit_bytes=40 << 20),
        name=body.__name__,
        cost_estimate=pl.CostEstimate(flops=1, bytes_accessed=1, transcendentals=0),
    )(*operands)


def unit_rows(tokens):
    values = tokens.astype(jnp.float32)
    return lax.rsqrt(jnp.mean(values * values, axis=-1, keepdims=True) + EPSILON)


def lanes_product(left, right):
    return lax.dot_general(
        left, right, (((1,), (1,)), ((), ())), preferred_element_type=jnp.float32
    )


def rows_product(left, right):
    return lax.dot_general(
        left, right, (((0,), (0,)), ((), ())), preferred_element_type=jnp.float32
    )


def lane_half(size):
    return pl.ds(pl.multiple_of(owner_place() * size, LANES), size)


def half_means(tokens_ref, size):
    return tokens_ref[:, lane_half(size)].astype(jnp.float32) * unit_rows(tokens_ref[...])


def norm_body(first_ref, second_ref, gain_ref, out_first_ref, out_second_ref):
    for tokens_ref, out_ref in ((first_ref, out_first_ref), (second_ref, out_second_ref)):
        means = half_means(tokens_ref, out_ref.shape[1])
        out_ref[...] = (means * gain_ref[...]).astype(jnp.bfloat16)


def project_rest(normed, weight_ref, rest_ref, inner_width):
    rest_width = weight_ref.shape[0] - inner_width
    whole_tiles = rest_width // LANES * LANES
    rest_ref[:, :whole_tiles] = lanes_product(
        normed, weight_ref[inner_width : inner_width + whole_tiles, :]
    ).astype(rest_ref.dtype)
    tail = lanes_product(normed, weight_ref[inner_width + whole_tiles :, :])
    blank = jnp.zeros((tail.shape[0], LANES - tail.shape[1]), jnp.float32)
    rest_ref[:, whole_tiles:] = jnp.concatenate([tail, blank], axis=1).astype(rest_ref.dtype)


def project_own_body(tokens_ref, cotangent_ref, gain_ref, weight_ref, out_weight_ref, normed_ref, rest_ref, gate_ref, q_ref):
    inner_width = gate_ref.shape[1]
    normed = (half_means(tokens_ref, normed_ref.shape[1]) * gain_ref[...]).astype(jnp.bfloat16)
    normed_ref[...] = normed
    project_rest(normed, weight_ref, rest_ref, inner_width)
    gate_ref[...] = lanes_product(normed, weight_ref[:inner_width, :])
    q_ref[...] = lanes_product(cotangent_ref[...], out_weight_ref[...])


def project_far_body(inner_width, tokens_ref, gain_ref, weight_ref, normed_ref, wide_ref, rest_ref):
    normed = (half_means(tokens_ref, normed_ref.shape[1]) * gain_ref[...]).astype(jnp.bfloat16)
    normed_ref[...] = normed
    wide = wide_ref.shape[1]
    wide_ref[...] = lanes_product(
        normed, weight_ref[inner_width : inner_width + wide, :]
    ).astype(wide_ref.dtype)
    project_rest(normed, weight_ref, rest_ref, inner_width + wide)


def gate_far_body(normed_ref, cotangent_ref, weight_ref, out_weight_ref, send_ref):
    inner_width = send_ref.shape[1] - out_weight_ref.shape[0]
    send_ref[:, :inner_width] = lanes_product(
        normed_ref[...], weight_ref[:inner_width, :]
    ).astype(send_ref.dtype)
    send_ref[:, inner_width:] = lanes_product(
        cotangent_ref[...], out_weight_ref[...]
    ).astype(send_ref.dtype)


def branch_body(keep_ref, got_ref, weight_ref, own_ref, send_ref):
    send_ref[...] = jnp.dot(
        got_ref[: send_ref.shape[0], :], weight_ref[...], preferred_element_type=jnp.float32
    ).astype(send_ref.dtype)
    own_ref[...] = jnp.dot(keep_ref[...], weight_ref[...], preferred_element_type=jnp.float32)


def input_grad_body(*refs):
    tokens, gates, rests = refs[0:4], refs[4:8], refs[8:12]
    gain_ref, weight_ref = refs[12:14]
    rows = tokens[0].shape[0]
    gate_starts = (0, rows, 0, 0)
    own_ref, far_ref, sib_ref, gain_grad_ref = refs[14:18]
    outs = (
        own_ref,
        far_ref.at[0:rows],
        sib_ref,
        far_ref.at[rows:],
    )
    core = core_place()
    half_inner = gates[0].shape[1]
    half_channels = rests[0].shape[1] - LANES
    tail = weight_ref.shape[0] - 2 * (half_inner + half_channels)
    gate_rows = pl.ds(pl.multiple_of(core * half_inner, LANES), half_inner)
    rest_rows = pl.ds(
        pl.multiple_of(2 * half_inner + core * half_channels, LANES), half_channels
    )
    gate_weight = weight_ref[gate_rows, :]
    rest_weight = weight_ref[rest_rows, :]
    tail_weight = weight_ref[2 * (half_inner + half_channels) :, :]
    gain = gain_ref[...]
    gain_grad = jnp.zeros_like(gain)
    for tokens_ref, gate_ref, at, rest_ref, out_ref in zip(
        tokens, gates, gate_starts, rests, outs
    ):
        dnormed = jnp.dot(
            gate_ref[at : at + rows, :], gate_weight, preferred_element_type=jnp.float32
        )
        dnormed = dnormed + jnp.dot(
            rest_ref[:, :half_channels], rest_weight, preferred_element_type=jnp.float32
        )
        dtail = jnp.dot(
            rest_ref[:, half_channels : half_channels + tail],
            tail_weight,
            preferred_element_type=jnp.float32,
        )
        dnormed = dnormed + jnp.where(core == 0, dtail, 0.0)
        means = half_means(tokens_ref, gain.shape[1])
        gain_grad = gain_grad + jnp.sum(dnormed * means, axis=0, keepdims=True)
        out_ref[...] = (dnormed * gain).astype(out_ref.dtype)
    gain_grad_ref[...] = gain_grad


def tokens_grad_body(tokens_ref, cotangent_ref, own_ref, far_ref, sib_ref, out_ref):
    rows, half = own_ref.shape
    first = owner_place() == 0
    inverse = unit_rows(tokens_ref[...])
    own = own_ref[...] + sib_ref[:rows].astype(jnp.float32)
    far = far_ref[:rows].astype(jnp.float32) + sib_ref[rows:].astype(jnp.float32)
    parts = []
    cross = jnp.zeros_like(inverse)
    for side in range(2):
        cut = slice(side * half, (side + 1) * half)
        dmeans = jnp.where(first == (side == 0), own, far)
        means = tokens_ref[:, cut].astype(jnp.float32) * inverse
        cross = cross + jnp.sum(dmeans * means, axis=1, keepdims=True)
        parts.append((cut, dmeans, means))
    for cut, dmeans, means in parts:
        out_ref[:, cut] = cotangent_ref[:, cut].astype(jnp.float32) + inverse * (
            dmeans - means * (cross / (2 * half))
        )


def left_lanes(lefts, starts, rows, at, size):
    cut = pl.ds(pl.multiple_of(at, LANES), size)
    return jnp.concatenate(
        [ref[first : first + rows, cut] for ref, first in zip(lefts, starts)], axis=0
    )


def block_grad_body(part, starts, right_half, *refs):
    lefts, rights, (send_ref, keep_ref) = refs[0:4], refs[4:8], refs[8:]
    rows = rights[0].shape[0]
    width = send_ref.shape[1]
    lanes = slice(None)
    if right_half:
        lanes = pl.ds(pl.multiple_of(core_place() * width, LANES), width)
    right = jnp.concatenate([ref[:, lanes] for ref in rights], axis=0)
    at, size, order = part
    bit = chip_bit(order[0])
    half = size // 2
    for ref, side in ((send_ref, 1 - bit), (keep_ref, bit)):
        left = left_lanes(lefts, starts, rows, at + side * half, half)
        ref[...] = rows_product(left, right).astype(ref.dtype)


SMALL_ROWS = 16


def block_small_body(part, starts, *refs):
    lefts, rights, (mine_ref, far_ref, send_ref, keep_ref) = refs[0:4], refs[4:8], refs[8:]
    rows = rights[0].shape[0]
    width = send_ref.shape[1]
    right = jnp.concatenate([ref[...] for ref in rights], axis=0)
    total = mine_ref[...] + far_ref[...]
    count, wide = total.shape
    blank = jnp.zeros((SMALL_ROWS - count, width), jnp.float32)
    smalls = []
    for quarter in range(4):
        piece = total[:, quarter * width : min(wide, (quarter + 1) * width)]
        if piece.shape[1] < width:
            rest = jnp.zeros((count, width - piece.shape[1]), jnp.float32)
            piece = jnp.concatenate([piece, rest], axis=1) if piece.shape[1] else rest
        smalls.append(jnp.concatenate([piece, blank], axis=0))
    heads = total[6:7, :width]
    high = heads.astype(jnp.bfloat16).astype(jnp.float32)
    row = lax.broadcasted_iota(jnp.int32, (SMALL_ROWS, 1), 0)
    chip = lax.div(lax.axis_index("replica"), 2)
    smalls[3] = jnp.where(row == chip, high, 0.0) + jnp.where(
        row == chip + SMALL_ROWS // 2, heads - high, 0.0
    )
    at, size, order = part
    bit = chip_bit(order[0])
    quarter = size // 4
    for ref, side in ((send_ref, 1 - bit), (keep_ref, bit)):
        left = left_lanes(lefts, starts, rows, at + side * 2 * quarter, 2 * quarter)
        block = rows_product(left, right)
        for q in range(2):
            base = q * (quarter + SMALL_ROWS)
            ref[base : base + quarter, :] = block[q * quarter : (q + 1) * quarter].astype(
                ref.dtype
            )
            ref[base + quarter : base + quarter + SMALL_ROWS, :] = jnp.where(
                side == 0, smalls[q], smalls[2 + q]
            ).astype(ref.dtype)


def block_norm_body(part, starts, norm_row, *refs):
    lefts, rights, (norm_ref, send_ref, keep_ref) = refs[0:4], refs[4:8], refs[8:]
    rows = rights[0].shape[0]
    right = jnp.concatenate([ref[...] for ref in rights], axis=0)
    at, size, order = part
    bit = chip_bit(order[0])
    half = size // 2
    row = lax.broadcasted_iota(jnp.int32, (half, 1), 0)
    for ref, side in ((send_ref, 1 - bit), (keep_ref, bit)):
        left = left_lanes(lefts, starts, rows, at + side * half, half)
        block = rows_product(left, right)
        here = (row + (at + side * half)) == norm_row
        ref[...] = jnp.where(here, norm_ref[...], block).astype(ref.dtype)


def halve_body(bit, keep_ref, got_ref, send_ref, out_ref):
    rows = send_ref.shape[0]
    bit = chip_bit(bit)
    for ref, side in ((send_ref, 1 - bit), (out_ref, bit)):
        cut = pl.ds(pl.multiple_of(side * rows, 16), rows)
        ref[...] = (keep_ref[cut, :] + got_ref[cut, :].astype(jnp.float32)).astype(ref.dtype)


def add_body(keep_ref, got_ref, out_ref):
    out_ref[...] = (
        keep_ref[...].astype(jnp.float32) + got_ref[...].astype(jnp.float32)
    ).astype(out_ref.dtype)


def after(value, *earlier):
    return lax.optimization_barrier((value, *earlier))[0]


class PartSum:
    def __init__(self, order, make_block, early=False):
        self.order, self.make_block, self.early = order, make_block, early
        self.steps = 0
        self.pieces = None

    def advance(self, token):
        f32, low = jnp.float32, jnp.bfloat16
        step = self.steps
        self.steps += 1
        if step == 0:
            send, self.keep = self.make_block(token)
            bit = self.order[0]
        elif step == 1:
            keep = after(self.keep, token)
            shape = (keep.shape[0] // 2, keep.shape[1])

            def halve(*refs):
                halve_body(self.order[1], *refs)

            send, self.keep = call(
                halve, [whole(shape, low), whole(shape, f32)], (keep, self.got)
            )
            bit = self.order[1]
        elif step < 4:
            keep = after(self.keep, token)
            (send,) = call(add_body, [whole(keep.shape, low)], (keep, self.got))
            self.keep = send
            bit = self.order[2] if step == 2 else self.order[1]
        elif step == 4:
            send = jnp.concatenate([after(self.keep, token), self.got], axis=0)
            self.keep = send
            if self.early:
                self.sibling = swap_core(send)
            bit = self.order[0]
        else:
            got = after(self.got, token)
            sibling = after(self.sibling, got) if self.early else swap_core(self.keep)
            self.pieces = [self.keep, got, sibling, swap_core(got)]
            return got
        self.got = swap_chip(send, bit)
        return send


def part_quarters(order, pieces):
    first, second = chip_bit(order[0]), chip_bit(order[1])
    for which in range(2):
        side = first if which == 0 else 1 - first
        mine, sibling = pieces[which], pieces[2 + which]
        size = mine.shape[0] // 2
        for p in range(2):
            quarter = 2 * side + (second if p == 0 else 1 - second)
            yield quarter, mine, sibling, p * size


def write_part(out_ref, base, part, pieces, other):
    at, size, order = part
    size = size // 4
    for quarter, mine, sibling, row in part_quarters(order, pieces):
        rows = slice(row, row + size)
        value = jnp.where(other, sibling[rows, :], mine[rows, :]).astype(jnp.float32)
        out_ref[pl.ds(pl.multiple_of(base + at + quarter * size, 8), size), :] = value


def in_weight_body(gate_part, rest_parts, *refs):
    (out_ref, norm_ref), refs = refs[-2:], refs[:-2]
    gates, rests = refs[0:4], refs[4:]
    core = core_place()
    half_inner = gate_part[1]
    last_at, last_size, last_order = rest_parts[1]
    half_channels = last_at + last_size - LANES
    tail_at = 2 * (half_inner + half_channels)
    tail = out_ref.shape[0] - tail_at
    for side in range(2):
        other = core != side
        base = 2 * half_inner + side * half_channels
        write_part(out_ref, side * half_inner, gate_part, gates, other)
        write_part(out_ref, base, rest_parts[0], rests[0:4], other)
        size = last_size // 4
        for quarter, mine, sibling, row in part_quarters(last_order, rests[4:8]):
            rows = slice(row, row + size)
            value = jnp.where(other, sibling[rows, :], mine[rows, :]).astype(jnp.float32)

            @pl.when(quarter < 3)
            def _():
                place = base + last_at + quarter * size
                out_ref[pl.ds(pl.multiple_of(place, 8), size), :] = value

            if side == 0:

                @pl.when(quarter == 3)
                def _():
                    out_ref[tail_at:, :] = value[:tail]
                    both = mine[rows, :].astype(jnp.float32) + sibling[rows, :].astype(
                        jnp.float32
                    )
                    norm_ref[...] = both[tail : tail + norm_ref.shape[0]]


def small_body(order, *refs):
    pieces, out_ref = refs[:-1], refs[-1]
    count, wide = out_ref.shape[0] // 2, out_ref.shape[1]
    width = pieces[0].shape[1]
    for quarter, mine, sibling, row in part_quarters(order, pieces):
        size = mine.shape[0] // 2
        rows = slice(row + size - SMALL_ROWS, row + size)
        both = mine[rows, :].astype(jnp.float32) + sibling[rows, :].astype(jnp.float32)
        for place in range((wide + width - 1) // width):
            lanes = slice(place * width, min(wide, (place + 1) * width))

            @pl.when(quarter == place)
            def _():
                out_ref[:count, lanes] = both[:count, : lanes.stop - lanes.start]

        @pl.when(quarter == 3)
        def _():
            out_ref[count : count + 1, :width] = jnp.sum(both, axis=0, keepdims=True)


def out_weight_body(part, blocks, *refs):
    side = lax.div(pl.program_id(0), blocks)
    write_part(refs[-1], 0, part, refs[:-1], core_place() != side)


def assemble(body, outs, pieces, block):
    blocks = pieces[0].shape[1] // block
    return pl.pallas_call(
        body,
        grid=(outs[0].shape[1] // block,),
        out_shape=outs,
        in_specs=[
            pl.BlockSpec((item.shape[0], block), lambda i: (0, lax.rem(i, blocks)))
            for item in pieces
        ],
        out_specs=[pl.BlockSpec((out.shape[0], block), lambda i: (0, i)) for out in outs],
        compiler_params=pltpu.CompilerParams(vmem_limit_bytes=48 << 20),
        name=body.__name__,
        cost_estimate=pl.CostEstimate(flops=1, bytes_accessed=1, transcendentals=0),
    )(*pieces)


def swap(value, replica_bits, fsdp_bits):
    replicas, owners = lax.axis_size("replica"), lax.axis_size("fsdp")
    pairs = [
        (r * owners + f, (r ^ replica_bits) * owners + (f ^ fsdp_bits))
        for r in range(replicas)
        for f in range(owners)
    ]
    return lax.ppermute(value, AXES, pairs)


def swap_owner(value):
    return swap(value, 0, 1)


def swap_core(value):
    return swap(value, 1, 0)


def swap_chip(value, bit):
    return swap(value, 2 << bit, 0)


def join(place, own, other, axis):
    return jnp.where(
        place == 0,
        jnp.concatenate([own, other], axis=axis),
        jnp.concatenate([other, own], axis=axis),
    )


def part_of(value, place, parts, axis):
    size = value.shape[axis] // parts
    return lax.dynamic_slice_in_dim(value, place * size, size, axis)


def total_over_chips(block):
    chip = lax.axis_index("replica") // 2
    bits = range((lax.axis_size("replica") // 2).bit_length() - 1)
    rows, cols = block.shape
    kept = block.reshape((2,) * len(bits) + (rows >> len(bits), cols))
    for bit in bits:
        mine = (chip >> bit) & 1
        sent = lax.dynamic_index_in_dim(kept, 1 - mine, 0, keepdims=False).astype(jnp.bfloat16)
        got = swap_chip(sent, bit)
        kept = lax.dynamic_index_in_dim(kept, mine, 0, keepdims=False) + got.astype(jnp.float32)
    chunk = kept.astype(jnp.bfloat16)
    for bit in reversed(bits):
        chunk = join((chip >> bit) & 1, chunk, swap_chip(chunk, bit), 0)
    return chunk


def per_device(
    tokens,
    seq_lens,
    norm_gain,
    in_weight,
    conv_weight,
    conv_bias,
    step_bias,
    decay_log,
    skip_gain,
    out_gain,
    out_weight,
    cotangent,
):
    f32, low = jnp.float32, jnp.bfloat16
    owner = lax.axis_index("fsdp")
    core = lax.axis_index("replica") % 2
    chips = lax.axis_size("replica") // 2
    rows, width = tokens.shape
    half_width = width // 2
    half_inner = out_weight.shape[0]
    inner_width = 2 * half_inner
    half_channels = conv_bias.shape[0]
    channels = 2 * half_channels
    half_heads = skip_gain.shape[0]
    heads = 2 * half_heads
    weight = in_weight.T
    gain = norm_gain.astype(f32).reshape(1, -1)

    tokens_far = swap_owner(tokens)
    cotangent_far = swap_owner(cotangent)
    def project_far(*refs):
        project_far_body(inner_width, *refs)

    normed_far, wide_send, rest_send = call(
        project_far,
        [
            whole((rows, half_width), low),
            whole((rows, inner_width), low),
            whole((rows, channels + LANES - inner_width), f32),
        ],
        (after(tokens_far, cotangent_far), gain, weight),
    )
    rest_got, wide_got = swap_owner(rest_send), swap_owner(wide_send)
    normed_own, rest_own, gate_own, q_own = call(
        project_own_body,
        [
            whole((rows, half_width), low),
            whole((rows, channels + LANES), f32),
            whole((rows, inner_width), f32),
            whole((rows, half_inner), f32),
        ],
        (after(tokens, rest_send), cotangent, gain, weight, out_weight),
    )
    (gate_send,) = call(
        gate_far_body,
        [whole((rows, inner_width + half_inner), low)],
        (normed_far, cotangent_far, weight, out_weight),
    )
    conv_weight, conv_bias, step_bias, decay_log, skip_gain, out_gain = after(
        (conv_weight, conv_bias, step_bias, decay_log, skip_gain, out_gain), gate_send
    )

    def row(item):
        item = item.astype(f32).reshape(-1, item.shape[-1])
        return jnp.pad(item, ((0, 0), (0, half_channels - item.shape[-1])))

    def head_row(item):
        item = item.astype(f32)
        there = jnp.zeros_like(item)
        placed = jnp.where(
            owner == 0, jnp.concatenate([item, there]), jnp.concatenate([there, item])
        )
        return jnp.pad(placed, (0, LANES - heads))

    head_rows = jnp.concatenate([head_row(step_bias), head_row(decay_log), head_row(skip_gain)])
    mine = jnp.concatenate(
        [
            row(conv_weight),
            row(conv_bias),
            row(out_gain),
            row(head_rows),
            jnp.zeros((1, half_channels), f32),
        ],
        axis=0,
    )
    peer = swap_owner(mine)
    gate_got = swap_owner(after(gate_send, rest_got, wide_got, peer))
    tokens_sib, tokens_far_sib = swap_core(tokens), swap_core(tokens_far)
    cotangent_sib, cotangent_far_sib = swap_core(cotangent), swap_core(cotangent_far)
    normed_sib, normed_far_sib = call(
        norm_body,
        [whole((rows, half_width), low)] * 2,
        (tokens_sib, tokens_far_sib, gain),
    )

    xbc, conv, mixed, rates = call(
        forward_body,
        [
            whole((rows, channels), f32),
            whole((rows, channels), f32),
            whole((rows, inner_width), f32),
            whole((3, rows, heads), f32),
        ],
        (rest_own, wide_got, rest_got, mine, peer),
        lens=seq_lens,
    )
    out_keep, out_send, inverse = call(
        gate_out_body,
        [*[whole((rows, half_inner), low)] * 2, whole((rows, 1), f32)],
        (mixed, gate_own, gate_got, mine, peer),
        scratch=[whole((2, rows, half_inner), low)],
    )
    out_far, out_sib = swap_owner(out_send), swap_core(out_keep)
    dgate, dgate_send, far_send, dmixed, gain_grad = call(
        gate_grad_body,
        [
            *[whole((rows, half_inner), low)] * 2,
            whole((2 * rows, half_inner), low),
            whole((rows, inner_width), f32),
            whole((1, inner_width), f32),
        ],
        (
            after(mixed, normed_sib, normed_far_sib, cotangent_sib, cotangent_far_sib),
            gate_own,
            q_own,
            gate_got,
            mine,
            peer,
            inverse,
        ),
        scratch=[whole((2, rows, half_inner), low)],
    )
    far, dgate_sib = swap_owner(far_send), swap_core(dgate_send)
    drest, drest_send, small_keep, small_send = call(
        backward_body,
        [
            *[whole((rows, half_channels + LANES), low)] * 2,
            *[whole((8, half_channels), f32)] * 2,
        ],
        (dmixed, xbc, conv, rates, mine, peer, gain_grad),
        scratch=[
            whole((2, rows, half_channels + LANES), low),
            whole((2, 8, half_channels), f32),
        ],
        lens=seq_lens,
    )
    small_far = swap_owner(small_send)
    out_far_sib = swap_core(after(out_far, drest))
    drest_far, drest_far_sib = swap_owner(drest), swap(drest_send, 1, 1)
    drest_sib = swap_core(drest_send)

    tokens_all = (tokens, tokens_far, tokens_sib, tokens_far_sib)
    normed_all = (normed_own, normed_far, normed_sib, normed_far_sib)
    cotangent_all = (cotangent, cotangent_far, cotangent_sib, cotangent_far_sib)
    drest_all = (drest, drest_far, drest_sib, drest_far_sib)
    out_all = (out_keep, out_far, out_sib, out_far_sib)
    out_starts, gate_starts, rest_starts = (0,) * 4, (0, rows, 0, 0), (0,) * 4
    state = {}
    if chips == 8:
        cut = (half_channels + LANES) * 3 // 5 // LANES * LANES
        out_part = (0, half_inner, (0, 1, 2))
        gate_part = (0, half_inner, (1, 0, 2))
        rest_parts = ((0, cut, (0, 1, 2)), (cut, half_channels + LANES - cut, (1, 0, 2)))
        norm_row = half_channels + heads

        def maker(body, part, given, size, extra=(), early=False):
            lefts, starts, rights = given

            def make(token):
                def block_grad(*refs):
                    body(part, starts, *refs)

                if lefts is None:
                    state["far_sib"] = swap_core(after(far, token))
                    sources = (dgate, far, dgate_sib, state["far_sib"])
                else:
                    sources = lefts
                tied = sources if token is None else (after(sources[0], token), *sources[1:])
                more = [item() for item in extra]
                sizes = [whole((size // 2, half_width), dtype) for dtype in (low, f32)]
                return call(block_grad, sizes, (*tied, *rights, *more))

            return PartSum(part[2], make, early)

        def out_block(part, starts, *refs):
            block_grad_body(part, starts, True, *refs)

        def rest_block(part, starts, *refs):
            block_grad_body(part, starts, False, *refs)

        def norm_block(part, starts, *refs):
            block_norm_body(part, starts, norm_row, *refs)

        gate_sources = (None, gate_starts, normed_all)
        rest_sources = (drest_all, rest_starts, normed_all)
        sums = (
            maker(out_block, out_part, (out_all, out_starts, cotangent_all), half_inner),
            maker(
                block_small_body,
                gate_part,
                gate_sources,
                half_inner + 4 * SMALL_ROWS,
                (lambda: small_keep, lambda: small_far),
            ),
            maker(rest_block, rest_parts[0], rest_sources, rest_parts[0][1], early=True),
            maker(
                norm_block,
                rest_parts[1],
                rest_sources,
                rest_parts[1][1],
                (lambda: state["norm_grad"],),
                early=True,
            ),
        )
        token = None
    else:
        token = drest

        def total_of(left, starts, right):
            left = [item[first : first + rows] for item, first in zip(left, starts)]
            return total_over_chips(
                rows_product(jnp.concatenate(left, axis=0), jnp.concatenate(right, axis=0))
            )

        out_total = total_of(
            out_all,
            out_starts,
            [part_of(item, core, 2, 1) for item in cotangent_all],
        )
        state["far_sib"] = swap_core(far)
        dgate_all = (dgate, far, dgate_sib, state["far_sib"])
        gate_total = total_of(dgate_all, gate_starts, normed_all)
        rest_total = total_of(drest_all, rest_starts, normed_all)
        rest_sib = swap_core(rest_total)
        out_weight_grad = join(core, out_total, swap_core(out_total), 1).astype(f32)
        in_weight_grad = (
            jnp.concatenate(
                [
                    join(core, gate_total, swap_core(gate_total), 0),
                    join(core, rest_total[:half_channels], rest_sib[:half_channels], 0),
                    rest_total[half_channels : half_channels + heads],
                ],
                axis=0,
            )
            .astype(f32)
            .T
        )

    def out_projection(token):
        own, send = call(
            branch_body,
            [whole((rows, width), f32), whole((rows, width), low)],
            (after(out_keep, token), out_far, out_weight),
        )
        state["branch"] = (own, swap_owner(send))
        return send

    def block_sum(token):
        own, far = state["branch"]
        state["block_out"] = (
            tokens.astype(f32) + after(own, token) + far.astype(f32)
        ).astype(low)
        return state["block_out"]

    def input_norm(token):
        state["dmeans"] = call(
            input_grad_body,
            [
                whole((rows, half_width), f32),
                whole((2 * rows, half_width), low),
                whole((rows, half_width), low),
                whole((1, half_width), f32),
            ],
            (
                *tokens_all,
                after(dgate, token),
                far,
                dgate_sib,
                state["far_sib"],
                *drest_all,
                gain,
                weight,
            ),
        )
        state["norm_grad"] = state["dmeans"][3]
        return state["norm_grad"]

    def means_far(token):
        send = after(state["dmeans"][1], token)
        state["means_far"] = swap_owner(send)
        return send

    def means_sib(token):
        far = after(state["means_far"], token)
        send = jnp.concatenate([state["dmeans"][2], far[rows:]], axis=0)
        state["means_sib"] = swap_core(send)
        return send

    def tokens_grad(token):
        (state["grad_tokens"],) = call(
            tokens_grad_body,
            [whole((rows, width), f32)],
            (
                tokens,
                cotangent,
                after(state["dmeans"][0], token),
                state["means_far"],
                state["means_sib"],
            ),
        )
        return state["grad_tokens"]

    def small_results(total, row):
        return (
            total[0:4],
            total[4],
            total[row, 0:half_heads],
            total[row, LANES : LANES + half_heads],
            total[row, 2 * LANES : 2 * LANES + half_heads],
            total[5, :half_inner],
        )

    def small_assembly(token):
        def small_rows(*refs):
            small_body(gate_part[2], *refs)

        pieces = sums[1].pieces
        (total,) = call(
            small_rows,
            [whole((16, half_channels), f32)],
            (after(pieces[0], token), *pieces[1:]),
        )
        state["smalls"] = small_results(total, 8)
        return state["smalls"][1]

    def out_assembly(token):
        def out_weight_lanes(*refs):
            out_weight_body(out_part, 2, *refs)

        pieces = sums[0].pieces
        (state["out_weight"],) = assemble(
            out_weight_lanes,
            [whole(out_weight.shape, f32)],
            [after(pieces[0], token), *pieces[1:]],
            half_width // 2,
        )
        return state["out_weight"]

    if chips == 8:
        steps = {
            "n": input_norm,
            "x": means_far,
            "k": means_sib,
            "t": tokens_grad,
            "b": out_projection,
            "p": block_sum,
            "s": small_assembly,
            "o": out_assembly,
        }
        for mark in ORDER:
            step = steps[mark] if mark in steps else sums[int(mark)].advance
            token = step(token)

        def in_weight_rows(*refs):
            in_weight_body(gate_part, rest_parts, *refs)

        pieces = [piece for part in sums[1:] for piece in part.pieces]
        in_weight_rows_grad, norm_rows = assemble(
            in_weight_rows,
            [whole(weight.shape, f32), whole((8, half_width), f32)],
            [after(pieces[0], token), *pieces[1:]],
            LANES,
        )
        in_weight_grad = in_weight_rows_grad.T
        out_weight_grad = state["out_weight"]
        norm_gain_grad = norm_rows[0]
    else:
        for step in (out_projection, block_sum, input_norm, means_far, means_sib, tokens_grad):
            step(token)
        total = jnp.concatenate(
            [(small_keep + small_far)[:7], row(state["norm_grad"])], axis=0
        )
        bits = 1
        while bits < 2 * chips:
            total = total + swap(total, bits, 0)
            bits *= 2
        norm_gain_grad = total[7, :half_width]
        state["smalls"] = small_results(total, 6)
    return (
        state["block_out"],
        state["grad_tokens"],
        norm_gain_grad,
        in_weight_grad,
        *state["smalls"],
        out_weight_grad,
    )


def solution(mesh):
    placed = (
        P(("replica", "fsdp"), None),
        P(("replica", "fsdp"), None),
        P("fsdp"),
        P("fsdp", None),
        P(None, "fsdp"),
        P("fsdp"),
        P("fsdp"),
        P("fsdp"),
        P("fsdp"),
        P("fsdp"),
        P("fsdp", None),
        P(("replica", "fsdp"), None),
    )
    return jax.shard_map(
        per_device,
        mesh=mesh,
        in_specs=placed,
        out_specs=(
            P(("replica", "fsdp"), None),
            P(("replica", "fsdp"), None),
            P("fsdp"),
            P("fsdp", None),
            P(None, "fsdp"),
            P("fsdp"),
            P("fsdp"),
            P("fsdp"),
            P("fsdp"),
            P("fsdp"),
            P("fsdp", None),
        ),
        check_vma=False,
    )
```

```python
import jax
import jax.numpy as jnp
from jax import lax
from jax.experimental import pallas as pl
from jax.experimental.pallas import tpu as pltpu
from jax.sharding import PartitionSpec as P

EPSILON = 1e-05
AXES = ("replica", "fsdp")
LANES = 128
FAR = -1e30
ORDER = "01012n3x01k2301t2301b2301p2os323"


def owner_place():
    return lax.axis_index("fsdp")


def core_place():
    return lax.rem(lax.axis_index("replica"), 2)


def chip_bit(bit):
    return lax.rem(lax.div(lax.axis_index("replica"), 2 << bit), 2)


def full_rows(mine_ref, peer_ref):
    first = owner_place() == 0
    mine, peer = mine_ref[...], peer_ref[...]
    return (jnp.where(first, mine, peer), jnp.where(first, peer, mine), mine + peer)


def row_marks(lens_ref, rows):
    end_one, end_two = lens_ref[0, 0], lens_ref[0, 0] + lens_ref[0, 1]
    position = lax.broadcasted_iota(jnp.int32, (rows, 1), 0)
    start = jnp.where(position >= end_two, end_two, jnp.where(position >= end_one, end_one, 0))
    return (position, start)


def kept_pairs(start, rows):
    key = lax.broadcasted_iota(jnp.int32, (rows, rows), 1)
    query = lax.broadcasted_iota(jnp.int32, (rows, rows), 0)
    return (key <= query) & (key >= start)


def channel_row(low, high, row, tile):
    half = low.shape[1] // LANES
    source = low if tile < half else high
    at = (tile if tile < half else tile - half) * LANES
    return source[row : row + 1, at : at + LANES]


def exact_dot(left, right):
    return jnp.dot(
        left, right, precision=lax.Precision.HIGHEST, preferred_element_type=jnp.float32
    )


def pair_operand(values, lane):
    zero = jnp.zeros_like(values)
    return jnp.concatenate(
        [jnp.where(lane < LANES // 2, values, zero), jnp.where(lane < LANES // 2, zero, values)],
        axis=0,
    )


def forward_body(lens_ref, own_ref, wide_ref, got_ref, mine_ref, peer_ref, xbc_ref, conv_ref, mixed_ref, rates_ref):
    rows, channels = conv_ref.shape
    tiles = channels // LANES
    pairs = tiles - 2
    heads = 2 * pairs
    taps = 4
    low, high, both = full_rows(mine_ref, peer_ref)
    position, start = row_marks(lens_ref, rows)
    usable = [position - (taps - 1 - k) >= start for k in range(taps)]
    lane = lax.broadcasted_iota(jnp.int32, (1, LANES), 1)
    bias = both[6:7, 0:heads]
    decay = both[6:7, LANES : LANES + heads]
    skip = both[6:7, 2 * LANES : 2 * LANES + heads]
    tail = slice(channels, channels + heads)
    wide = wide_ref.shape[1]
    rate = own_ref[:, tail] + got_ref[:, channels - wide : channels - wide + heads] + bias
    step = jnp.maximum(rate, 0.0) + jnp.log1p(jnp.exp(-jnp.abs(rate)))
    rate_sigmoid = jax.nn.sigmoid(rate)
    lower = jnp.where(
        lax.broadcasted_iota(jnp.int32, (rows, rows), 1)
        <= lax.broadcasted_iota(jnp.int32, (rows, rows), 0),
        1.0,
        0.0,
    ).astype(jnp.float32)
    cum = exact_dot(lower, step * -jnp.exp(decay))
    rates_ref[0] = step
    rates_ref[1] = cum
    rates_ref[2] = rate_sigmoid
    step_t, cum_t = step.T, cum.T
    mask = kept_pairs(start, rows)

    def active_tile(tile):
        at = tile * LANES
        if at < wide:
            far = wide_ref[:, at : at + LANES].astype(jnp.float32)
        else:
            far = got_ref[:, at - wide : at - wide + LANES]
        xbc = own_ref[:, at : at + LANES] + far
        xbc_ref[:, at : at + LANES] = xbc
        conv = channel_row(low, high, 4, tile) + channel_row(low, high, taps - 1, tile) * xbc
        for k in range(taps - 1):
            shifted = pltpu.roll(xbc, taps - 1 - k, 0)
            conv = conv + channel_row(low, high, k, tile) * jnp.where(usable[k], shifted, 0.0)
        conv_ref[:, at : at + LANES] = conv
        return conv * jax.nn.sigmoid(conv)

    keys = active_tile(tiles - 2).astype(jnp.bfloat16)
    queries = active_tile(tiles - 1).astype(jnp.bfloat16)
    inner = lax.dot_general(
        queries, keys, (((1,), (1,)), ((), ())), preferred_element_type=jnp.float32
    )
    for pair in range(pairs):
        act = active_tile(pair)
        mixing = []
        for h in (2 * pair, 2 * pair + 1):
            spread = jnp.where(mask, cum[:, h : h + 1] - cum_t[h : h + 1, :], FAR)
            mixing.append((inner * jnp.exp(spread) * step_t[h : h + 1, :]).astype(jnp.bfloat16))
        scan = jnp.dot(
            jnp.concatenate(mixing, axis=1),
            pair_operand(act.astype(jnp.bfloat16), lane),
            preferred_element_type=jnp.float32,
        )
        gain = jnp.where(
            lane < LANES // 2, skip[:, 2 * pair : 2 * pair + 1], skip[:, 2 * pair + 1 : 2 * pair + 2]
        )
        mixed_ref[:, pair * LANES : (pair + 1) * LANES] = scan + gain * act


def half_cut(tile, width, half):
    at = tile * width % half
    return slice(at, at + width)


def gate_tile(own_ref, got_ref, cut):
    gate = own_ref[:, cut] + got_ref[:, cut].astype(jnp.float32)
    return (gate, jax.nn.sigmoid(gate))


def gate_out_body(mixed_ref, own_ref, got_ref, mine_ref, peer_ref, keep_ref, send_ref, inverse_ref, out_ref):
    rows, inner_width = mixed_ref.shape
    half = inner_width // 2
    owner = owner_place()
    low, high, _ = full_rows(mine_ref, peer_ref)
    width = 2 * LANES
    cuts = [slice(at, at + width) for at in range(0, inner_width, width)]
    squares = jnp.zeros((rows, 1), jnp.float32)
    for cut in cuts:
        gate, sigmoid = gate_tile(own_ref, got_ref, cut)
        gated = mixed_ref[:, cut] * (gate * sigmoid)
        squares = squares + jnp.sum(gated * gated, axis=1, keepdims=True)
    inverse = lax.rsqrt(squares / inner_width + EPSILON)
    inverse_ref[...] = inverse
    for tile, cut in enumerate(cuts):
        gate, sigmoid = gate_tile(own_ref, got_ref, cut)
        near = half_cut(tile, width, half)
        gain = (low if cut.start < half else high)[5:6, near]
        normed = mixed_ref[:, cut] * (gate * sigmoid) * inverse
        out_ref[cut.start // half, :, near] = (normed * gain).astype(jnp.bfloat16)
    keep_ref[...] = out_ref[owner]
    send_ref[...] = out_ref[1 - owner]


def gate_grad_body(mixed_ref, own_ref, q_own_ref, got_ref, mine_ref, peer_ref, inverse_ref, keep_ref, send_ref, far_send_ref, dmixed_ref, gain_grad_ref, dgate_ref):
    rows, inner_width = mixed_ref.shape
    half = inner_width // 2
    owner, core = owner_place(), core_place()
    low, high, _ = full_rows(mine_ref, peer_ref)
    width = 2 * LANES
    cuts = [slice(at, at + width) for at in range(0, inner_width, width)]
    inverse = inverse_ref[...]

    def operands(tile, cut):
        near = half_cut(tile, width, half)
        in_low = cut.start < half
        gain = (low if in_low else high)[5:6, near]
        far = got_ref[:, inner_width + near.start : inner_width + near.stop]
        q = jnp.where((owner == 0) == in_low, q_own_ref[:, near], far.astype(jnp.float32))
        return (near, gain, q)

    cross = jnp.zeros((rows, 1), jnp.float32)
    for tile, cut in enumerate(cuts):
        _, gain, q = operands(tile, cut)
        gate, sigmoid = gate_tile(own_ref, got_ref, cut)
        cross = cross + jnp.sum(
            q * gain * (mixed_ref[:, cut] * (gate * sigmoid)), axis=1, keepdims=True
        )
    mean_cross = cross * inverse / inner_width
    for tile, cut in enumerate(cuts):
        near, gain, q = operands(tile, cut)
        gate, sigmoid = gate_tile(own_ref, got_ref, cut)
        silu = gate * sigmoid
        mixed = mixed_ref[:, cut]
        normed = mixed * silu * inverse
        gain_grad_ref[:, cut] = jnp.sum(q * normed, axis=0, keepdims=True)
        dgated = inverse * (q * gain - normed * mean_cross)
        dmixed_ref[:, cut] = dgated * silu
        dgate_ref[cut.start // half, :, near] = (
            dgated * mixed * (sigmoid * (1.0 + gate * (1.0 - sigmoid)))
        ).astype(jnp.bfloat16)
    keep_ref[...] = dgate_ref[core]
    send_ref[...] = dgate_ref[1 - core]
    far_send_ref[:rows] = dgate_ref[1 - core]
    far_send_ref[rows:] = dgate_ref[core]


def backward_body(lens_ref, dmixed_ref, xbc_ref, conv_ref, rates_ref, mine_ref, peer_ref, gain_grad_ref, keep_ref, send_ref, small_keep_ref, small_send_ref, rest_ref, small_ref):
    rows, channels = conv_ref.shape
    tiles = channels // LANES
    pairs = tiles - 2
    heads = 2 * pairs
    taps = 4
    half_tiles = tiles // 2
    small_ref[...] = jnp.zeros(small_ref.shape, jnp.float32)
    low, high, both = full_rows(mine_ref, peer_ref)
    position, start = row_marks(lens_ref, rows)
    usable = [position - (taps - 1 - k) >= start for k in range(taps)]
    lane = lax.broadcasted_iota(jnp.int32, (1, LANES), 1)
    decay = both[6:7, LANES : LANES + heads]
    skip = both[6:7, 2 * LANES : 2 * LANES + heads]
    step, cum, rate_sigmoid = rates_ref[0], rates_ref[1], rates_ref[2]
    step_t, cum_t = step.T, cum.T
    mask = kept_pairs(start, rows)

    def cut(tile):
        return slice(tile * LANES, (tile + 1) * LANES)

    def act_of(tile):
        conv = conv_ref[:, cut(tile)]
        sigmoid = jax.nn.sigmoid(conv)
        return (conv * sigmoid, sigmoid * (1.0 + conv * (1.0 - sigmoid)))

    def finish_tile(tile, dconv):
        owner, at = tile // half_tiles, tile % half_tiles * LANES
        xbc = xbc_ref[:, cut(tile)]
        small_ref[owner, 4:5, at : at + LANES] = jnp.sum(dconv, axis=0, keepdims=True)
        small_ref[owner, taps - 1 : taps, at : at + LANES] = jnp.sum(
            dconv * xbc, axis=0, keepdims=True
        )
        total = channel_row(low, high, taps - 1, tile) * dconv
        for k in range(taps - 1):
            behind = taps - 1 - k
            kept = jnp.where(usable[k], dconv, 0.0)
            small_ref[owner, k : k + 1, at : at + LANES] = jnp.sum(
                kept * pltpu.roll(xbc, behind, 0), axis=0, keepdims=True
            )
            total = total + channel_row(low, high, k, tile) * pltpu.roll(kept, rows - behind, 0)
        rest_ref[owner, :, at : at + LANES] = total.astype(jnp.bfloat16)

    keys_act, keys_slope = act_of(tiles - 2)
    queries_act, queries_slope = act_of(tiles - 1)
    keys, queries = keys_act.astype(jnp.bfloat16), queries_act.astype(jnp.bfloat16)
    inner = lax.dot_general(
        queries, keys, (((1,), (1,)), ((), ())), preferred_element_type=jnp.float32
    )
    dinner = jnp.zeros((rows, rows), jnp.float32)
    dstep_rows = []
    dcum = jnp.zeros((rows, heads), jnp.float32)
    skip_grad = jnp.zeros((1, heads), jnp.float32)
    head_lane = lax.broadcasted_iota(jnp.int32, (1, heads), 1)
    for pair in range(pairs):
        act, slope = act_of(pair)
        dmixed = dmixed_ref[:, cut(pair)]
        dscan = dmixed.astype(jnp.bfloat16)
        operand = pair_operand(act.astype(jnp.bfloat16), lane)
        dmixing = lax.dot_general(
            dscan, operand, (((1,), (1,)), ((), ())), preferred_element_type=jnp.float32
        )
        direct = jnp.sum(dmixed * act, axis=0, keepdims=True)
        mixing = []
        for j in range(2):
            h = 2 * pair + j
            spread = jnp.where(mask, cum[:, h : h + 1] - cum_t[h : h + 1, :], FAR)
            decays = jnp.exp(spread)
            step_row = step_t[h : h + 1, :]
            weight = inner * decays
            mixing.append((weight * step_row).astype(jnp.bfloat16))
            grad = dmixing[:, j * rows : (j + 1) * rows]
            dinner = dinner + grad * decays * step_row
            term = grad * weight
            dstep_rows.append(jnp.sum(term, axis=0, keepdims=True))
            dcum = dcum + jnp.where(
                head_lane == h, jnp.sum(term * step_row, axis=1, keepdims=True), 0.0
            )
            in_head = (lane < LANES // 2) if j == 0 else (lane >= LANES // 2)
            skip_grad = skip_grad + jnp.where(
                head_lane == h,
                jnp.sum(jnp.where(in_head, direct, 0.0), axis=1, keepdims=True),
                0.0,
            )
        dinput = lax.dot_general(
            jnp.concatenate(mixing, axis=1),
            dscan,
            (((0,), (0,)), ((), ())),
            preferred_element_type=jnp.float32,
        )
        gain = jnp.where(
            lane < LANES // 2, skip[:, 2 * pair : 2 * pair + 1], skip[:, 2 * pair + 1 : 2 * pair + 2]
        )
        dact = jnp.where(lane < LANES // 2, dinput[:rows], dinput[rows:]) + gain * dmixed
        finish_tile(pair, dact * slope)
    dinner_low = dinner.astype(jnp.bfloat16)
    dqueries = jnp.dot(dinner_low, keys, preferred_element_type=jnp.float32)
    dkeys = lax.dot_general(
        dinner_low, queries, (((0,), (0,)), ((), ())), preferred_element_type=jnp.float32
    )
    finish_tile(tiles - 2, dkeys * keys_slope)
    finish_tile(tiles - 1, dqueries * queries_slope)
    dstep_t = jnp.concatenate(dstep_rows, axis=0)
    dstep = dstep_t.T
    dcum = dcum - step * dstep
    upper = jnp.where(
        lax.broadcasted_iota(jnp.int32, (rows, rows), 1)
        >= lax.broadcasted_iota(jnp.int32, (rows, rows), 0),
        1.0,
        0.0,
    ).astype(jnp.float32)
    drate = exact_dot(upper, dcum)
    speed = jnp.exp(decay)
    draw = (dstep - drate * speed) * rate_sigmoid
    tail = jnp.concatenate([draw, jnp.zeros((rows, LANES - heads), jnp.float32)], axis=1)
    for side in range(2):
        rest_ref[side, :, channels // 2 :] = tail.astype(jnp.bfloat16)
    bias_grad = jnp.sum(draw, axis=0, keepdims=True)
    decay_grad = jnp.sum(-drate * step * speed, axis=0, keepdims=True)
    half_inner = pairs * LANES // 2
    half_heads = heads // 2
    for owner in range(2):
        small_ref[owner, 5:6, 0:half_inner] = gain_grad_ref[
            :, owner * half_inner : (owner + 1) * half_inner
        ]
        for place, item in enumerate((bias_grad, decay_grad, skip_grad)):
            at = place * LANES
            small_ref[owner, 6:7, at : at + half_heads] = item[
                :, owner * half_heads : (owner + 1) * half_heads
            ]
    core, place = core_place(), owner_place()
    keep_ref[...] = rest_ref[core]
    send_ref[...] = rest_ref[1 - core]
    small_keep_ref[...] = small_ref[place]
    small_send_ref[...] = small_ref[1 - place]


def whole(shape, dtype):
    return jax.ShapeDtypeStruct(shape, dtype)


def call(body, out_shape, operands, scratch=(), lens=None):
    vmem = pl.BlockSpec(memory_space=pltpu.VMEM)
    in_specs = [vmem for _ in operands]
    if lens is not None:
        operands = (lens, *operands)
        in_specs = [pl.BlockSpec(memory_space=pltpu.SMEM), *in_specs]
    return pl.pallas_call(
        body,
        out_shape=out_shape,
        in_specs=in_specs,
        out_specs=[vmem for _ in out_shape],
        scratch_shapes=[pltpu.VMEM(item.shape, item.dtype) for item in scratch],
        compiler_params=pltpu.CompilerParams(vmem_limit_bytes=40 << 20),
        name=body.__name__,
        cost_estimate=pl.CostEstimate(flops=1, bytes_accessed=1, transcendentals=0),
    )(*operands)


def unit_rows(tokens):
    values = tokens.astype(jnp.float32)
    return lax.rsqrt(jnp.mean(values * values, axis=-1, keepdims=True) + EPSILON)


def lanes_product(left, right):
    return lax.dot_general(
        left, right, (((1,), (1,)), ((), ())), preferred_element_type=jnp.float32
    )


def rows_product(left, right):
    return lax.dot_general(
        left, right, (((0,), (0,)), ((), ())), preferred_element_type=jnp.float32
    )


def lane_half(size):
    return pl.ds(pl.multiple_of(owner_place() * size, LANES), size)


def half_means(tokens_ref, size):
    return tokens_ref[:, lane_half(size)].astype(jnp.float32) * unit_rows(tokens_ref[...])


def norm_body(first_ref, second_ref, gain_ref, out_first_ref, out_second_ref):
    for tokens_ref, out_ref in ((first_ref, out_first_ref), (second_ref, out_second_ref)):
        means = half_means(tokens_ref, out_ref.shape[1])
        out_ref[...] = (means * gain_ref[...]).astype(jnp.bfloat16)


def project_rest(normed, weight_ref, rest_ref, inner_width):
    rest_width = weight_ref.shape[0] - inner_width
    whole_tiles = rest_width // LANES * LANES
    rest_ref[:, :whole_tiles] = lanes_product(
        normed, weight_ref[inner_width : inner_width + whole_tiles, :]
    ).astype(rest_ref.dtype)
    tail = lanes_product(normed, weight_ref[inner_width + whole_tiles :, :])
    blank = jnp.zeros((tail.shape[0], LANES - tail.shape[1]), jnp.float32)
    rest_ref[:, whole_tiles:] = jnp.concatenate([tail, blank], axis=1).astype(rest_ref.dtype)


def project_own_body(tokens_ref, cotangent_ref, gain_ref, weight_ref, out_weight_ref, normed_ref, rest_ref, gate_ref, q_ref):
    inner_width = gate_ref.shape[1]
    normed = (half_means(tokens_ref, normed_ref.shape[1]) * gain_ref[...]).astype(jnp.bfloat16)
    normed_ref[...] = normed
    project_rest(normed, weight_ref, rest_ref, inner_width)
    gate_ref[...] = lanes_product(normed, weight_ref[:inner_width, :])
    q_ref[...] = lanes_product(cotangent_ref[...], out_weight_ref[...])


def project_far_body(inner_width, tokens_ref, gain_ref, weight_ref, normed_ref, wide_ref, rest_ref):
    normed = (half_means(tokens_ref, normed_ref.shape[1]) * gain_ref[...]).astype(jnp.bfloat16)
    normed_ref[...] = normed
    wide = wide_ref.shape[1]
    wide_ref[...] = lanes_product(
        normed, weight_ref[inner_width : inner_width + wide, :]
    ).astype(wide_ref.dtype)
    project_rest(normed, weight_ref, rest_ref, inner_width + wide)


def gate_far_body(normed_ref, cotangent_ref, weight_ref, out_weight_ref, send_ref):
    inner_width = send_ref.shape[1] - out_weight_ref.shape[0]
    send_ref[:, :inner_width] = lanes_product(
        normed_ref[...], weight_ref[:inner_width, :]
    ).astype(send_ref.dtype)
    send_ref[:, inner_width:] = lanes_product(
        cotangent_ref[...], out_weight_ref[...]
    ).astype(send_ref.dtype)


def branch_body(keep_ref, got_ref, weight_ref, own_ref, send_ref):
    send_ref[...] = jnp.dot(
        got_ref[: send_ref.shape[0], :], weight_ref[...], preferred_element_type=jnp.float32
    ).astype(send_ref.dtype)
    own_ref[...] = jnp.dot(keep_ref[...], weight_ref[...], preferred_element_type=jnp.float32)


def input_grad_body(*refs):
    tokens, gates, rests = refs[0:4], refs[4:8], refs[8:12]
    gain_ref, weight_ref = refs[12:14]
    rows = tokens[0].shape[0]
    gate_starts = (0, rows, 0, 0)
    own_ref, far_ref, sib_ref, gain_grad_ref = refs[14:18]
    outs = (
        own_ref,
        far_ref.at[0:rows],
        sib_ref,
        far_ref.at[rows:],
    )
    core = core_place()
    half_inner = gates[0].shape[1]
    half_channels = rests[0].shape[1] - LANES
    tail = weight_ref.shape[0] - 2 * (half_inner + half_channels)
    gate_rows = pl.ds(pl.multiple_of(core * half_inner, LANES), half_inner)
    rest_rows = pl.ds(
        pl.multiple_of(2 * half_inner + core * half_channels, LANES), half_channels
    )
    gate_weight = weight_ref[gate_rows, :]
    rest_weight = weight_ref[rest_rows, :]
    tail_weight = weight_ref[2 * (half_inner + half_channels) :, :]
    gain = gain_ref[...]
    gain_grad = jnp.zeros_like(gain)
    for tokens_ref, gate_ref, at, rest_ref, out_ref in zip(
        tokens, gates, gate_starts, rests, outs
    ):
        dnormed = jnp.dot(
            gate_ref[at : at + rows, :], gate_weight, preferred_element_type=jnp.float32
        )
        dnormed = dnormed + jnp.dot(
            rest_ref[:, :half_channels], rest_weight, preferred_element_type=jnp.float32
        )
        dtail = jnp.dot(
            rest_ref[:, half_channels : half_channels + tail],
            tail_weight,
            preferred_element_type=jnp.float32,
        )
        dnormed = dnormed + jnp.where(core == 0, dtail, 0.0)
        means = half_means(tokens_ref, gain.shape[1])
        gain_grad = gain_grad + jnp.sum(dnormed * means, axis=0, keepdims=True)
        out_ref[...] = (dnormed * gain).astype(out_ref.dtype)
    gain_grad_ref[...] = gain_grad


def tokens_grad_body(tokens_ref, cotangent_ref, own_ref, far_ref, sib_ref, out_ref):
    rows, half = own_ref.shape
    first = owner_place() == 0
    inverse = unit_rows(tokens_ref[...])
    own = own_ref[...] + sib_ref[:rows].astype(jnp.float32)
    far = far_ref[:rows].astype(jnp.float32) + sib_ref[rows:].astype(jnp.float32)
    parts = []
    cross = jnp.zeros_like(inverse)
    for side in range(2):
        cut = slice(side * half, (side + 1) * half)
        dmeans = jnp.where(first == (side == 0), own, far)
        means = tokens_ref[:, cut].astype(jnp.float32) * inverse
        cross = cross + jnp.sum(dmeans * means, axis=1, keepdims=True)
        parts.append((cut, dmeans, means))
    for cut, dmeans, means in parts:
        out_ref[:, cut] = cotangent_ref[:, cut].astype(jnp.float32) + inverse * (
            dmeans - means * (cross / (2 * half))
        )


def left_lanes(lefts, starts, rows, at, size):
    cut = pl.ds(pl.multiple_of(at, LANES), size)
    return jnp.concatenate(
        [ref[first : first + rows, cut] for ref, first in zip(lefts, starts)], axis=0
    )


def block_grad_body(part, starts, right_half, *refs):
    lefts, rights, (send_ref, keep_ref) = refs[0:4], refs[4:8], refs[8:]
    rows = rights[0].shape[0]
    width = send_ref.shape[1]
    lanes = slice(None)
    if right_half:
        lanes = pl.ds(pl.multiple_of(core_place() * width, LANES), width)
    right = jnp.concatenate([ref[:, lanes] for ref in rights], axis=0)
    at, size, order = part
    bit = chip_bit(order[0])
    half = size // 2
    for ref, side in ((send_ref, 1 - bit), (keep_ref, bit)):
        left = left_lanes(lefts, starts, rows, at + side * half, half)
        ref[...] = rows_product(left, right).astype(ref.dtype)


SMALL_ROWS = 16


def block_small_body(part, starts, *refs):
    lefts, rights, (mine_ref, far_ref, send_ref, keep_ref) = refs[0:4], refs[4:8], refs[8:]
    rows = rights[0].shape[0]
    width = send_ref.shape[1]
    right = jnp.concatenate([ref[...] for ref in rights], axis=0)
    total = mine_ref[...] + far_ref[...]
    count, wide = total.shape
    blank = jnp.zeros((SMALL_ROWS - count, width), jnp.float32)
    smalls = []
    for quarter in range(4):
        piece = total[:, quarter * width : min(wide, (quarter + 1) * width)]
        if piece.shape[1] < width:
            rest = jnp.zeros((count, width - piece.shape[1]), jnp.float32)
            piece = jnp.concatenate([piece, rest], axis=1) if piece.shape[1] else rest
        smalls.append(jnp.concatenate([piece, blank], axis=0))
    heads = total[6:7, :width]
    high = heads.astype(jnp.bfloat16).astype(jnp.float32)
    row = lax.broadcasted_iota(jnp.int32, (SMALL_ROWS, 1), 0)
    chip = lax.div(lax.axis_index("replica"), 2)
    smalls[3] = jnp.where(row == chip, high, 0.0) + jnp.where(
        row == chip + SMALL_ROWS // 2, heads - high, 0.0
    )
    at, size, order = part
    bit = chip_bit(order[0])
    quarter = size // 4
    for ref, side in ((send_ref, 1 - bit), (keep_ref, bit)):
        left = left_lanes(lefts, starts, rows, at + side * 2 * quarter, 2 * quarter)
        block = rows_product(left, right)
        for q in range(2):
            base = q * (quarter + SMALL_ROWS)
            ref[base : base + quarter, :] = block[q * quarter : (q + 1) * quarter].astype(
                ref.dtype
            )
            ref[base + quarter : base + quarter + SMALL_ROWS, :] = jnp.where(
                side == 0, smalls[q], smalls[2 + q]
            ).astype(ref.dtype)


def block_norm_body(part, starts, norm_row, *refs):
    lefts, rights, (norm_ref, send_ref, keep_ref) = refs[0:4], refs[4:8], refs[8:]
    rows = rights[0].shape[0]
    right = jnp.concatenate([ref[...] for ref in rights], axis=0)
    at, size, order = part
    bit = chip_bit(order[0])
    half = size // 2
    row = lax.broadcasted_iota(jnp.int32, (half, 1), 0)
    for ref, side in ((send_ref, 1 - bit), (keep_ref, bit)):
        left = left_lanes(lefts, starts, rows, at + side * half, half)
        block = rows_product(left, right)
        here = (row + (at + side * half)) == norm_row
        ref[...] = jnp.where(here, norm_ref[...], block).astype(ref.dtype)


def halve_body(bit, keep_ref, got_ref, send_ref, out_ref):
    rows = send_ref.shape[0]
    bit = chip_bit(bit)
    for ref, side in ((send_ref, 1 - bit), (out_ref, bit)):
        cut = pl.ds(pl.multiple_of(side * rows, 16), rows)
        ref[...] = (keep_ref[cut, :] + got_ref[cut, :].astype(jnp.float32)).astype(ref.dtype)


def add_body(keep_ref, got_ref, out_ref):
    out_ref[...] = (
        keep_ref[...].astype(jnp.float32) + got_ref[...].astype(jnp.float32)
    ).astype(out_ref.dtype)


def after(value, *earlier):
    return lax.optimization_barrier((value, *earlier))[0]


class PartSum:
    def __init__(self, order, make_block, early=False):
        self.order, self.make_block, self.early = order, make_block, early
        self.steps = 0
        self.pieces = None

    def advance(self, token):
        f32, low = jnp.float32, jnp.bfloat16
        step = self.steps
        self.steps += 1
        if step == 0:
            send, self.keep = self.make_block(token)
            bit = self.order[0]
        elif step == 1:
            keep = after(self.keep, token)
            shape = (keep.shape[0] // 2, keep.shape[1])

            def halve(*refs):
                halve_body(self.order[1], *refs)

            send, self.keep = call(
                halve, [whole(shape, low), whole(shape, f32)], (keep, self.got)
            )
            bit = self.order[1]
        elif step < 4:
            keep = after(self.keep, token)
            (send,) = call(add_body, [whole(keep.shape, low)], (keep, self.got))
            self.keep = send
            bit = self.order[2] if step == 2 else self.order[1]
        elif step == 4:
            send = jnp.concatenate([after(self.keep, token), self.got], axis=0)
            self.keep = send
            if self.early:
                self.sibling = swap_core(send)
            bit = self.order[0]
        else:
            got = after(self.got, token)
            sibling = after(self.sibling, got) if self.early else swap_core(self.keep)
            self.pieces = [self.keep, got, sibling, swap_core(got)]
            return got
        self.got = swap_chip(send, bit)
        return send


def part_quarters(order, pieces):
    first, second = chip_bit(order[0]), chip_bit(order[1])
    for which in range(2):
        side = first if which == 0 else 1 - first
        mine, sibling = pieces[which], pieces[2 + which]
        size = mine.shape[0] // 2
        for p in range(2):
            quarter = 2 * side + (second if p == 0 else 1 - second)
            yield quarter, mine, sibling, p * size


def write_part(out_ref, base, part, pieces, other):
    at, size, order = part
    size = size // 4
    for quarter, mine, sibling, row in part_quarters(order, pieces):
        rows = slice(row, row + size)
        value = jnp.where(other, sibling[rows, :], mine[rows, :]).astype(jnp.float32)
        out_ref[pl.ds(pl.multiple_of(base + at + quarter * size, 8), size), :] = value


def in_weight_body(gate_part, rest_parts, *refs):
    (out_ref, norm_ref), refs = refs[-2:], refs[:-2]
    gates, rests = refs[0:4], refs[4:]
    core = core_place()
    half_inner = gate_part[1]
    last_at, last_size, last_order = rest_parts[1]
    half_channels = last_at + last_size - LANES
    tail_at = 2 * (half_inner + half_channels)
    tail = out_ref.shape[0] - tail_at
    for side in range(2):
        other = core != side
        base = 2 * half_inner + side * half_channels
        write_part(out_ref, side * half_inner, gate_part, gates, other)
        write_part(out_ref, base, rest_parts[0], rests[0:4], other)
        size = last_size // 4
        for quarter, mine, sibling, row in part_quarters(last_order, rests[4:8]):
            rows = slice(row, row + size)
            value = jnp.where(other, sibling[rows, :], mine[rows, :]).astype(jnp.float32)

            @pl.when(quarter < 3)
            def _():
                place = base + last_at + quarter * size
                out_ref[pl.ds(pl.multiple_of(place, 8), size), :] = value

            if side == 0:

                @pl.when(quarter == 3)
                def _():
                    out_ref[tail_at:, :] = value[:tail]
                    both = mine[rows, :].astype(jnp.float32) + sibling[rows, :].astype(
                        jnp.float32
                    )
                    norm_ref[...] = both[tail : tail + norm_ref.shape[0]]


def small_body(order, *refs):
    pieces, out_ref = refs[:-1], refs[-1]
    count, wide = out_ref.shape[0] // 2, out_ref.shape[1]
    width = pieces[0].shape[1]
    for quarter, mine, sibling, row in part_quarters(order, pieces):
        size = mine.shape[0] // 2
        rows = slice(row + size - SMALL_ROWS, row + size)
        both = mine[rows, :].astype(jnp.float32) + sibling[rows, :].astype(jnp.float32)
        for place in range((wide + width - 1) // width):
            lanes = slice(place * width, min(wide, (place + 1) * width))

            @pl.when(quarter == place)
            def _():
                out_ref[:count, lanes] = both[:count, : lanes.stop - lanes.start]

        @pl.when(quarter == 3)
        def _():
            out_ref[count : count + 1, :width] = jnp.sum(both, axis=0, keepdims=True)


def out_weight_body(part, blocks, *refs):
    side = lax.div(pl.program_id(0), blocks)
    write_part(refs[-1], 0, part, refs[:-1], core_place() != side)


def assemble(body, outs, pieces, block):
    blocks = pieces[0].shape[1] // block
    return pl.pallas_call(
        body,
        grid=(outs[0].shape[1] // block,),
        out_shape=outs,
        in_specs=[
            pl.BlockSpec((item.shape[0], block), lambda i: (0, lax.rem(i, blocks)))
            for item in pieces
        ],
        out_specs=[pl.BlockSpec((out.shape[0], block), lambda i: (0, i)) for out in outs],
        compiler_params=pltpu.CompilerParams(vmem_limit_bytes=48 << 20),
        name=body.__name__,
        cost_estimate=pl.CostEstimate(flops=1, bytes_accessed=1, transcendentals=0),
    )(*pieces)


def swap(value, replica_bits, fsdp_bits):
    replicas, owners = lax.axis_size("replica"), lax.axis_size("fsdp")
    pairs = [
        (r * owners + f, (r ^ replica_bits) * owners + (f ^ fsdp_bits))
        for r in range(replicas)
        for f in range(owners)
    ]
    return lax.ppermute(value, AXES, pairs)


def swap_owner(value):
    return swap(value, 0, 1)


def swap_core(value):
    return swap(value, 1, 0)


def swap_chip(value, bit):
    return swap(value, 2 << bit, 0)


def join(place, own, other, axis):
    return jnp.where(
        place == 0,
        jnp.concatenate([own, other], axis=axis),
        jnp.concatenate([other, own], axis=axis),
    )


def part_of(value, place, parts, axis):
    size = value.shape[axis] // parts
    return lax.dynamic_slice_in_dim(value, place * size, size, axis)


def total_over_chips(block):
    chip = lax.axis_index("replica") // 2
    bits = range((lax.axis_size("replica") // 2).bit_length() - 1)
    rows, cols = block.shape
    kept = block.reshape((2,) * len(bits) + (rows >> len(bits), cols))
    for bit in bits:
        mine = (chip >> bit) & 1
        sent = lax.dynamic_index_in_dim(kept, 1 - mine, 0, keepdims=False).astype(jnp.bfloat16)
        got = swap_chip(sent, bit)
        kept = lax.dynamic_index_in_dim(kept, mine, 0, keepdims=False) + got.astype(jnp.float32)
    chunk = kept.astype(jnp.bfloat16)
    for bit in reversed(bits):
        chunk = join((chip >> bit) & 1, chunk, swap_chip(chunk, bit), 0)
    return chunk


def per_device(
    tokens,
    seq_lens,
    norm_gain,
    in_weight,
    conv_weight,
    conv_bias,
    step_bias,
    decay_log,
    skip_gain,
    out_gain,
    out_weight,
    cotangent,
):
    f32, low = jnp.float32, jnp.bfloat16
    owner = lax.axis_index("fsdp")
    core = lax.axis_index("replica") % 2
    chips = lax.axis_size("replica") // 2
    rows, width = tokens.shape
    half_width = width // 2
    half_inner = out_weight.shape[0]
    inner_width = 2 * half_inner
    half_channels = conv_bias.shape[0]
    channels = 2 * half_channels
    half_heads = skip_gain.shape[0]
    heads = 2 * half_heads
    weight = in_weight.T
    gain = norm_gain.astype(f32).reshape(1, -1)

    tokens_far = swap_owner(tokens)
    cotangent_far = swap_owner(cotangent)
    def project_far(*refs):
        project_far_body(inner_width, *refs)

    normed_far, wide_send, rest_send = call(
        project_far,
        [
            whole((rows, half_width), low),
            whole((rows, inner_width), low),
            whole((rows, channels + LANES - inner_width), f32),
        ],
        (after(tokens_far, cotangent_far), gain, weight),
    )
    rest_got, wide_got = swap_owner(rest_send), swap_owner(wide_send)
    normed_own, rest_own, gate_own, q_own = call(
        project_own_body,
        [
            whole((rows, half_width), low),
            whole((rows, channels + LANES), f32),
            whole((rows, inner_width), f32),
            whole((rows, half_inner), f32),
        ],
        (after(tokens, rest_send), cotangent, gain, weight, out_weight),
    )
    (gate_send,) = call(
        gate_far_body,
        [whole((rows, inner_width + half_inner), low)],
        (normed_far, cotangent_far, weight, out_weight),
    )
    conv_weight, conv_bias, step_bias, decay_log, skip_gain, out_gain = after(
        (conv_weight, conv_bias, step_bias, decay_log, skip_gain, out_gain), gate_send
    )

    def row(item):
        item = item.astype(f32).reshape(-1, item.shape[-1])
        return jnp.pad(item, ((0, 0), (0, half_channels - item.shape[-1])))

    def head_row(item):
        item = item.astype(f32)
        there = jnp.zeros_like(item)
        placed = jnp.where(
            owner == 0, jnp.concatenate([item, there]), jnp.concatenate([there, item])
        )
        return jnp.pad(placed, (0, LANES - heads))

    head_rows = jnp.concatenate([head_row(step_bias), head_row(decay_log), head_row(skip_gain)])
    mine = jnp.concatenate(
        [
            row(conv_weight),
            row(conv_bias),
            row(out_gain),
            row(head_rows),
            jnp.zeros((1, half_channels), f32),
        ],
        axis=0,
    )
    peer = swap_owner(mine)
    gate_got = swap_owner(after(gate_send, rest_got, wide_got, peer))
    tokens_sib, tokens_far_sib = swap_core(tokens), swap_core(tokens_far)
    cotangent_sib, cotangent_far_sib = swap_core(cotangent), swap_core(cotangent_far)
    normed_sib, normed_far_sib = call(
        norm_body,
        [whole((rows, half_width), low)] * 2,
        (tokens_sib, tokens_far_sib, gain),
    )

    xbc, conv, mixed, rates = call(
        forward_body,
        [
            whole((rows, channels), f32),
            whole((rows, channels), f32),
            whole((rows, inner_width), f32),
            whole((3, rows, heads), f32),
        ],
        (rest_own, wide_got, rest_got, mine, peer),
        lens=seq_lens,
    )
    out_keep, out_send, inverse = call(
        gate_out_body,
        [*[whole((rows, half_inner), low)] * 2, whole((rows, 1), f32)],
        (mixed, gate_own, gate_got, mine, peer),
        scratch=[whole((2, rows, half_inner), low)],
    )
    out_far, out_sib = swap_owner(out_send), swap_core(out_keep)
    dgate, dgate_send, far_send, dmixed, gain_grad = call(
        gate_grad_body,
        [
            *[whole((rows, half_inner), low)] * 2,
            whole((2 * rows, half_inner), low),
            whole((rows, inner_width), f32),
            whole((1, inner_width), f32),
        ],
        (
            after(mixed, normed_sib, normed_far_sib, cotangent_sib, cotangent_far_sib),
            gate_own,
            q_own,
            gate_got,
            mine,
            peer,
            inverse,
        ),
        scratch=[whole((2, rows, half_inner), low)],
    )
    far, dgate_sib = swap_owner(far_send), swap_core(dgate_send)
    drest, drest_send, small_keep, small_send = call(
        backward_body,
        [
            *[whole((rows, half_channels + LANES), low)] * 2,
            *[whole((8, half_channels), f32)] * 2,
        ],
        (dmixed, xbc, conv, rates, mine, peer, gain_grad),
        scratch=[
            whole((2, rows, half_channels + LANES), low),
            whole((2, 8, half_channels), f32),
        ],
        lens=seq_lens,
    )
    small_far = swap_owner(small_send)
    out_far_sib = swap_core(after(out_far, drest))
    drest_far, drest_far_sib = swap_owner(drest), swap(drest_send, 1, 1)
    drest_sib = swap_core(drest_send)

    tokens_all = (tokens, tokens_far, tokens_sib, tokens_far_sib)
    normed_all = (normed_own, normed_far, normed_sib, normed_far_sib)
    cotangent_all = (cotangent, cotangent_far, cotangent_sib, cotangent_far_sib)
    drest_all = (drest, drest_far, drest_sib, drest_far_sib)
    out_all = (out_keep, out_far, out_sib, out_far_sib)
    out_starts, gate_starts, rest_starts = (0,) * 4, (0, rows, 0, 0), (0,) * 4
    state = {}
    if chips == 8:
        cut = (half_channels + LANES) * 3 // 5 // LANES * LANES
        out_part = (0, half_inner, (0, 1, 2))
        gate_part = (0, half_inner, (1, 0, 2))
        rest_parts = ((0, cut, (0, 1, 2)), (cut, half_channels + LANES - cut, (1, 0, 2)))
        norm_row = half_channels + heads

        def maker(body, part, given, size, extra=(), early=False):
            lefts, starts, rights = given

            def make(token):
                def block_grad(*refs):
                    body(part, starts, *refs)

                if lefts is None:
                    state["far_sib"] = swap_core(after(far, token))
                    sources = (dgate, far, dgate_sib, state["far_sib"])
                else:
                    sources = lefts
                tied = sources if token is None else (after(sources[0], token), *sources[1:])
                more = [item() for item in extra]
                sizes = [whole((size // 2, half_width), dtype) for dtype in (low, f32)]
                return call(block_grad, sizes, (*tied, *rights, *more))

            return PartSum(part[2], make, early)

        def out_block(part, starts, *refs):
            block_grad_body(part, starts, True, *refs)

        def rest_block(part, starts, *refs):
            block_grad_body(part, starts, False, *refs)

        def norm_block(part, starts, *refs):
            block_norm_body(part, starts, norm_row, *refs)

        gate_sources = (None, gate_starts, normed_all)
        rest_sources = (drest_all, rest_starts, normed_all)
        sums = (
            maker(out_block, out_part, (out_all, out_starts, cotangent_all), half_inner),
            maker(
                block_small_body,
                gate_part,
                gate_sources,
                half_inner + 4 * SMALL_ROWS,
                (lambda: small_keep, lambda: small_far),
            ),
            maker(rest_block, rest_parts[0], rest_sources, rest_parts[0][1], early=True),
            maker(
                norm_block,
                rest_parts[1],
                rest_sources,
                rest_parts[1][1],
                (lambda: state["norm_grad"],),
                early=True,
            ),
        )
        token = None
    else:
        token = drest

        def total_of(left, starts, right):
            left = [item[first : first + rows] for item, first in zip(left, starts)]
            return total_over_chips(
                rows_product(jnp.concatenate(left, axis=0), jnp.concatenate(right, axis=0))
            )

        out_total = total_of(
            out_all,
            out_starts,
            [part_of(item, core, 2, 1) for item in cotangent_all],
        )
        state["far_sib"] = swap_core(far)
        dgate_all = (dgate, far, dgate_sib, state["far_sib"])
        gate_total = total_of(dgate_all, gate_starts, normed_all)
        rest_total = total_of(drest_all, rest_starts, normed_all)
        rest_sib = swap_core(rest_total)
        out_weight_grad = join(core, out_total, swap_core(out_total), 1).astype(f32)
        in_weight_grad = (
            jnp.concatenate(
                [
                    join(core, gate_total, swap_core(gate_total), 0),
                    join(core, rest_total[:half_channels], rest_sib[:half_channels], 0),
                    rest_total[half_channels : half_channels + heads],
                ],
                axis=0,
            )
            .astype(f32)
            .T
        )

    def out_projection(token):
        own, send = call(
            branch_body,
            [whole((rows, width), f32), whole((rows, width), low)],
            (after(out_keep, token), out_far, out_weight),
        )
        state["branch"] = (own, swap_owner(send))
        return send

    def block_sum(token):
        own, far = state["branch"]
        state["block_out"] = (
            tokens.astype(f32) + after(own, token) + far.astype(f32)
        ).astype(low)
        return state["block_out"]

    def input_norm(token):
        state["dmeans"] = call(
            input_grad_body,
            [
                whole((rows, half_width), f32),
                whole((2 * rows, half_width), low),
                whole((rows, half_width), low),
                whole((1, half_width), f32),
            ],
            (
                *tokens_all,
                after(dgate, token),
                far,
                dgate_sib,
                state["far_sib"],
                *drest_all,
                gain,
                weight,
            ),
        )
        state["norm_grad"] = state["dmeans"][3]
        return state["norm_grad"]

    def means_far(token):
        send = after(state["dmeans"][1], token)
        state["means_far"] = swap_owner(send)
        return send

    def means_sib(token):
        far = after(state["means_far"], token)
        send = jnp.concatenate([state["dmeans"][2], far[rows:]], axis=0)
        state["means_sib"] = swap_core(send)
        return send

    def tokens_grad(token):
        (state["grad_tokens"],) = call(
            tokens_grad_body,
            [whole((rows, width), f32)],
            (
                tokens,
                cotangent,
                after(state["dmeans"][0], token),
                state["means_far"],
                state["means_sib"],
            ),
        )
        return state["grad_tokens"]

    def small_results(total, row):
        return (
            total[0:4],
            total[4],
            total[row, 0:half_heads],
            total[row, LANES : LANES + half_heads],
            total[row, 2 * LANES : 2 * LANES + half_heads],
            total[5, :half_inner],
        )

    def small_assembly(token):
        def small_rows(*refs):
            small_body(gate_part[2], *refs)

        pieces = sums[1].pieces
        (total,) = call(
            small_rows,
            [whole((16, half_channels), f32)],
            (after(pieces[0], token), *pieces[1:]),
        )
        state["smalls"] = small_results(total, 8)
        return state["smalls"][1]

    def out_assembly(token):
        def out_weight_lanes(*refs):
            out_weight_body(out_part, 2, *refs)

        pieces = sums[0].pieces
        (state["out_weight"],) = assemble(
            out_weight_lanes,
            [whole(out_weight.shape, f32)],
            [after(pieces[0], token), *pieces[1:]],
            half_width // 2,
        )
        return state["out_weight"]

    if chips == 8:
        steps = {
            "n": input_norm,
            "x": means_far,
            "k": means_sib,
            "t": tokens_grad,
            "b": out_projection,
            "p": block_sum,
            "s": small_assembly,
            "o": out_assembly,
        }
        for mark in ORDER:
            step = steps[mark] if mark in steps else sums[int(mark)].advance
            token = step(token)

        def in_weight_rows(*refs):
            in_weight_body(gate_part, rest_parts, *refs)

        pieces = [piece for part in sums[1:] for piece in part.pieces]
        in_weight_rows_grad, norm_rows = assemble(
            in_weight_rows,
            [whole(weight.shape, f32), whole((8, half_width), f32)],
            [after(pieces[0], token), *pieces[1:]],
            LANES,
        )
        in_weight_grad = in_weight_rows_grad.T
        out_weight_grad = state["out_weight"]
        norm_gain_grad = norm_rows[0]
    else:
        for step in (out_projection, block_sum, input_norm, means_far, means_sib, tokens_grad):
            step(token)
        total = jnp.concatenate(
            [(small_keep + small_far)[:7], row(state["norm_grad"])], axis=0
        )
        bits = 1
        while bits < 2 * chips:
            total = total + swap(total, bits, 0)
            bits *= 2
        norm_gain_grad = total[7, :half_width]
        state["smalls"] = small_results(total, 6)
    return (
        state["block_out"],
        state["grad_tokens"],
        norm_gain_grad,
        in_weight_grad,
        *state["smalls"],
        out_weight_grad,
    )


def solution(mesh):
    placed = (
        P(("replica", "fsdp"), None),
        P(("replica", "fsdp"), None),
        P("fsdp"),
        P("fsdp", None),
        P(None, "fsdp"),
        P("fsdp"),
        P("fsdp"),
        P("fsdp"),
        P("fsdp"),
        P("fsdp"),
        P("fsdp", None),
        P(("replica", "fsdp"), None),
    )
    return jax.shard_map(
        per_device,
        mesh=mesh,
        in_specs=placed,
        out_specs=(
            P(("replica", "fsdp"), None),
            P(("replica", "fsdp"), None),
            P("fsdp"),
            P("fsdp", None),
            P(None, "fsdp"),
            P("fsdp"),
            P("fsdp"),
            P("fsdp"),
            P("fsdp"),
            P("fsdp"),
            P("fsdp", None),
        ),
        check_vma=False,
    )
```
